32 devices in a mesh: tiles: 8 (over z, x), ens: 4 (over y, core).
Axes of the slice: x: 2, y: 2, z: 4, core: 2. Of those that a mesh axis runs over, the one named last changes fastest.
Arguments:
- depth: float32 [8, 128, 16384], P('ens', 'tiles'), may hold values from 0.3 to 1.5
- bed: float32 [128, 16384], P('tiles'), may hold values from -1.5 to 1.5
- rain: float32 [8, 128, 16384], P('ens', 'tiles'), may hold values from 0.005 to 0.05
- rough_class: int32 [128, 16384], P('tiles'), may hold values from 0 to 15
- class_n: float32 [16], replicated, may hold values from 0.5 to 2
- contact_seg: int32 [8, 8, 8], P('tiles'), may hold values from 0 to 1023, as said below
- contact_lake: int32 [8, 8, 8], P('tiles'), may hold values from -1 to 319, as said below
- lake_slot: int32 [320], replicated, may hold values from 0 to 319, as said below
- storage: float32 [8, 320], P('ens', 'tiles'), may hold values from 0.5 to 3
- area: float32 [320], P('tiles'), may hold values from 1 to 4
- release: float32 [320], P('tiles'), may hold values from 0.5 to 0.98
- upstream_link: int32 [320], P('tiles'), may hold values from 0 to 1, as said below
Outputs:
- new_depth: float32 [8, 128, 16384], P('ens', 'tiles')
- new_storage: float32 [8, 320], P('ens', 'tiles')
- ens_outflow: float32 [320], P('tiles')
The draws below stay inside these ranges and needn't reach their ends.
Inputs may be any that keep to these rules, and one draw needn't show every extreme that they name: `contact_seg`: within one source tile the segments of all contact slots are distinct. `contact_lake`: A live entry [d, e, c] names a lake whose slot lake_slot lies on owner tile e (slots e * 40 onward); at most 8 live contacts go from one tile to one owner, and some owner receives 8 from every tile. `lake_slot`: A permutation of the slots. `upstream_link`: slots with index below 40 have 0; runs of linked slots form cascades of at most 8 reservoirs, and one cascade has exactly 8.
All inputs are finite; a program needn't handle non-finite values.
Results may differ from the reference program's by a relative error of at most 0.0001.
Values sent between devices are 32-bit elements; how exact they have to be, the bound alone decides.
No kernel may reach another device: no remote copies, remote signals or barrier semaphores. Data moves between devices by JAX's collectives and lax.ppermute only.
A program may use at most 64 MiB of HBM per device.

```python
import math
import jax
import jax.numpy as jnp
from jax import lax

R_DEV = 16
W = 16384
SEG = 256
LAKE_DEV = 40
CAP = 8
NCLASS = 16
STEPS = 4
NY = 128
MEMB = 8
LAKES = 320
DEPTH = 8
N_TILES = 8


def lake_order(key):
    return jax.random.permutation(jax.random.fold_in(key, 11), LAKES).astype(jnp.int32)


def draw_lake_slot(key, part):
    return lake_order(key)


def draw_contact_lake(key, part):
    shuffle = lake_order(key)
    slot_lake = jnp.argsort(shuffle, stable=True).astype(jnp.int32)
    key_count, key_hot, key_place = jax.random.split(jax.random.fold_in(key, 12), 3)
    counts = jax.random.randint(key_count, (N_TILES, N_TILES), 0, CAP + 1)
    hot_owner = jax.random.randint(key_hot, (2,), 0, N_TILES)
    owners = jnp.arange(N_TILES, dtype=jnp.int32)
    is_hot = jnp.any(owners[:, None] == hot_owner[None, :], axis=1)
    counts = jnp.where(is_hot[None, :], CAP, counts)
    position = jax.random.randint(key_place, (N_TILES, N_TILES, CAP), 0, LAKE_DEV)
    slot_id = owners[None, :, None] * LAKE_DEV + position
    live_mask = jnp.arange(CAP)[None, None, :] < counts[:, :, None]
    return jnp.where(live_mask, slot_lake[slot_id], -1).astype(jnp.int32)


def draw_contact_seg(key, part):
    wanted = N_TILES * CAP
    total_segs = R_DEV * (W // SEG)
    key_list = jax.random.split(jax.random.fold_in(key, 13), N_TILES)

    def one_device(device_key):
        key_first, key_second = jax.random.split(device_key)
        others = 1 + jax.random.permutation(key_first, total_segs - 2)[:wanted - 2]
        chosen = jnp.concatenate([jnp.array([0, total_segs - 1], jnp.int32), others.astype(jnp.int32)])
        return jax.random.permutation(key_second, chosen)
    return jax.vmap(one_device)(key_list).reshape(N_TILES, N_TILES, CAP).astype(jnp.int32)


def draw_upstream_link(key, part):
    key_length, key_offset = jax.random.split(jax.random.fold_in(key, 14))
    lengths = jax.random.randint(key_length, (LAKE_DEV,), 1, DEPTH + 1).at[0].set(DEPTH)
    offsets = (jax.random.randint(key_offset, (LAKE_DEV,), 0, DEPTH) % lengths).at[0].set(0)
    device_row = jnp.arange(N_TILES, dtype=jnp.int32)[:, None]
    linked = ((device_row - offsets[None, :]) % lengths[None, :] != 0) & (device_row > 0)
    return linked.astype(jnp.int32).reshape(-1)


def set_ends(entries, rng, least, top_value):
    longest = entries.shape.index(max(entries.shape))
    spots = []
    for shift in (0, 1):
        where = [jax.random.randint(jax.random.fold_in(rng, axis), (), 0, length) for axis, length in enumerate(entries.shape)]
        where[longest] = (where[longest] + shift) % entries.shape[longest]
        spots.append(tuple(where))
    return entries.at[spots[0]].set(least).at[spots[1]].set(top_value)


def shard_levels(rng, dims, cuts, least, top_value):
    def one(dim, blocks):
        steps = jax.random.uniform(jax.random.fold_in(jax.random.fold_in(rng, 6), dim), (blocks,), jnp.float32, least / len(cuts), top_value / len(cuts))
        return jnp.repeat(jnp.exp(steps), dims[dim] // blocks).reshape((-1,) + (1,) * (len(dims) - dim - 1))

    level = one(*cuts[0])
    for cut in cuts[1:]:
        level = level * one(*cut)
    return level


def centred(key, extent, spread, most, cuts=(), kind=jnp.bfloat16):
    loudness = shard_levels(key, extent, cuts, -0.22, 0.18) if cuts else 1.0
    result = jax.random.normal(key, extent, jnp.float32) * spread * loudness
    return jnp.minimum(jnp.maximum(result, -most), most).astype(kind)


def setup_inputs(seed: int = 0) -> dict:
    splits = jax.random.split(jax.random.key(seed), 13)
    depth = jnp.clip(0.3 + 1.2 * jax.random.uniform(splits[0], (MEMB, NY, W), jnp.float32) ** shard_levels(splits[0], (MEMB, NY, W), ((0, 4), (1, 8)), -0.2, 0.2), 0.3, 1.5)
    bed = centred(splits[1], (NY, W), 0.3, 1.5, ((0, 8),), jnp.float32)
    rain = jnp.clip(jnp.exp(math.log(0.05) - 2.3025851 * jax.random.uniform(splits[2], (MEMB, NY, W), jnp.float32) ** shard_levels(splits[2], (MEMB, NY, W), ((0, 4), (1, 8)), -0.2, 0.2)), 0.005, 0.05)
    rough_class = set_ends(jax.random.randint(splits[3], (NY, W), 0, NCLASS), jax.random.fold_in(splits[3], 1), 0, NCLASS - 1).astype(jnp.int32)
    class_n = jnp.clip(jnp.exp(jax.random.uniform(splits[4], (NCLASS,), jnp.float32, math.log(0.5), math.log(2.0))), 0.5, 2.0)
    contact_seg = draw_contact_seg(jax.random.fold_in(splits[12], 71), 0)
    contact_lake = draw_contact_lake(jax.random.fold_in(splits[12], 71), 0)
    lake_slot = draw_lake_slot(jax.random.fold_in(splits[12], 71), 0)
    storage = jnp.clip(0.5 + 2.5 * jax.random.uniform(splits[8], (MEMB, LAKES), jnp.float32) ** shard_levels(splits[8], (MEMB, LAKES), ((0, 4), (1, 8)), -0.2, 0.2), 0.5, 3.0)
    area = jnp.clip(jnp.exp(math.log(4.0) - 1.3862944 * jax.random.uniform(splits[9], (LAKES,), jnp.float32) ** shard_levels(splits[9], (LAKES,), ((0, 8),), -0.2, 0.2)), 1.0, 4.0)
    release = jnp.clip(0.5 + 0.48000002 * jax.random.uniform(splits[10], (LAKES,), jnp.float32) ** shard_levels(splits[10], (LAKES,), ((0, 8),), -0.2, 0.2), 0.5, 0.98)
    upstream_link = draw_upstream_link(jax.random.fold_in(splits[12], 71), 0)
    return dict(depth=depth, bed=bed, rain=rain, rough_class=rough_class, class_n=class_n, contact_seg=contact_seg, contact_lake=contact_lake, lake_slot=lake_slot, storage=storage, area=area, release=release, upstream_link=upstream_link)


flow_rate = 0.035
drain_rate = 0.4


def mobility(water, inv_n):
    root = jnp.cbrt(water)
    return water * root * root * inv_n


def surface_flow(water, bed, inv_n):
    surface = bed[None] + water
    mobile = mobility(water, inv_n[None])
    pad_surface = jnp.pad(surface, ((0, 0), (1, 1), (0, 0)))
    pad_mobile = jnp.pad(mobile, ((0, 0), (1, 1), (0, 0)))
    face_count = surface.shape[1] + 1
    face_index = jnp.arange(face_count)
    face_mask = ((face_index > 0) & (face_index < face_count - 1)).astype(water.dtype)[None, :, None]
    across = face_mask * 0.5 * (pad_mobile[:, :-1] + pad_mobile[:, 1:]) * (pad_surface[:, :-1] - pad_surface[:, 1:])
    sideways = 0.5 * (mobile[..., :-1] + mobile[..., 1:]) * (surface[..., :-1] - surface[..., 1:])
    zero_col = jnp.zeros(water.shape[:2] + (1,), water.dtype)
    inflow_net = across[:, :-1] - across[:, 1:] + jnp.concatenate([zero_col, sideways], -1) - jnp.concatenate([sideways, zero_col], -1)
    return water + flow_rate * inflow_net


def reference(depth, bed, rain, rough_class, class_n, contact_seg, contact_lake, lake_slot, storage, area, release, upstream_link):
    classes = jnp.arange(NCLASS, dtype=jnp.int32)
    inv_n = jnp.sum(jnp.where(rough_class[None] == classes[:, None, None], (1.0 / class_n)[:, None, None], 0.0), axis=0)
    per_row = W // SEG
    segs_dev = R_DEV * per_row
    source = jnp.arange(N_TILES, dtype=jnp.int32)[:, None, None]
    global_seg = (contact_seg + source * segs_dev).reshape(-1).astype(jnp.int32)
    lake_ids = contact_lake.reshape(-1)
    live_mask = lake_ids >= 0
    slots = jnp.where(live_mask, lake_slot[jnp.maximum(lake_ids, 0)], 0).astype(jnp.int32)
    live_float = live_mask.astype(storage.dtype)[None, :, None]
    linked = upstream_link.astype(storage.dtype)
    scale_a = (release * linked).reshape(N_TILES, LAKE_DEV)
    water = depth
    pool_store = storage
    outflow_sum = jnp.zeros_like(storage)
    for routing_step in range(STEPS):
        wetted = surface_flow(water, bed, inv_n) + rain
        pool_level = pool_store / area[None]
        wet_seg = wetted.reshape(MEMB, NY * per_row, SEG)
        bed_seg = bed.reshape(NY * per_row, SEG)
        wet_contact = wet_seg[:, global_seg]
        surf_contact = bed_seg[global_seg][None] + wet_contact
        excess = jnp.maximum(surf_contact - pool_level[:, slots][..., None], 0.0)
        taken_water = drain_rate * wet_contact * excess / (1.0 + excess) * live_float
        water = wet_seg.at[:, global_seg].add(-taken_water).reshape(MEMB, NY, W)
        slot_sums = jnp.sum(taken_water, axis=-1)
        lateral = jax.ops.segment_sum(slot_sums.T, slots, num_segments=LAKES).T / SEG
        scale_b = (release[None] * (pool_store + lateral)).reshape(MEMB, N_TILES, LAKE_DEV).transpose(1, 0, 2)

        def link_step(carried, inputs):
            factor, offset = inputs
            released_now = factor * carried + offset
            return released_now, (released_now, carried)

        start = jnp.zeros((MEMB, LAKE_DEV), storage.dtype)
        unused, (released_blocks, above_blocks) = lax.scan(link_step, start, (scale_a[:, None, :], scale_b))
        released = released_blocks.transpose(1, 0, 2).reshape(MEMB, LAKES)
        from_above = above_blocks.transpose(1, 0, 2).reshape(MEMB, LAKES)
        pool_store = pool_store + lateral + linked[None] * from_above - released
        outflow_sum = outflow_sum + released
    ens_outflow = jnp.sum(outflow_sum, axis=0) / MEMB
    return water, pool_store, ens_outflow
```

```python
import functools
import types

import jax
import jax.numpy as jnp
from jax import lax
from jax.experimental import pallas as pl
from jax.experimental.pallas import tpu as pltpu
from jax.sharding import PartitionSpec as P

SEG = 256
STEPS = 4
LANES = 128
SUBLANES = 8
FAR = 1e30

flow_rate = 0.035
drain_rate = 0.4

F32 = jnp.float32
I32 = jnp.int32
PARAMS = pltpu.CompilerParams(vmem_limit_bytes=24 * 2**20)


def up_to(value, unit):
    return -(-value // unit) * unit


def lane_ids(shape):
    return lax.broadcasted_iota(I32, shape, len(shape) - 1)


def row_ids(shape):
    return lax.broadcasted_iota(I32, shape, len(shape) - 2)


def mobility(water, inv_n):
    return water * jnp.exp2(jnp.log2(jnp.abs(water)) * (2.0 / 3.0)) * inv_n


def taken_of(water, surface, level):
    excess = jnp.maximum(surface - level, 0.0)
    return drain_rate * water * excess / (1.0 + excess)


def in_vmem(x):
    return pltpu.with_memory_space_constraint(x, pltpu.VMEM)


def vmem_out(*shape):
    return pltpu.VMEM(shape, F32)


def plain_out(*shape):
    return jax.ShapeDtypeStruct(shape, F32)


V = pl.BlockSpec(memory_space=pltpu.VMEM)
S = pl.BlockSpec(memory_space=pltpu.SMEM)
A = pl.BlockSpec(memory_space=pl.ANY)


def pack_kernel(
    z, depth, bed, cls, class_n, seg, lake, slot, storage, area, release, link,
    down, up, payload, table, rows, cls_rows, ids, sems,
):
    copies = []
    for side, row in enumerate((z.R - 1, 0)):
        for m in range(z.M):
            copies.append((depth.at[m, pl.ds(row, 1)], rows.at[side, pl.ds(m, 1)]))
        copies.append((bed.at[pl.ds(row, 1)], rows.at[side, pl.ds(z.M, 1)]))
        copies.append((cls.at[pl.ds(row, 1)], cls_rows.at[pl.ds(side, 1)]))
    copies = [pltpu.make_async_copy(a, b, sems.at[i]) for i, (a, b) in enumerate(copies)]
    for copy in copies:
        copy.start()

    lane = lane_ids((1, LANES))
    names = jnp.ones((1, LANES), F32)
    for k in range(z.classes):
        names = jnp.where(lane == k, class_n[k], names)
    table[...] = flow_rate * 0.5 / names

    payload[...] = jnp.zeros_like(payload)
    block = payload.at[0]
    for m in range(z.M):
        block[m : m + 1, : z.LD] = storage[m : m + 1, :]
    for k, ref in enumerate((area, release, link)):
        block[z.M + k : z.M + k + 1, : z.LD] = ref[...].astype(F32)
    for tile in range(z.CT):
        segs = jnp.zeros((1, LANES), I32)
        slots = jnp.full((1, LANES), z.LK, I32)
        for c in range(tile * LANES, min(z.C, (tile + 1) * LANES)):
            owner, place = divmod(c, z.CAP)
            lake_id = lake[0, owner, place]
            found = jnp.where(lake_id >= 0, slot[jnp.maximum(lake_id, 0)], z.LK)
            segs = jnp.where(lane == c - tile * LANES, seg[0, owner, place], segs)
            slots = jnp.where(lane == c - tile * LANES, found, slots)
        r = z.M + 3 + tile
        block[r : r + 1, :] = segs.astype(F32)
        block[r + z.CT : r + z.CT + 1, :] = slots.astype(F32)

    def spread(k, _):
        payload[k] = payload[0]
        return 0

    lax.fori_loop(1, z.E * z.NT, spread, 0)

    for copy in copies:
        copy.wait()
    tbl = jnp.broadcast_to(table[...], (z.PR, LANES))
    for side, out in enumerate((down, up)):
        for g in range(z.PR):
            at = slice(g * SEG, (g + 1) * SEG)
            for m in range(z.M + 1):
                out[m, g : g + 1, :] = rows[side, m : m + 1, at]
            ids[g : g + 1, :] = cls_rows[side : side + 1, at]
        for half in range(0, SEG, LANES):
            at = slice(half, half + LANES)
            out[z.M + 1, :, at] = jnp.take_along_axis(tbl, ids[:, at], axis=1, mode="promise_in_bounds")


def flow_rows(z, water, rain, bed, inv, out, first, last, halo, flag_up, flag_down, edges):
    shape = (z.R, SEG)
    lane = lane_ids(shape)
    row = row_ids(shape)
    right_end = lane == SEG - 1
    left_end = lane == 0
    bottom = row == z.R - 1
    top = row == 0
    keep = jnp.where(bottom, flag_down, 1.0)

    def state(m, j):
        at = pl.ds(pl.multiple_of(j * SEG, SEG), SEG)
        w = water[m, :, at]
        s = bed[:, at] + w
        k = mobility(w, inv[:, at])
        return s, k, pltpu.roll(s, SEG - 1, 1), pltpu.roll(k, SEG - 1, 1)

    def chunk(j, carry):
        at = pl.ds(pl.multiple_of(j * SEG, SEG), SEG)
        ahead = jnp.minimum(j + 1, z.PR - 1)
        inner = jnp.where(j == z.PR - 1, 0.0, 1.0)
        close = jnp.where(right_end, inner, 1.0)
        new = []
        for m in range(z.M):
            s, k, s_left, k_left, before = carry[m]
            s2, k2, s2_left, k2_left = state(m, ahead)
            s_right = jnp.where(right_end, s2_left, s_left)
            k_right = jnp.where(right_end, k2_left, k_left)
            f = (k + k_right) * (s - s_right) * close
            f_roll = pltpu.roll(f, 1, 1)
            net = jnp.where(left_end, before, f_roll) - f
            s_down = pltpu.roll(s, z.R - 1, 0)
            k_down = pltpu.roll(k, z.R - 1, 0)
            if halo is not None:
                hs, hk = halo
                s_down = jnp.where(bottom, hs[1, m, pl.ds(j, 1), :], s_down)
                k_down = jnp.where(bottom, hk[1, m, pl.ds(j, 1), :], k_down)
            v = (k + k_down) * (s - s_down) * keep
            v_up = pltpu.roll(v, 1, 0)
            if halo is not None:
                enter = (k[:1] + hk[0, m, pl.ds(j, 1), :]) * (hs[0, m, pl.ds(j, 1), :] - s[:1])
                v_up = jnp.where(top, enter * flag_up, v_up)
            else:
                v_up = jnp.where(top, 0.0, v_up)
            wet = water[m, :, at] + (net + (v_up - v)) + rain[m, :, at]
            out[m, :, at] = wet
            if edges is not None:
                edges[0][m, pl.ds(j, 1), :] = wet[z.R - 1 :, :]
                edges[1][m, pl.ds(j, 1), :] = wet[:1, :]
            new.append((s2, k2, s2_left, k2_left, f_roll))
        return tuple(new)

    return chunk, state


def run_flow(z, water, rain, bed, inv, out, halo, flag_up, flag_down, edges, gates=None):
    chunk, state = flow_rows(z, water, rain, bed, inv, out, 0, z.PR, halo, flag_up, flag_down, edges)
    parts = len(gates) if gates else 1
    if gates:
        gates[0]()
    zero = jnp.zeros((z.R, SEG), F32)
    carry = tuple(state(m, 0) + (zero,) for m in range(z.M))
    size = z.PR // parts
    unroll = z.unroll
    for p in range(parts):
        begin = p * size - (1 if p else 0)
        end = (p + 1) * size - (1 if p < parts - 1 else 0)
        if gates and p:
            gates[p]()
        carry = lax.fori_loop(begin, end, chunk, carry, unroll=min(unroll, end - begin))


def gather_contacts(z, seg, water, out):
    for c in range(z.C):
        owner, place = divmod(c, z.CAP)
        s = seg[0, owner, place]
        r = s // z.PR
        at = pl.ds(pl.multiple_of((s % z.PR) * SEG, SEG), SEG)
        for m in range(z.M):
            out[m * z.C + c : m * z.C + c + 1, :] = water[m, pl.ds(r, 1), at]


def scatter_contacts(z, seg, values, water):
    for c in range(z.C):
        owner, place = divmod(c, z.CAP)
        s = seg[0, owner, place]
        r = s // z.PR
        at = pl.ds(pl.multiple_of((s % z.PR) * SEG, SEG), SEG)
        for m in range(z.M):
            water[m, pl.ds(r, 1), at] = values[m * z.C + c : m * z.C + c + 1, :]


def first_kernel(z, depth, bed, cls, rain, table, seg, out, bed_v, inv_v, rain_v, bed_c, depth_v, cls_v, sems):
    parts = z.parts
    width = z.W // parts
    copies = []
    for p in range(parts):
        at = pl.ds(p * width, width)
        group = [
            pltpu.make_async_copy(cls.at[:, at], cls_v.at[:, at], sems.at[0, p]),
            pltpu.make_async_copy(bed.at[:, at], bed_v.at[:, at], sems.at[1, p]),
            pltpu.make_async_copy(depth.at[:, :, at], depth_v.at[:, :, at], sems.at[2, p]),
            pltpu.make_async_copy(rain.at[:, :, at], rain_v.at[:, :, at], sems.at[3, p]),
        ]
        for copy in group:
            copy.start()
        copies.append(group)
    tbl = jnp.broadcast_to(table[...], (z.R, LANES))

    def gate(p):
        for copy in copies[p]:
            copy.wait()

        def look(i, _):
            at = pl.ds(pl.multiple_of(p * width + i * LANES, LANES), LANES)
            inv_v[:, at] = jnp.take_along_axis(tbl, cls_v[:, at], axis=1, mode="promise_in_bounds")
            return 0

        lax.fori_loop(0, width // LANES, look, 0, unroll=8)

    gates = [functools.partial(gate, p) for p in range(parts)]
    run_flow(z, depth_v, rain_v, bed_v, inv_v, out, None, 0.0, 0.0, None, gates)
    for c in range(z.C):
        owner, place = divmod(c, z.CAP)
        s = seg[0, owner, place]
        at = pl.ds(pl.multiple_of((s % z.PR) * SEG, SEG), SEG)
        bed_c[c : c + 1, :] = bed_v[pl.ds(s // z.PR, 1), at]


def edge_kernel(z, wet_in, own_down, own_up, from_up, from_down, seg, wet, down, up, wet_c):
    tile = lax.axis_index("tiles")
    for own, other, row, out, there in (
        (own_up, from_up, 0, up, tile > 0),
        (own_down, from_down, z.R - 1, down, tile < z.NT - 1),
    ):
        flag = jnp.where(there, 1.0, 0.0)
        for m in range(z.M):
            s0 = own[z.M] + own[m]
            k0 = mobility(own[m], own[z.M + 1])
            s1 = other[z.M] + other[m]
            k1 = mobility(other[m], other[z.M + 1])
            out[m] = (k0 + k1) * (s1 - s0) * flag
            for g in range(z.PR):
                at = pl.ds(g * SEG, SEG)
                new = wet[m, row : row + 1, at] + out[m, g : g + 1, :]
                wet[m, row : row + 1, at] = new
                out[m, g : g + 1, :] = new
    gather_contacts(z, seg, wet, wet_c)


def flow_kernel(
    z, exchange, wet_in, water_c, level, near_up, near_down, edge_up, edge_down, pack_up, pack_down,
    bed, inv, rain, seg, *rest,
):
    if exchange:
        water, out, wet_c, down, up, hs, hk = rest
    else:
        water, out, wet_c, hs, hk = rest
    tile = lax.axis_index("tiles")
    flag_up = jnp.where(tile > 0, 1.0, 0.0)
    flag_down = jnp.where(tile < z.NT - 1, 1.0, 0.0)
    scatter_contacts(z, seg, water_c, water)
    for side, (near, edge, pack) in enumerate(((near_up, edge_up, pack_up), (near_down, edge_down, pack_down))):
        for m in range(z.M):
            w = edge[m]
            w = w - taken_of(w, pack[z.M] + w, pick(z, near, level, m))
            hs[side, m] = pack[z.M] + w
            hk[side, m] = mobility(w, pack[z.M + 1])
    run_flow(z, water, rain, bed, inv, out, (hs, hk), flag_up, flag_down, (down, up) if exchange else None)
    gather_contacts(z, seg, out, wet_c)


def last_kernel(z, wet_in, water_c, seg, water, new_depth, sem):
    scatter_contacts(z, seg, water_c, water)
    copy = pltpu.make_async_copy(water, new_depth, sem)
    copy.start()
    copy.wait()


def pick(z, near, table, m):
    total = near[0] * table[m * z.LT : m * z.LT + 1, :]
    for j in range(1, z.LT):
        total += near[j] * table[m * z.LT + j : m * z.LT + j + 1, :]
    return jnp.sum(total, axis=1, keepdims=True)


def shift_slots(x, count):
    rows, lanes = divmod(count, LANES)
    size = x.shape[0]
    turned = pltpu.roll(x, lanes, 1) if lanes else x
    low = pltpu.roll(turned, rows % size, 0) if rows % size else turned
    if not lanes:
        return low
    high = pltpu.roll(turned, (rows + 1) % size, 0)
    return jnp.where(lane_ids(x.shape) < lanes, high, low)


def laps(z):
    count = z.LD
    while count < z.LK:
        yield count
        count *= 2


def slot_ids(z):
    shape = (z.SR, LANES)
    return (row_ids(shape) % z.LT) * LANES + lane_ids(shape)


def levels_of(z, pool, area):
    return jnp.where(slot_ids(z) == z.LK, FAR, pool / area)


def setup_levels(z, got, seg_slot, pool, consts, near, near_up, near_down):
    tile = lax.axis_index("tiles")
    pool[...] = jnp.zeros_like(pool)
    consts[...] = jnp.zeros_like(consts)
    consts[0] = jnp.ones((z.SR, LANES), F32)
    for t in range(z.NT):
        done = 0
        while done < z.LD:
            j, at = divmod(t * z.LD + done, LANES)
            n = min(z.LD - done, LANES - at)
            for m in range(z.M):
                r = m * z.LT + j
                for e in range(z.E):
                    pool[e, r : r + 1, at : at + n] = got[e * z.NT + t, m : m + 1, done : done + n]
                for k in range(3):
                    consts[k, r : r + 1, at : at + n] = got[t, z.M + k : z.M + k + 1, done : done + n]
            done += n
    slot = slot_ids(z)
    consts[2] = jnp.where(slot >= z.LD, consts[2], 0.0)
    factor = consts[1] * consts[2]
    for lap, count in enumerate(laps(z)):
        consts[3 + lap] = factor
        factor = factor * shift_slots(factor, count)


def one_hots(z, block, near, base, rows):
    found = jnp.zeros((rows, 1), F32)
    for tile in range(z.CT):
        r = z.M + 3 + tile
        live = lane_ids((rows, LANES)) + tile * LANES < z.C
        target = (row_ids((rows, LANES)) + base).astype(F32)
        segs = block[r : r + 1, :]
        slots = block[r + z.CT : r + z.CT + 1, :]
        found += jnp.sum(jnp.where((segs == target) & live, slots - z.LK, 0.0), axis=1, keepdims=True)
    found += float(z.LK)
    for j in range(z.LT):
        near[j] = jnp.where(found == (lane_ids((rows, LANES)) + j * LANES).astype(F32), 1.0, 0.0)


def own_hots(z, block, near):
    found = jnp.zeros((z.C, 1), F32)
    for tile in range(z.CT):
        r = z.M + 3 + z.CT + tile
        same = lane_ids((z.C, LANES)) + tile * LANES == row_ids((z.C, LANES))
        found += jnp.sum(jnp.where(same, block[r : r + 1, :], 0.0), axis=1, keepdims=True)
    for j in range(z.LT):
        near[j] = jnp.where(found == (lane_ids((z.C, LANES)) + j * LANES).astype(F32), 1.0, 0.0)


def contact_step(z, level, near, wet_c, bed_c, water_c, payload):
    rows = []
    bed = bed_c[...]
    for m in range(z.M):
        w = wet_c[m * z.C : (m + 1) * z.C, :]
        taken = taken_of(w, bed + w, pick(z, near, level, m))
        water_c[m * z.C : (m + 1) * z.C, :] = w - taken
        sums = jnp.sum(taken, axis=1, keepdims=True) * (1.0 / SEG)
        for j in range(z.LT):
            rows.append(jnp.sum(near[j] * sums, axis=0, keepdims=True))
    spare = z.SR - len(rows)
    if spare:
        rows.append(jnp.zeros((spare, LANES), F32))
    block = jnp.concatenate(rows, axis=0)
    for k in range(z.E * z.NT):
        payload[k] = block


def open_kernel(z, got, wet_c, bed_c, pool, consts, near, near_up, near_down, level, water_c, payload):
    tile = lax.axis_index("tiles")
    member = lax.axis_index("ens")
    setup_levels(z, got, None, pool, consts, near, near_up, near_down)
    own_hots(z, got.at[member * z.NT + tile], near)
    above = jnp.maximum(tile - 1, 0)
    below = jnp.minimum(tile + 1, z.NT - 1)
    one_hots(z, got.at[member * z.NT + above], near_up, (z.R - 1) * z.PR, z.PR)
    one_hots(z, got.at[member * z.NT + below], near_down, 0, z.PR)
    level[...] = levels_of(z, pool[member], consts[0])
    contact_step(z, level, near, wet_c, bed_c, water_c, payload)


def reservoirs(z, got, pool_in, sum_in, consts, pool, total, e):
    area, release, link = consts[0], consts[1], consts[2]
    lateral = got[e * z.NT]
    for t in range(1, z.NT):
        lateral += got[e * z.NT + t]
    store = pool_in[e]
    released = release * (store + lateral)
    for lap, count in enumerate(laps(z)):
        released += consts[3 + lap] * shift_slots(released, count)
    new = store + lateral + link * shift_slots(released, z.LD) - released
    pool[e] = new
    total[e] = released if sum_in is None else sum_in[e] + released


def contact_kernel(z, first, got, pool_in, *rest):
    if first:
        sum_in = None
        consts, near, wet_c, bed_c, pool, total, level, water_c, payload = rest
    else:
        sum_in, consts, near, wet_c, bed_c, pool, total, level, water_c, payload = rest
    for e in range(z.E):
        reservoirs(z, got, pool_in, sum_in, consts, pool, total, e)
    level[...] = levels_of(z, pool[lax.axis_index("ens")], consts[0])
    contact_step(z, level, near, wet_c, bed_c, water_c, payload)


def own_slots(z, x, tile):
    begin = tile * z.LD
    at = begin % LANES
    j = begin // LANES
    out = jnp.zeros((1, LANES), F32)
    turned = pltpu.roll(x, LANES - at, 1)
    lane = lane_ids((1, LANES))
    for k in range(z.LT):
        out = jnp.where((j == k) & (lane < LANES - at), turned[k : k + 1], out)
        out = jnp.where((j + 1 == k) & (lane >= LANES - at), turned[k : k + 1], out)
    return out


def close_kernel(z, got, pool_in, sum_in, consts, storage, outflow, pool, total):
    tile = lax.axis_index("tiles")
    member = lax.axis_index("ens")
    for e in range(z.E):
        reservoirs(z, got, pool_in, sum_in, consts, pool, total, e)
    for m in range(z.M):
        at = slice(m * z.LT, (m + 1) * z.LT)
        storage[m : m + 1, :] = own_slots(z, pool[member, at], tile)[:, : z.LD]
    summed = total[0]
    for e in range(1, z.E):
        summed += total[e]
    mean = summed[: z.LT]
    for m in range(1, z.M):
        mean += summed[m * z.LT : (m + 1) * z.LT]
    outflow[...] = own_slots(z, mean, tile)[:, : z.LD] * (1.0 / (z.M * z.E))


def shards(
    depth, bed, rain, rough_class, class_n, contact_seg, contact_lake, lake_slot, storage, area, release, upstream_link
):
    z = types.SimpleNamespace()
    z.M, z.R, z.W = depth.shape
    z.NT = lax.axis_size("tiles")
    z.E = lax.axis_size("ens")
    z.LD = storage.shape[1]
    z.LK = z.NT * z.LD
    z.CAP = contact_seg.shape[2]
    z.C = contact_seg.shape[1] * z.CAP
    z.CT = -(-z.C // LANES)
    z.PR = z.W // SEG
    z.classes = class_n.shape[0]
    z.LT = z.LK // LANES + 1
    z.SR = up_to(z.M * z.LT, SUBLANES)
    z.BR = up_to(z.M + 3 + 2 * z.CT, SUBLANES)
    z.unroll = 4
    z.parts = 4
    peers = z.E * z.NT
    levels = len(list(laps(z)))
    forward = [(i, i + 1) for i in range(z.NT - 1)]
    backward = [(b, a) for a, b in forward]

    def call(kernel, ins, outs, specs_in, specs_out, scratch=(), alias=None, **extra):
        return pl.pallas_call(
            functools.partial(kernel, z),
            out_shape=outs,
            in_specs=specs_in,
            out_specs=specs_out,
            scratch_shapes=list(scratch),
            input_output_aliases=alias or {},
            compiler_params=PARAMS,
            **extra,
        )(*ins)

    def share(x):
        return lax.all_to_all(x, ("ens", "tiles"), 0, 0, tiled=True)

    def halo(down, up):
        return lax.ppermute(down, "tiles", forward), lax.ppermute(up, "tiles", backward)

    n_copies = 2 * (z.M + 2)
    down0, up0, opening, table = call(
        pack_kernel,
        (depth, bed, rough_class, class_n, contact_seg, contact_lake, lake_slot, storage,
         area.reshape(1, -1), release.reshape(1, -1), upstream_link.reshape(1, -1)),
        (plain_out(z.M + 2, z.PR, SEG), plain_out(z.M + 2, z.PR, SEG), plain_out(peers, z.BR, LANES), vmem_out(1, LANES)),
        [A, A, A, S, S, S, S, V, V, V, V],
        [V, V, V, V],
        [pltpu.VMEM((2, z.M + 1, z.W), F32), pltpu.VMEM((2, z.W), I32), pltpu.VMEM((z.PR, SEG), I32),
         pltpu.SemaphoreType.DMA((n_copies,))],
    )
    pack_up, pack_down = halo(down0, up0)
    opened = share(opening)

    wet, bed_v, inv_v, rain_v, bed_c = call(
        first_kernel,
        (depth, bed, rough_class, rain, in_vmem(table), contact_seg),
        (vmem_out(z.M, z.R, z.W), vmem_out(z.R, z.W), vmem_out(z.R, z.W), vmem_out(z.M, z.R, z.W), vmem_out(z.C, SEG)),
        [A, A, A, A, V, S],
        [V, V, V, V, V],
        [pltpu.VMEM((z.M, z.R, z.W), F32), pltpu.VMEM((z.R, z.W), I32), pltpu.SemaphoreType.DMA((4, z.parts))],
    )
    wet, down, up, wet_c = call(
        edge_kernel,
        (in_vmem(wet), down0, up0, pack_up, pack_down, contact_seg),
        (vmem_out(z.M, z.R, z.W), plain_out(z.M, z.PR, SEG), plain_out(z.M, z.PR, SEG), vmem_out(z.M * z.C, SEG)),
        [V, V, V, V, V, S],
        [V, V, V, V],
        alias={0: 0},
    )
    edge_up, edge_down = halo(down, up)

    state = vmem_out(z.E, z.SR, LANES)
    pool, consts, near, near_up, near_down, level, water_c, payload = call(
        open_kernel,
        (opened, in_vmem(wet_c), in_vmem(bed_c)),
        (state, vmem_out(3 + levels, z.SR, LANES), vmem_out(z.LT, z.C, LANES), vmem_out(z.LT, z.PR, LANES),
         vmem_out(z.LT, z.PR, LANES), vmem_out(z.SR, LANES), vmem_out(z.M * z.C, SEG), plain_out(peers, z.SR, LANES)),
        [V, V, V],
        [V] * 8,
    )
    total = None
    for step in range(1, STEPS + 1):
        got = share(payload)
        if step == STEPS:
            _, new_depth = call(
                last_kernel,
                (in_vmem(wet), in_vmem(water_c), contact_seg),
                (vmem_out(z.M, z.R, z.W), plain_out(z.M, z.R, z.W)),
                [V, V, S],
                [V, A],
                [pltpu.SemaphoreType.DMA],
                alias={0: 0},
            )
            break
        exchange = step < STEPS - 1
        edge_shape = (plain_out(z.M, z.PR, SEG),) * (2 if exchange else 0)
        results = call(
            lambda zz, *refs, exchange=exchange: flow_kernel(zz, exchange, *refs),
            (in_vmem(wet), in_vmem(water_c), in_vmem(level), in_vmem(near_up), in_vmem(near_down), edge_up, edge_down,
             pack_up, pack_down, in_vmem(bed_v), in_vmem(inv_v), in_vmem(rain_v), contact_seg),
            (vmem_out(z.M, z.R, z.W), vmem_out(z.M, z.R, z.W), vmem_out(z.M * z.C, SEG)) + edge_shape,
            [V] * 12 + [S],
            [V] * (3 + len(edge_shape)),
            [pltpu.VMEM((2, z.M, z.PR, SEG), F32)] * 2,
            alias={0: 0},
        )
        wet, wet_c = results[1], results[2]
        if exchange:
            edge_up, edge_down = halo(results[3], results[4])
        sums = () if total is None else (in_vmem(total),)
        pool, total, level, water_c, payload = call(
            lambda zz, *refs, first=total is None: contact_kernel(zz, first, *refs),
            (got, in_vmem(pool)) + sums + (in_vmem(consts), in_vmem(near), in_vmem(wet_c), in_vmem(bed_c)),
            (state, state, vmem_out(z.SR, LANES), vmem_out(z.M * z.C, SEG), plain_out(peers, z.SR, LANES)),
            [V] * (6 + len(sums)),
            [V] * 5,
        )
    new_storage, outflow = call(
        close_kernel,
        (got, in_vmem(pool), in_vmem(total), in_vmem(consts)),
        (plain_out(z.M, z.LD), plain_out(1, z.LD)),
        [V] * 4,
        [V] * 2,
        [pltpu.VMEM((z.E, z.SR, LANES), F32)] * 2,
    )
    return new_depth, new_storage, outflow.reshape(-1)


def solution(mesh):
    return jax.shard_map(
        shards,
        mesh=mesh,
        in_specs=(
            P("ens", "tiles", None),
            P("tiles", None),
            P("ens", "tiles", None),
            P("tiles", None),
            P(),
            P("tiles", None, None),
            P("tiles", None, None),
            P(),
            P("ens", "tiles"),
            P("tiles"),
            P("tiles"),
            P("tiles"),
        ),
        out_specs=(P("ens", "tiles", None), P("ens", "tiles"), P("tiles")),
        check_vma=False,
    )
```

```python
import functools
import types

import jax
import jax.numpy as jnp
from jax import lax
from jax.experimental import pallas as pl
from jax.experimental.pallas import tpu as pltpu
from jax.sharding import PartitionSpec as P

SEG = 256
STEPS = 4
LANES = 128
SUBLANES = 8
FAR = 1e30

flow_rate = 0.035
drain_rate = 0.4

F32 = jnp.float32
I32 = jnp.int32
VMEM_LIMIT = 40 * 2**20
BLOCK = 4096


def up_to(value, unit):
    return -(-value // unit) * unit


def lane_ids(shape):
    return lax.broadcasted_iota(I32, shape, len(shape) - 1)


def row_ids(shape):
    return lax.broadcasted_iota(I32, shape, len(shape) - 2)


def mobility(water, inv_n):
    return water * jnp.exp2(jnp.log2(jnp.abs(water)) * (2.0 / 3.0)) * inv_n


def taken_of(water, surface, level):
    excess = jnp.maximum(surface - level, 0.0)
    return drain_rate * water * excess / (1.0 + excess)


class Array:
    def __init__(self, kernel, h, v):
        self.kernel, self.h, self.v = kernel, h, v

    def load(self):
        self.coming = self.kernel.copy(self.h, self.v)

    def wait(self):
        self.coming.wait()

    def send(self):
        self.kernel.stores.append(self.kernel.copy(self.v, self.h))


class Kernel:
    def __init__(self, sems):
        self.sems, self.count, self.stores = sems, 0, []

    def copy(self, source, target):
        copy = pltpu.make_async_copy(source, target, self.sems.at[self.count])
        self.count += 1
        copy.start()
        return copy

    def finish(self):
        for copy in self.stores:
            copy.wait()


def load(*arrays):
    for array in arrays:
        array.load()


def wait(*arrays):
    for array in arrays:
        array.wait()


def send(*arrays):
    for array in arrays:
        array.send()


class Staged:
    space = pltpu.VMEM

    def __init__(self, x):
        self.x = x


class Scalars(Staged):
    space = pltpu.SMEM


class Raw(Staged):
    space = None


class Here(Staged):
    space = None


def staged_call(body, z, ins, outs, scratch=None, alias=None, extra_sems=0, micros=60):
    scratch = scratch or {}
    ins = {n: x if isinstance(x, Staged) else Staged(x) for n, x in ins.items()}
    outs = {n: x if isinstance(x, Raw) else Staged(x) for n, x in outs.items()}
    shapes = [x.space(x.x.shape, x.x.dtype) for x in ins.values() if x.space]
    shapes += [x.space(x.x, F32) for x in outs.values() if x.space]
    count = len(shapes) + extra_sems
    shapes += list(scratch.values())
    shapes.append(pltpu.SemaphoreType.DMA((count,)))

    def kernel(*refs):
        refs = list(refs)
        k = Kernel(refs.pop())
        arrays_in, arrays_out = [{n: refs.pop(0) for n in names} for names in (ins, outs)]
        for held, kinds in ((arrays_in, ins), (arrays_out, outs)):
            for n, x in kinds.items():
                held[n] = Array(k, held[n], refs.pop(0) if x.space else held[n])
        k.i = types.SimpleNamespace(**arrays_in)
        k.o = types.SimpleNamespace(**arrays_out)
        k.s = types.SimpleNamespace(**{n: refs.pop(0) for n in scratch})
        body(z, k)
        k.finish()

    in_hbm = pl.BlockSpec(memory_space=pltpu.HBM)
    in_vmem = pl.BlockSpec(memory_space=pltpu.VMEM)
    order_in, order_out = list(ins), list(outs)
    results = pl.pallas_call(
        kernel,
        out_shape=[pltpu.HBM(x.x, F32) for x in outs.values()],
        in_specs=[in_vmem if isinstance(x, Here) else in_hbm for x in ins.values()],
        out_specs=[in_hbm] * len(outs),
        scratch_shapes=shapes,
        input_output_aliases={order_in.index(a): order_out.index(b) for a, b in (alias or {}).items()},
        compiler_params=pltpu.CompilerParams(vmem_limit_bytes=VMEM_LIMIT),
        cost_estimate=pl.CostEstimate(
            flops=int(micros * 1e9), transcendentals=int(micros * 1e6), bytes_accessed=int(micros * 3e6)
        ),
    )(*[x.x if isinstance(x, Here) else pltpu.with_memory_space_constraint(x.x, pltpu.HBM) for x in ins.values()])
    return types.SimpleNamespace(**dict(zip(order_out, results)))


def side_of(n):
    tile = lax.axis_index("tiles")
    odd = tile % 2
    side = 1 - odd if n == 0 else odd
    there = jnp.where(side == 0, tile > 0, tile < lax.axis_size("tiles") - 1)
    return side, jnp.where(there, 1.0, 0.0)


def pack_kernel(z, k):
    small = k.i.class_n, k.i.storage, k.i.area, k.i.release, k.i.link
    load(*small)
    rows, cls_rows = k.s.rows, k.s.cls_rows
    copies = []
    for side, row in enumerate((0, z.R - 1)):
        for m in range(z.M):
            copies.append(k.copy(k.i.depth.h.at[m, pl.ds(row, 1)], rows.at[side, pl.ds(m, 1)]))
        copies.append(k.copy(k.i.bed.h.at[pl.ds(row, 1)], rows.at[side, pl.ds(z.M, 1)]))
        copies.append(k.copy(k.i.cls.h.at[pl.ds(row, 1)], cls_rows.at[side]))
    wait(*small)
    payload = k.o.payload.v
    payload[0] = jnp.zeros((z.BR, LANES), F32)
    payload[0, : z.M, : z.LD] = k.i.storage.v[...]
    for n, x in enumerate((k.i.area, k.i.release, k.i.link)):
        payload[0, z.M + n : z.M + n + 1, : z.LD] = x.v[...].astype(F32)
    for n in range(1, z.NT):
        payload[n] = payload[0]
    k.o.payload.send()
    wide = inv_table(z, k.i.class_n.v, z.PR)
    for copy in copies:
        copy.wait()
    ids = k.s.ids
    for n, out in enumerate((k.o.pack0, k.o.pack1)):
        side, _ = side_of(n)
        for g in range(z.PR):
            at = slice(g * SEG, (g + 1) * SEG)
            for m in range(z.M + 1):
                out.v[m, g : g + 1, :] = rows[side, m : m + 1, at]
            ids[g : g + 1, :] = cls_rows[side, :, at]
        for half in range(0, SEG, LANES):
            at = slice(half, half + LANES)
            out.v[z.M + 1, :, at] = look_up(wide, ids[:, at])
        out.send()


def inv_table(z, class_n, rows):
    lane = lane_ids((rows, LANES))
    names = jnp.ones((rows, LANES), F32)
    for n in range(z.classes):
        names = jnp.where(lane == n, class_n[n], names)
    return flow_rate * 0.5 / names


def look_up(table, ids):
    return jnp.take_along_axis(table, ids, axis=1, mode="promise_in_bounds")


def widen(z, ref, index=(), left=True, right=True):
    rows = slice(None)
    if left:
        ref[index + (rows, slice(0, LANES))] = pltpu.roll(ref[index + (rows, slice(LANES, 2 * LANES))], LANES - 1, 1)
    if right:
        ref[index + (rows, slice(z.W + LANES, z.W + 2 * LANES))] = pltpu.roll(
            ref[index + (rows, slice(z.W, z.W + LANES))], 1, 1
        )


def flow_blocks(z, water, bed, inv, rain, out, edges, done, ready=None):
    size = min(BLOCK, z.W)
    segs = size // SEG
    row = row_ids((z.R, size))
    bottom = row == z.R - 1
    top = row == 0

    def block(j, _):
        base = j * size if ready else pl.multiple_of(j * size, size)
        wide = pl.ds(base, size + 2 * LANES)
        at = pl.ds(base, size)
        b, v = bed[:, wide], inv[:, wide]
        for m in range(z.M):
            w = water[m, :, wide]
            s = b + w
            q = mobility(w, v)
            s_right = pltpu.roll(s, size + 2 * LANES - 1, 1)
            q_right = pltpu.roll(q, size + 2 * LANES - 1, 1)
            f = ((q + q_right) * (s - s_right))[:, : size + LANES]
            net = pltpu.roll(f, 1, 1)[:, LANES:] - f[:, LANES:]
            s = s[:, LANES : size + LANES]
            q = q[:, LANES : size + LANES]
            flow = (q + pltpu.roll(q, z.R - 1, 0)) * (s - pltpu.roll(s, z.R - 1, 0))
            flow = jnp.where(bottom, 0.0, flow)
            above = jnp.where(top, 0.0, pltpu.roll(flow, 1, 0))
            wet = w[:, LANES : size + LANES] + (net + (above - flow)) + rain[m, :, at]
            out[m, :, at] = wet
            for i in range(segs):
                part = slice(i * SEG, (i + 1) * SEG)
                edges[0, m, pl.ds(j * segs + i, 1), :] = wet[:1, part]
                edges[1, m, pl.ds(j * segs + i, 1), :] = wet[z.R - 1 :, part]
        done(j, at)
        return 0

    if ready:
        for j in range(z.W // size):
            ready(j)
            block(j, 0)
    else:
        lax.fori_loop(0, z.W // size, block, 0)


def send_blocks(z, k, source, target):
    size = min(BLOCK, z.W)
    first = k.count
    k.count += z.W // size

    def copy(j):
        at = pl.ds(pl.multiple_of(j * size, size), size)
        return pltpu.make_async_copy(source.at[:, :, at], target.at[:, :, at], k.sems.at[first + j])

    for j in range(z.W // size):
        k.stores.append(copy(j))
    return lambda j, at: copy(j).start()


def contact_places(z, seg):
    for c in range(z.C):
        owner, place = divmod(c, z.CAP)
        s = seg[0, owner, place]
        yield c, s // z.PR, pl.multiple_of((s % z.PR) * SEG, SEG)


def gather_contacts(z, seg, water, out):
    for c, r, at in contact_places(z, seg):
        for m in range(z.M):
            out[m * z.C + c : m * z.C + c + 1, :] = water[m, pl.ds(r, 1), pl.ds(at, SEG)]


def scatter_contacts(z, seg, values, water, shift):
    for c, r, at in contact_places(z, seg):
        for m in range(z.M):
            water[m, pl.ds(r, 1), pl.ds(at + shift, SEG)] = values[m * z.C + c : m * z.C + c + 1, :]


def set_edges(z, edges, water, shift):
    for side, row in enumerate((0, z.R - 1)):
        for m in range(z.M):
            for g in range(z.PR):
                at = slice(g * SEG + shift, (g + 1) * SEG + shift)
                water[m, row : row + 1, at] = edges[side, m, g : g + 1, :]


def first_kernel(z, k):
    size = min(BLOCK, z.W)
    parts = z.W // size
    small = k.i.class_n, k.i.seg, k.i.lake, k.i.slot
    load(*small)
    inv, bed, water, cls, rain = k.s.inv, k.s.bed, k.s.water, k.s.cls, k.s.rain
    coming = []
    for p in range(parts):
        at, inner = pl.ds(p * size, size), pl.ds(p * size + LANES, size)
        coming.append([
            k.copy(k.i.cls.h.at[:, at], cls.at[:, at]),
            k.copy(k.i.bed.h.at[:, at], bed.at[:, inner]),
            k.copy(k.i.depth.h.at[:, :, at], water.at[:, :, inner]),
            k.copy(k.i.rain.h.at[:, :, at], rain.at[:, :, at]),
        ])
    wait(*small)
    table = inv_table(z, k.i.class_n.v, z.R)
    one_hots(z, k)
    send(k.o.near, k.o.near_edges)

    def prepare(p):
        for copy in coming[p]:
            copy.wait()

        def look(i, _):
            at = pl.multiple_of(p * size + i * LANES, LANES)
            inv[:, pl.ds(at + LANES, LANES)] = look_up(table, cls[:, pl.ds(at, LANES)])
            return 0

        lax.fori_loop(0, size // LANES, look, 0, unroll=16)
        sides = dict(left=p == 0, right=p == parts - 1)
        widen(z, inv, **sides)
        widen(z, bed, **sides)
        for m in range(z.M):
            widen(z, water, (m,), **sides)
        at, inner = pl.ds(p * size, size), pl.ds(p * size + LANES, size)
        k.stores.append(k.copy(inv.at[:, inner], k.o.inv.h.at[:, at]))

    def ready(j):
        if j == 0:
            prepare(0)
        if j + 1 < parts:
            prepare(j + 1)

    done = send_blocks(z, k, k.s.out, k.o.wet.h)
    flow_blocks(z, water, bed, inv, rain, k.s.out, k.o.edges.v, done, ready)
    k.o.edges.send()
    gather_contacts(z, k.i.seg.v, k.s.out, k.o.wet_c.v)
    for c, r, at in contact_places(z, k.i.seg.v):
        k.o.bed_c.v[c : c + 1, :] = bed[pl.ds(r, 1), pl.ds(at + LANES, SEG)]
    send(k.o.wet_c, k.o.bed_c)


def one_hots(z, k):
    lane = lane_ids((1, LANES))
    contact = row_ids((z.C, LANES))
    place_g = row_ids((z.PR, LANES))
    inside = jnp.full((z.C, 1), z.LK, F32)
    on_edge = [jnp.full((z.PR, 1), z.LK, F32) for _ in range(2)]
    firsts = (0, (z.R - 1) * z.PR)
    for tile in range(z.CT):
        segs = jnp.full((1, LANES), -1, I32)
        slots = jnp.full((1, LANES), z.LK, I32)
        for c in range(tile * LANES, min(z.C, (tile + 1) * LANES)):
            owner, place = divmod(c, z.CAP)
            lake_id = k.i.lake.v[0, owner, place]
            found = jnp.where(lake_id >= 0, k.i.slot.v[jnp.maximum(lake_id, 0)], z.LK)
            segs = jnp.where(lane == c - tile * LANES, k.i.seg.v[0, owner, place], segs)
            slots = jnp.where(lane == c - tile * LANES, found, slots)
        more = (slots - z.LK).astype(F32)
        central = (segs >= z.PR) & (segs < firsts[1])
        mine = lane_ids((z.C, LANES)) + tile * LANES == contact
        inside += jnp.sum(jnp.where(mine & central, more, 0.0), axis=1, keepdims=True)
        for side in range(2):
            here = place_g + firsts[side] == segs
            on_edge[side] += jnp.sum(jnp.where(here, more, 0.0), axis=1, keepdims=True)
    for j in range(z.LT):
        k.o.near.v[j] = jnp.where(inside == (lane_ids((z.C, LANES)) + j * LANES).astype(F32), 1.0, 0.0)
        for side in range(2):
            ids = (lane_ids((z.PR, LANES)) + j * LANES).astype(F32)
            k.o.near_edges.v[side * z.LT + j] = jnp.where(on_edge[side] == ids, 1.0, 0.0)


def flow_kernel(z, k):
    size = min(BLOCK, z.W)
    parts = z.W // size
    inv, bed, water, rain = k.s.inv, k.s.bed, k.s.water, k.s.rain
    load(k.i.seg, k.i.water_c)
    whole = k.copy(k.i.wet.h, water.at[:, :, pl.ds(LANES, z.W)])
    k.i.edges.load()
    coming = []
    for p in range(parts):
        at, inner = pl.ds(p * size, size), pl.ds(p * size + LANES, size)
        coming.append([
            k.copy(k.i.bed.h.at[:, at], bed.at[:, inner]),
            k.copy(k.i.inv.h.at[:, at], inv.at[:, inner]),
            k.copy(k.i.rain.h.at[:, :, at], rain.at[:, :, at]),
        ])
    wait(k.i.seg, k.i.water_c)
    whole.wait()
    scatter_contacts(z, k.i.seg.v, k.i.water_c.v, water, LANES)
    k.i.edges.wait()
    set_edges(z, k.i.edges.v, water, LANES)
    for m in range(z.M):
        widen(z, water, (m,))

    def prepare(p):
        for copy in coming[p]:
            copy.wait()
        sides = dict(left=p == 0, right=p == parts - 1)
        widen(z, inv, **sides)
        widen(z, bed, **sides)

    def ready(j):
        if j == 0:
            prepare(0)
        if j + 1 < parts:
            prepare(j + 1)

    done = send_blocks(z, k, k.s.out, k.o.next.h)
    flow_blocks(z, water, bed, inv, rain, k.s.out, k.o.edges.v, done, ready)
    k.o.edges.send()
    gather_contacts(z, k.i.seg.v, k.s.out, k.o.wet_c.v)
    k.o.wet_c.send()


def last_kernel(z, k):
    load(k.i.wet, k.i.seg, k.i.water_c, k.i.edges)
    wait(k.i.wet, k.i.seg, k.i.water_c, k.i.edges)
    scatter_contacts(z, k.i.seg.v, k.i.water_c.v, k.i.wet.v, 0)
    set_edges(z, k.i.edges.v, k.i.wet.v, 0)
    k.stores.append(k.copy(k.i.wet.v, k.o.depth.h))


def pick(z, near, table, m):
    total = near[0] * table[m * z.LT : m * z.LT + 1, :]
    for j in range(1, z.LT):
        total += near[j] * table[m * z.LT + j : m * z.LT + j + 1, :]
    return jnp.sum(total, axis=1, keepdims=True)


def shift_slots(x, count):
    rows, lanes = divmod(count, LANES)
    size = x.shape[0]
    turned = pltpu.roll(x, lanes, 1) if lanes else x
    low = pltpu.roll(turned, rows % size, 0) if rows % size else turned
    if not lanes:
        return low
    high = pltpu.roll(turned, (rows + 1) % size, 0)
    return jnp.where(lane_ids(x.shape) < lanes, high, low)


def laps(z):
    count = z.LD
    while count < z.LK:
        yield count
        count *= 2


def cascade(z, consts, entering):
    for lap, count in enumerate(laps(z)):
        entering = entering + consts[3 + lap] * shift_slots(entering, count)
    return entering


def slot_ids(z):
    shape = (z.SR, LANES)
    return (row_ids(shape) % z.LT) * LANES + lane_ids(shape)


def levels_of(z, pool, area):
    return jnp.where(slot_ids(z) == z.LK, FAR, pool / area)


def lay_out(z, got, pool, consts):
    pool[...] = jnp.zeros_like(pool)
    consts[...] = jnp.zeros_like(consts)
    consts[0] = jnp.ones((z.SR, LANES), F32)
    for t in range(z.NT):
        done = 0
        while done < z.LD:
            j, at = divmod(t * z.LD + done, LANES)
            n = min(z.LD - done, LANES - at)
            for m in range(z.M):
                r = m * z.LT + j
                pool[r : r + 1, at : at + n] = got[t, m : m + 1, done : done + n]
                for i in range(3):
                    consts[i, r : r + 1, at : at + n] = got[t, z.M + i : z.M + i + 1, done : done + n]
            done += n
    consts[2] = jnp.where(slot_ids(z) >= z.LD, consts[2], 0.0)
    factor = consts[1] * consts[2]
    for lap, count in enumerate(laps(z)):
        consts[3 + lap] = factor
        factor = factor * shift_slots(factor, count)


def cross_edges(z, k, own, other, rows):
    for n in range(2):
        side, flag = side_of(n)
        own_bed, own_inv, other_bed, other_inv = rows(side, n)
        for m in range(z.M):
            a, b = own(side, n, m), other(n, m)
            flow = (mobility(a, own_inv) + mobility(b, other_inv)) * ((other_bed + b) - (own_bed + a))
            k.i.edges.v[side, m] += flow * flag


def contact_step(z, k, level, bed_rows):
    rows = [[jnp.zeros((SUBLANES, LANES), F32) for _ in range(z.LT)] for _ in range(z.M)]

    def take(near, m, w, bed):
        taken = taken_of(w, bed + w, pick(z, near, level, m))
        sums = jnp.sum(taken, axis=1, keepdims=True) * (1.0 / SEG)
        for j in range(z.LT):
            part = near[j] * sums
            for r in range(0, part.shape[0], SUBLANES):
                rows[m][j] += part[r : r + SUBLANES]
        return w - taken

    for side in range(2):
        near = k.i.near_edges.v.at[pl.ds(side * z.LT, z.LT)]
        for m in range(z.M):
            k.o.edges.v[side, m] = take(near, m, k.i.edges.v[side, m], bed_rows(side))
    bed = k.i.bed_c.v[...]
    for m in range(z.M):
        at = slice(m * z.C, (m + 1) * z.C)
        k.o.water_c.v[at, :] = take(k.i.near.v, m, k.i.wet_c.v[at, :], bed)
    found = [jnp.sum(rows[m][j], axis=0, keepdims=True) for m in range(z.M) for j in range(z.LT)]
    if z.SR > len(found):
        found.append(jnp.zeros((z.SR - len(found), LANES), F32))
    return jnp.concatenate(found, axis=0)


def send_edges(z, k, exchange):
    k.o.edges.send()
    if exchange:
        for n, out in enumerate((k.o.edge0, k.o.edge1)):
            side, _ = side_of(n)
            k.stores.append(k.copy(k.o.edges.v.at[side], out.h))


def open_kernel(z, k):
    load(k.i.edges, k.i.own0, k.i.own1, k.i.near, k.i.near_edges, k.i.wet_c, k.i.bed_c)
    own, other, pack = (k.i.own0, k.i.own1), (k.i.from0, k.i.from1), k.o.pack.v
    wait(k.i.edges, k.i.own0, k.i.own1)
    for n in range(2):
        side, _ = side_of(n)
        pack[side, :2] = own[n].v[z.M : z.M + 2]
        pack[side, 2:] = other[n].v[z.M : z.M + 2]
    k.o.pack.send()
    cross_edges(
        z, k,
        lambda side, n, m: own[n].v[m],
        lambda n, m: other[n].v[m],
        lambda side, n: [pack[side, i] for i in range(4)],
    )
    pool, consts = k.s.pool, k.o.consts.v
    lay_out(z, k.i.got.v, pool, consts)
    k.o.consts.send()
    k.o.state.v[0] = pool[...]
    k.o.state.v[1] = jnp.zeros((z.SR, LANES), F32)
    k.o.state.send()
    k.s.level[...] = levels_of(z, pool[...], consts[0])
    wait(k.i.near, k.i.near_edges, k.i.wet_c, k.i.bed_c)
    sums = contact_step(z, k, k.s.level, lambda side: pack[side, 0])
    for n in range(z.NT):
        k.o.payload.v[n] = sums
    send(k.o.payload, k.o.water_c)
    send_edges(z, k, True)


def step_reservoirs(z, consts, pool, total, lateral):
    area, release, link = consts[0], consts[1], consts[2]
    released = cascade(z, consts, release * (pool + lateral))
    pool = pool + lateral + link * shift_slots(released, z.LD) - released
    return pool, total + released


def sum_members(z, x):
    total = x
    for m in range(1, z.M):
        total = total + pltpu.roll(x, z.SR - m * z.LT, 0)
    return jnp.where(row_ids(x.shape) < z.LT, total, 0.0)


def contact_kernel(z, k, last):
    load(k.i.state, k.i.consts, k.i.own, k.i.pack, k.i.edges, k.i.near_edges, k.i.near, k.i.wet_c, k.i.bed_c)
    wait(k.i.state, k.i.consts)
    got, consts = k.i.got.v, k.i.consts.v
    lateral = got[0]
    for t in range(1, z.NT):
        lateral += got[t]
    pool, total = step_reservoirs(z, consts, k.i.state.v[0], k.i.state.v[1], lateral)
    k.o.state.v[0] = pool
    k.o.state.v[1] = total
    k.o.state.send()
    k.s.level[...] = levels_of(z, pool, consts[0])
    wait(k.i.own, k.i.pack, k.i.edges)
    other, pack = (k.i.from0, k.i.from1), k.i.pack.v
    cross_edges(
        z, k,
        lambda side, n, m: k.i.own.v[side, m],
        lambda n, m: other[n].v[m],
        lambda side, n: [pack[side, i] for i in range(4)],
    )
    wait(k.i.near_edges, k.i.near, k.i.wet_c, k.i.bed_c)
    sums = contact_step(z, k, k.s.level, lambda side: pack[side, 0])
    payload = k.o.payload.v
    if last:
        summed = sum_members(z, total) * (1.0 / z.NT)
        others = consts[1] * (sum_members(z, sums) + sum_members(z, pool) * (1.0 / z.NT))
        others = others + summed - consts[3] * shift_slots(summed, z.LD)
        member = lax.axis_index("ens")
        for e in range(z.E):
            block = jnp.where(member == e, sums, others)
            for t in range(z.NT):
                payload[e * z.NT + t] = block
    else:
        for t in range(z.NT):
            payload[t] = sums
    send(k.o.payload, k.o.water_c)
    send_edges(z, k, not last)


def own_slots(z, x, tile):
    begin = tile * z.LD
    at = begin % LANES
    j = begin // LANES
    out = jnp.zeros((1, LANES), F32)
    turned = pltpu.roll(x, LANES - at, 1)
    lane = lane_ids((1, LANES))
    for n in range(z.LT):
        out = jnp.where((j == n) & (lane < LANES - at), turned[n : n + 1], out)
        out = jnp.where((j + 1 == n) & (lane >= LANES - at), turned[n : n + 1], out)
    return out


def close_kernel(z, k):
    load(k.i.state, k.i.consts)
    wait(k.i.state, k.i.consts)
    tile = lax.axis_index("tiles")
    member = lax.axis_index("ens")
    got, consts = k.i.got.v, k.i.consts.v
    lateral = jnp.zeros((z.SR, LANES), F32)
    others = jnp.zeros((z.SR, LANES), F32)
    for e in range(z.E):
        part = got[e * z.NT]
        for t in range(1, z.NT):
            part += got[e * z.NT + t]
        lateral = jnp.where(member == e, part, lateral)
        others = others + jnp.where(member == e, 0.0, part)
    pool, total = step_reservoirs(z, consts, k.i.state.v[0], k.i.state.v[1], lateral)
    for m in range(z.M):
        at = slice(m * z.LT, (m + 1) * z.LT)
        k.o.storage.v[m : m + 1, :] = own_slots(z, pool[at], tile)[:, : z.LD]
    mean = (sum_members(z, total) + cascade(z, consts, others)) * (1.0 / (z.M * z.E))
    k.o.outflow.v[...] = own_slots(z, mean[: z.LT], tile)[:, : z.LD]
    send(k.o.storage, k.o.outflow)


def shards(
    depth, bed, rain, rough_class, class_n, contact_seg, contact_lake, lake_slot, storage, area, release, upstream_link
):
    z = types.SimpleNamespace()
    z.M, z.R, z.W = depth.shape
    z.NT = lax.axis_size("tiles")
    z.E = lax.axis_size("ens")
    z.LD = storage.shape[1]
    z.LK = z.NT * z.LD
    z.CAP = contact_seg.shape[2]
    z.C = contact_seg.shape[1] * z.CAP
    z.CT = -(-z.C // LANES)
    z.PR = z.W // SEG
    z.classes = class_n.shape[0]
    z.LT = z.LK // LANES + 1
    z.SR = up_to(z.M * z.LT, SUBLANES)
    z.BR = up_to(z.M + 3, SUBLANES)
    levels = len(list(laps(z)))
    blocks = z.W // min(BLOCK, z.W)
    tile_shape = (z.M, z.R, z.W)
    edge_shape = (z.M, z.PR, SEG)
    pack_shape = (z.M + 2, z.PR, SEG)
    near_shape = (z.LT, z.C, LANES)
    state_shape = (2, z.SR, LANES)
    const_shape = (3 + levels, z.SR, LANES)
    contact_shape = (z.M * z.C, SEG)
    wide_tile = pltpu.VMEM((z.M, z.R, z.W + 2 * LANES), F32)
    wide_rows = pltpu.VMEM((z.R, z.W + 2 * LANES), F32)
    plain_tile = pltpu.VMEM(tile_shape, F32)
    partner = [i ^ 1 for i in range(z.NT)], [((i + 1) ^ 1) - 1 for i in range(z.NT)]
    pairs = [[(i, j) for i, j in enumerate(js) if 0 <= j < z.NT] for js in partner]

    def share(x, axes):
        return lax.all_to_all(x, axes, 0, 0, tiled=True)

    def swap(x, y):
        return lax.ppermute(x, "tiles", pairs[0]), lax.ppermute(y, "tiles", pairs[1])

    edges_shape = (2,) + edge_shape
    level_buffer = pltpu.VMEM((z.SR, LANES), F32)
    opened = staged_call(
        pack_kernel, z,
        dict(depth=Raw(depth), bed=Raw(bed), cls=Raw(rough_class), class_n=Scalars(class_n), storage=storage,
             area=area.reshape(1, -1), release=release.reshape(1, -1), link=upstream_link.reshape(1, -1)),
        dict(pack0=pack_shape, pack1=pack_shape, payload=(z.NT, z.BR, LANES)),
        dict(rows=pltpu.VMEM((2, z.M + 1, z.W), F32), cls_rows=pltpu.VMEM((2, 1, z.W), I32), ids=pltpu.VMEM((z.PR, SEG), I32)),
        extra_sems=2 * (z.M + 2),
    )
    got = share(opened.payload, "tiles")
    from0, from1 = swap(opened.pack0, opened.pack1)
    flow = staged_call(
        first_kernel, z,
        dict(depth=Raw(depth), bed=Raw(bed), rain=Raw(rain), cls=Raw(rough_class), class_n=Scalars(class_n),
             seg=Scalars(contact_seg), lake=Scalars(contact_lake), slot=Scalars(lake_slot)),
        dict(wet=Raw(tile_shape), inv=Raw((z.R, z.W)), edges=edges_shape, wet_c=contact_shape, bed_c=(z.C, SEG),
             near=near_shape, near_edges=(2 * z.LT, z.PR, LANES)),
        dict(water=wide_tile, bed=wide_rows, inv=wide_rows, rain=plain_tile, out=plain_tile, cls=pltpu.VMEM((z.R, z.W), I32)),
        extra_sems=6 * blocks,
    )
    inv, bed_c, near, near_edges = flow.inv, flow.bed_c, flow.near, flow.near_edges
    wet, wet_c, edges = flow.wet, flow.wet_c, flow.edges

    step_out = dict(edges=edges_shape, water_c=contact_shape, state=state_shape)
    exchange_out = dict(edge0=Raw(edge_shape), edge1=Raw(edge_shape))
    now = staged_call(
        open_kernel, z,
        dict(got=Here(got), from0=Here(from0), from1=Here(from1), own0=opened.pack0, own1=opened.pack1, edges=edges,
             near=near, near_edges=near_edges, wet_c=wet_c, bed_c=bed_c),
        dict(payload=(z.NT, z.SR, LANES), pack=(2, 4, z.PR, SEG), consts=const_shape, **step_out, **exchange_out),
        dict(pool=level_buffer, level=level_buffer),
        extra_sems=2,
    )
    consts, pack = now.consts, now.pack
    for step in range(1, STEPS):
        got = share(now.payload, "tiles")
        from0, from1 = swap(now.edge0, now.edge1)
        last = step == STEPS - 1
        flow = staged_call(
            flow_kernel, z,
            dict(wet=Raw(wet), seg=Scalars(contact_seg), water_c=now.water_c, edges=now.edges, bed=Raw(bed), inv=Raw(inv),
                 rain=Raw(rain)),
            dict(next=Raw(tile_shape), wet_c=contact_shape, edges=edges_shape),
            dict(water=wide_tile, bed=wide_rows, inv=wide_rows, rain=plain_tile, out=plain_tile),
            extra_sems=1 + 4 * blocks,
        )
        wet, wet_c, edges = flow.next, flow.wet_c, flow.edges
        now = staged_call(
            functools.partial(contact_kernel, last=last), z,
            dict(got=Here(got), from0=Here(from0), from1=Here(from1), own=now.edges, edges=edges, state=now.state,
                 consts=consts, pack=pack, near=near, near_edges=near_edges, wet_c=wet_c, bed_c=bed_c),
            dict(payload=((z.E if last else 1) * z.NT, z.SR, LANES), **step_out, **({} if last else exchange_out)),
            dict(level=level_buffer),
            extra_sems=2,
        )
    got = share(now.payload, ("ens", "tiles"))
    new_depth = staged_call(
        last_kernel, z,
        dict(wet=wet, seg=Scalars(contact_seg), water_c=now.water_c, edges=now.edges),
        dict(depth=Raw(tile_shape)),
        extra_sems=1,
    ).depth
    closed = staged_call(
        close_kernel, z,
        dict(got=Here(got), state=now.state, consts=consts),
        dict(storage=(z.M, z.LD), outflow=(1, z.LD)),
    )
    return new_depth, closed.storage, closed.outflow.reshape(-1)


def solution(mesh):
    return jax.shard_map(
        shards,
        mesh=mesh,
        in_specs=(
            P("ens", "tiles", None),
            P("tiles", None),
            P("ens", "tiles", None),
            P("tiles", None),
            P(),
            P("tiles", None, None),
            P("tiles", None, None),
            P(),
            P("ens", "tiles"),
            P("tiles"),
            P("tiles"),
            P("tiles"),
        ),
        out_specs=(P("ens", "tiles", None), P("ens", "tiles"), P("tiles")),
        check_vma=False,
    )
```

```python
import functools
import types

import jax
import jax.numpy as jnp
from jax import lax
from jax.experimental import pallas as pl
from jax.experimental.pallas import tpu as pltpu
from jax.sharding import PartitionSpec as P

SEG = 256
STEPS = 4
LANES = 128
SUBLANES = 8
FAR = 1e30

flow_rate = 0.035
drain_rate = 0.4

F32 = jnp.float32
I32 = jnp.int32
VMEM_LIMIT = 40 * 2**20
BLOCK = 4096


def up_to(value, unit):
    return -(-value // unit) * unit


def lane_ids(shape):
    return lax.broadcasted_iota(I32, shape, len(shape) - 1)


def row_ids(shape):
    return lax.broadcasted_iota(I32, shape, len(shape) - 2)


def mobility(water, inv_n):
    return water * jnp.exp2(jnp.log2(jnp.abs(water)) * (2.0 / 3.0)) * inv_n


def taken_of(water, surface, level):
    excess = jnp.maximum(surface - level, 0.0)
    return drain_rate * water * excess / (1.0 + excess)


class Array:
    def __init__(self, kernel, h, v):
        self.kernel, self.h, self.v = kernel, h, v

    def load(self):
        self.coming = self.kernel.copy(self.h, self.v)

    def wait(self):
        self.coming.wait()

    def send(self):
        self.kernel.stores.append(self.kernel.copy(self.v, self.h))


class Kernel:
    def __init__(self, sems):
        self.sems, self.count, self.stores = sems, 0, []

    def copy(self, source, target):
        copy = pltpu.make_async_copy(source, target, self.sems.at[self.count])
        self.count += 1
        copy.start()
        return copy

    def pass_on(self):
        for source, target in self.passed:
            self.stores.append(self.copy(source, target))

    def finish(self):
        for copy in self.stores:
            copy.wait()


def load(*arrays):
    for array in arrays:
        array.load()


def wait(*arrays):
    for array in arrays:
        array.wait()


def send(*arrays):
    for array in arrays:
        array.send()


class Staged:
    space = pltpu.VMEM

    def __init__(self, x, free=False):
        self.x, self.free = x, free


class Scalars(Staged):
    space = pltpu.SMEM


class Raw(Staged):
    space = None


class Here(Staged):
    space = None


class Passed(Here):
    pass


def staged_call(body, z, ins, outs, scratch=None, alias=None, extra_sems=0, micros=60):
    scratch = scratch or {}
    ins = {n: x if isinstance(x, Staged) else Staged(x) for n, x in ins.items()}
    outs = {n: x if isinstance(x, Staged) else Staged(x) for n, x in outs.items()}
    passed = [n for n, x in ins.items() if isinstance(x, Passed)]
    outs.update({n: Here(ins[n].x.shape) for n in passed})
    extra_sems += len(passed)
    here_in = [isinstance(x, Here) and not isinstance(x, Passed) for x in ins.values()]
    here_out = [isinstance(x, Here) for x in outs.values()]
    shapes = [x.space(x.x.shape, x.x.dtype) for x in ins.values() if x.space]
    shapes += [x.space(x.x, F32) for x in outs.values() if x.space]
    count = len(shapes) + extra_sems
    shapes += list(scratch.values())
    shapes.append(pltpu.SemaphoreType.DMA((count,)))

    def kernel(*refs):
        refs = list(refs)
        k = Kernel(refs.pop())
        arrays_in, arrays_out = [{n: refs.pop(0) for n in names} for names in (ins, outs)]
        for held, kinds in ((arrays_in, ins), (arrays_out, outs)):
            for n, x in kinds.items():
                held[n] = Array(k, held[n], refs.pop(0) if x.space else held[n])
        k.i = types.SimpleNamespace(**arrays_in)
        k.o = types.SimpleNamespace(**arrays_out)
        k.s = types.SimpleNamespace(**{n: refs.pop(0) for n in scratch})
        k.passed = [(arrays_in[n].h, arrays_out[n].h) for n in passed]
        body(z, k)
        k.finish()

    in_hbm = pl.BlockSpec(memory_space=pltpu.HBM)
    in_vmem = pl.BlockSpec(memory_space=pltpu.VMEM)
    order_in, order_out = list(ins), list(outs)
    results = pl.pallas_call(
        kernel,
        out_shape=[(pltpu.VMEM if here else pltpu.HBM)(x.x, F32) for x, here in zip(outs.values(), here_out)],
        in_specs=[in_vmem if here else in_hbm for here in here_in],
        out_specs=[in_vmem if here else in_hbm for here in here_out],
        scratch_shapes=shapes,
        input_output_aliases={order_in.index(a): order_out.index(b) for a, b in (alias or {}).items()},
        compiler_params=pltpu.CompilerParams(vmem_limit_bytes=VMEM_LIMIT),
        cost_estimate=pl.CostEstimate(
            flops=int(micros * 1e9), transcendentals=int(micros * 1e6), bytes_accessed=int(micros * 3e6)
        ),
    )(*[
        pltpu.with_memory_space_constraint(x.x, pltpu.VMEM if here else pltpu.HBM) if not (here and x.free) else x.x
        for x, here in zip(ins.values(), here_in)
    ])
    return types.SimpleNamespace(**dict(zip(order_out, results)))


def side_of(n):
    tile = lax.axis_index("tiles")
    odd = tile % 2
    side = 1 - odd if n == 0 else odd
    there = jnp.where(side == 0, tile > 0, tile < lax.axis_size("tiles") - 1)
    return side, jnp.where(there, 1.0, 0.0)


def pack_kernel(z, k):
    k.i.class_n.load()
    rows, cls_rows = k.s.rows, k.s.cls_rows
    copies = []
    for side, row in enumerate((0, z.R - 1)):
        for m in range(z.M):
            copies.append(k.copy(k.i.depth.h.at[m, pl.ds(row, 1)], rows.at[side, pl.ds(m, 1)]))
        copies.append(k.copy(k.i.bed.h.at[pl.ds(row, 1)], rows.at[side, pl.ds(z.M, 1)]))
        copies.append(k.copy(k.i.cls.h.at[pl.ds(row, 1)], cls_rows.at[side]))
    k.i.class_n.wait()
    k.o.table.v[...] = inv_table(z, k.i.class_n.v, z.R)
    k.o.table.send()
    wide = inv_table(z, k.i.class_n.v, z.PR)
    for copy in copies:
        copy.wait()
    ids = k.s.ids
    for n, out in enumerate((k.o.pack0, k.o.pack1)):
        side, _ = side_of(n)
        for g in range(z.PR):
            at = slice(g * SEG, (g + 1) * SEG)
            for m in range(z.M + 1):
                out.v[m, g : g + 1, :] = rows[side, m : m + 1, at]
            ids[g : g + 1, :] = cls_rows[side, :, at]
        for half in range(0, SEG, LANES):
            at = slice(half, half + LANES)
            out.v[z.M + 1, :, at] = look_up(wide, ids[:, at])
        out.send()


def inv_table(z, class_n, rows):
    lane = lane_ids((rows, LANES))
    names = jnp.ones((rows, LANES), F32)
    for n in range(z.classes):
        names = jnp.where(lane == n, class_n[n], names)
    return flow_rate * 0.5 / names


def look_up(table, ids):
    return jnp.take_along_axis(table, ids, axis=1, mode="promise_in_bounds")


def widen(z, ref, index=(), left=True, right=True):
    rows = slice(None)
    if left:
        ref[index + (rows, slice(0, LANES))] = pltpu.roll(ref[index + (rows, slice(LANES, 2 * LANES))], LANES - 1, 1)
    if right:
        ref[index + (rows, slice(z.W + LANES, z.W + 2 * LANES))] = pltpu.roll(
            ref[index + (rows, slice(z.W, z.W + LANES))], 1, 1
        )


def flow_blocks(z, water, bed, inv, rain, out, edges, done, ready=None):
    size = min(BLOCK, z.W)
    segs = size // SEG
    row = row_ids((z.R, size))
    bottom = row == z.R - 1
    top = row == 0

    def block(j, _):
        base = j * size if ready else pl.multiple_of(j * size, size)
        wide = pl.ds(base, size + 2 * LANES)
        at = pl.ds(base, size)
        b, v = bed[:, wide], inv[:, wide]
        for m in range(z.M):
            w = water[m, :, wide]
            s = b + w
            q = mobility(w, v)
            s_right = pltpu.roll(s, size + 2 * LANES - 1, 1)
            q_right = pltpu.roll(q, size + 2 * LANES - 1, 1)
            f = ((q + q_right) * (s - s_right))[:, : size + LANES]
            net = pltpu.roll(f, 1, 1)[:, LANES:] - f[:, LANES:]
            s = s[:, LANES : size + LANES]
            q = q[:, LANES : size + LANES]
            flow = (q + pltpu.roll(q, z.R - 1, 0)) * (s - pltpu.roll(s, z.R - 1, 0))
            flow = jnp.where(bottom, 0.0, flow)
            above = jnp.where(top, 0.0, pltpu.roll(flow, 1, 0))
            wet = w[:, LANES : size + LANES] + (net + (above - flow)) + rain[m, :, at]
            out[m, :, at] = wet
            for i in range(segs):
                part = slice(i * SEG, (i + 1) * SEG)
                edges[0, m, pl.ds(j * segs + i, 1), :] = wet[:1, part]
                edges[1, m, pl.ds(j * segs + i, 1), :] = wet[z.R - 1 :, part]
        done(j, at)
        return 0

    if ready:
        for j in range(z.W // size):
            ready(j)
            block(j, 0)
    else:
        lax.fori_loop(0, z.W // size, block, 0)


def send_blocks(z, k, source, target):
    size = min(BLOCK, z.W)
    first = k.count
    k.count += z.W // size

    def copy(j):
        at = pl.ds(pl.multiple_of(j * size, size), size)
        return pltpu.make_async_copy(source.at[:, :, at], target.at[:, :, at], k.sems.at[first + j])

    for j in range(z.W // size):
        k.stores.append(copy(j))
    return lambda j, at: copy(j).start()


def contact_places(z, seg):
    for c in range(z.C):
        owner, place = divmod(c, z.CAP)
        s = seg[0, owner, place]
        yield c, s // z.PR, pl.multiple_of((s % z.PR) * SEG, SEG)


def gather_contacts(z, seg, water, out):
    for c, r, at in contact_places(z, seg):
        for m in range(z.M):
            out[m * z.C + c : m * z.C + c + 1, :] = water[m, pl.ds(r, 1), pl.ds(at, SEG)]


def scatter_contacts(z, seg, values, water, shift):
    for c, r, at in contact_places(z, seg):
        for m in range(z.M):
            water[m, pl.ds(r, 1), pl.ds(at + shift, SEG)] = values[m * z.C + c : m * z.C + c + 1, :]


def set_edges(z, edges, water, shift):
    for side, row in enumerate((0, z.R - 1)):
        for m in range(z.M):
            for g in range(z.PR):
                at = slice(g * SEG + shift, (g + 1) * SEG + shift)
                water[m, row : row + 1, at] = edges[side, m, g : g + 1, :]


def prepare_kernel(z, k):
    size = min(BLOCK, z.W)
    parts = z.W // size
    small = k.i.seg, k.i.lake, k.i.slot, k.i.storage, k.i.area, k.i.release, k.i.link, k.i.table
    load(*small)
    cls, inv = k.s.cls, k.s.inv
    columns = [pl.ds(p * size, size) for p in range(parts)]
    coming = [k.copy(k.i.cls.h.at[:, at], cls.at[:, at]) for at in columns]
    wait(*small)
    payload = k.o.payload.v
    payload[0] = jnp.zeros((z.BR, LANES), F32)
    payload[0, : z.M, : z.LD] = k.i.storage.v[...]
    for n, x in enumerate((k.i.area, k.i.release, k.i.link)):
        payload[0, z.M + n : z.M + n + 1, : z.LD] = x.v[...].astype(F32)
    for n in range(1, z.NT):
        payload[n] = payload[0]
    k.o.payload.send()
    table = k.i.table.v[...]
    for p in range(parts):
        coming[p].wait()

        def look(i, _):
            at = pl.ds(pl.multiple_of(p * size + i * LANES, LANES), LANES)
            inv[:, at] = look_up(table, cls[:, at])
            return 0

        lax.fori_loop(0, size // LANES, look, 0, unroll=16)
        k.stores.append(k.copy(inv.at[:, columns[p]], k.o.inv.h.at[:, columns[p]]))
    one_hots(z, k)
    send(k.o.near, k.o.near_edges)


def one_hots(z, k):
    lane = lane_ids((1, LANES))
    contact = row_ids((z.C, LANES))
    place_g = row_ids((z.PR, LANES))
    inside = jnp.full((z.C, 1), z.LK, F32)
    on_edge = [jnp.full((z.PR, 1), z.LK, F32) for _ in range(2)]
    firsts = (0, (z.R - 1) * z.PR)
    for tile in range(z.CT):
        segs = jnp.full((1, LANES), -1, I32)
        slots = jnp.full((1, LANES), z.LK, I32)
        for c in range(tile * LANES, min(z.C, (tile + 1) * LANES)):
            owner, place = divmod(c, z.CAP)
            lake_id = k.i.lake.v[0, owner, place]
            found = jnp.where(lake_id >= 0, k.i.slot.v[jnp.maximum(lake_id, 0)], z.LK)
            segs = jnp.where(lane == c - tile * LANES, k.i.seg.v[0, owner, place], segs)
            slots = jnp.where(lane == c - tile * LANES, found, slots)
        more = (slots - z.LK).astype(F32)
        central = (segs >= z.PR) & (segs < firsts[1])
        mine = lane_ids((z.C, LANES)) + tile * LANES == contact
        inside += jnp.sum(jnp.where(mine & central, more, 0.0), axis=1, keepdims=True)
        for side in range(2):
            here = place_g + firsts[side] == segs
            on_edge[side] += jnp.sum(jnp.where(here, more, 0.0), axis=1, keepdims=True)
    for j in range(z.LT):
        k.o.near.v[j] = jnp.where(inside == (lane_ids((z.C, LANES)) + j * LANES).astype(F32), 1.0, 0.0)
        for side in range(2):
            ids = (lane_ids((z.PR, LANES)) + j * LANES).astype(F32)
            k.o.near_edges.v[side * z.LT + j] = jnp.where(on_edge[side] == ids, 1.0, 0.0)


def flow_kernel(z, k, first):
    size = min(BLOCK, z.W)
    parts = z.W // size
    inv, bed, water, rain = k.s.inv, k.s.bed, k.s.water, k.s.rain
    k.i.seg.load()
    columns = [(pl.ds(p * size, size), pl.ds(p * size + LANES, size)) for p in range(parts)]
    if not first:
        k.i.water_c.load()
        whole = k.copy(k.i.wet.h, water.at[:, :, pl.ds(LANES, z.W)])
        k.i.edges.load()
    coming = []
    for at, inner in columns:
        coming.append([
            k.copy(k.i.bed.h.at[:, at], bed.at[:, inner]),
            k.copy(k.i.inv.h.at[:, at], inv.at[:, inner]),
            k.copy(k.i.rain.h.at[:, :, at], rain.at[:, :, at]),
        ])
        if first:
            coming[-1].append(k.copy(k.i.wet.h.at[:, :, at], water.at[:, :, inner]))
    k.pass_on()
    k.i.seg.wait()
    if not first:
        k.i.water_c.wait()
        whole.wait()
        scatter_contacts(z, k.i.seg.v, k.i.water_c.v, water, LANES)
        k.i.edges.wait()
        set_edges(z, k.i.edges.v, water, LANES)

    def prepare(p):
        for copy in coming[p]:
            copy.wait()
        sides = dict(left=p == 0, right=p == parts - 1)
        widen(z, inv, **sides)
        widen(z, bed, **sides)
        for m in range(z.M):
            widen(z, water, (m,), **sides)

    def ready(j):
        if j == 0:
            prepare(0)
        if j + 1 < parts:
            prepare(j + 1)

    done = send_blocks(z, k, k.s.out, k.o.next.h)
    flow_blocks(z, water, bed, inv, rain, k.s.out, k.o.edges.v, done, ready)
    gather_contacts(z, k.i.seg.v, k.s.out, k.o.wet_c.v)
    if first:
        for c, r, at in contact_places(z, k.i.seg.v):
            k.o.bed_c.v[c : c + 1, :] = bed[pl.ds(r, 1), pl.ds(at + LANES, SEG)]
            k.s.bed_c[c : c + 1, :] = bed[pl.ds(r, 1), pl.ds(at + LANES, SEG)]
        k.stores.append(k.copy(k.s.bed_c, k.o.bed_kept.h))


def last_kernel(z, k):
    load(k.i.wet, k.i.seg, k.i.water_c, k.i.edges)
    k.pass_on()
    wait(k.i.wet, k.i.seg, k.i.water_c, k.i.edges)
    scatter_contacts(z, k.i.seg.v, k.i.water_c.v, k.i.wet.v, 0)
    set_edges(z, k.i.edges.v, k.i.wet.v, 0)
    k.stores.append(k.copy(k.i.wet.v, k.o.depth.h))


def pick(z, near, table, m):
    total = near[0] * table[m * z.LT : m * z.LT + 1, :]
    for j in range(1, z.LT):
        total += near[j] * table[m * z.LT + j : m * z.LT + j + 1, :]
    return jnp.sum(total, axis=1, keepdims=True)


def shift_slots(x, count):
    rows, lanes = divmod(count, LANES)
    size = x.shape[0]
    turned = pltpu.roll(x, lanes, 1) if lanes else x
    low = pltpu.roll(turned, rows % size, 0) if rows % size else turned
    if not lanes:
        return low
    high = pltpu.roll(turned, (rows + 1) % size, 0)
    return jnp.where(lane_ids(x.shape) < lanes, high, low)


def laps(z):
    count = z.LD
    while count < z.LK:
        yield count
        count *= 2


def cascade(z, consts, entering):
    for lap, count in enumerate(laps(z)):
        entering = entering + consts[3 + lap] * shift_slots(entering, count)
    return entering


def slot_ids(z):
    shape = (z.SR, LANES)
    return (row_ids(shape) % z.LT) * LANES + lane_ids(shape)


def levels_of(z, pool, area):
    return jnp.where(slot_ids(z) == z.LK, FAR, pool / area)


def lay_out(z, got, pool, consts):
    pool[...] = jnp.zeros_like(pool)
    consts[...] = jnp.zeros_like(consts)
    consts[0] = jnp.ones((z.SR, LANES), F32)
    for t in range(z.NT):
        done = 0
        while done < z.LD:
            j, at = divmod(t * z.LD + done, LANES)
            n = min(z.LD - done, LANES - at)
            for m in range(z.M):
                r = m * z.LT + j
                pool[r : r + 1, at : at + n] = got[t, m : m + 1, done : done + n]
                for i in range(3):
                    consts[i, r : r + 1, at : at + n] = got[t, z.M + i : z.M + i + 1, done : done + n]
            done += n
    consts[2] = jnp.where(slot_ids(z) >= z.LD, consts[2], 0.0)
    factor = consts[1] * consts[2]
    for lap, count in enumerate(laps(z)):
        consts[3 + lap] = factor
        factor = factor * shift_slots(factor, count)


def cross_edges(z, k, own, other, rows):
    for n in range(2):
        side, flag = side_of(n)
        own_bed, own_inv, other_bed, other_inv = rows(side, n)
        for m in range(z.M):
            a, b = own(side, n, m), other(n, m)
            flow = (mobility(a, own_inv) + mobility(b, other_inv)) * ((other_bed + b) - (own_bed + a))
            k.i.edges.v[side, m] += flow * flag


def contact_step(z, k, level, bed_rows):
    rows = [[jnp.zeros((SUBLANES, LANES), F32) for _ in range(z.LT)] for _ in range(z.M)]

    def take(near, m, w, bed):
        taken = taken_of(w, bed + w, pick(z, near, level, m))
        sums = jnp.sum(taken, axis=1, keepdims=True) * (1.0 / SEG)
        for j in range(z.LT):
            part = near[j] * sums
            for r in range(0, part.shape[0], SUBLANES):
                rows[m][j] += part[r : r + SUBLANES]
        return w - taken

    for side in range(2):
        near = k.i.near_edges.v.at[pl.ds(side * z.LT, z.LT)]
        for m in range(z.M):
            k.o.edges.v[side, m] = take(near, m, k.i.edges.v[side, m], bed_rows(side))
    bed = k.i.bed_c.v[...]
    for m in range(z.M):
        at = slice(m * z.C, (m + 1) * z.C)
        k.o.water_c.v[at, :] = take(k.i.near.v, m, k.i.wet_c.v[at, :], bed)
    found = [jnp.sum(rows[m][j], axis=0, keepdims=True) for m in range(z.M) for j in range(z.LT)]
    if z.SR > len(found):
        found.append(jnp.zeros((z.SR - len(found), LANES), F32))
    return jnp.concatenate(found, axis=0)


def send_edges(z, k, exchange):
    k.o.edges.send()
    if exchange:
        for n, out in enumerate((k.o.edge0, k.o.edge1)):
            side, _ = side_of(n)
            k.stores.append(k.copy(k.o.edges.v.at[side], out.h))


def open_kernel(z, k):
    own, other, pack = (k.i.own0, k.i.own1), (k.i.from0, k.i.from1), k.o.pack.v
    for n in range(2):
        side, _ = side_of(n)
        pack[side, :2] = own[n].v[z.M : z.M + 2]
        pack[side, 2:] = other[n].v[z.M : z.M + 2]
    k.o.pack.send()
    cross_edges(
        z, k,
        lambda side, n, m: own[n].v[m],
        lambda n, m: other[n].v[m],
        lambda side, n: [pack[side, i] for i in range(4)],
    )
    pool, consts = k.s.pool, k.o.consts.v
    lay_out(z, k.i.got.v, pool, consts)
    k.o.consts.send()
    k.o.state.v[0] = pool[...]
    k.o.state.v[1] = jnp.zeros((z.SR, LANES), F32)
    k.o.state.send()
    k.s.level[...] = levels_of(z, pool[...], consts[0])
    sums = contact_step(z, k, k.s.level, lambda side: pack[side, 0])
    for n in range(z.NT):
        k.o.payload.v[n] = sums
    send(k.o.payload, k.o.water_c)
    send_edges(z, k, True)


def step_reservoirs(z, consts, pool, total, lateral):
    area, release, link = consts[0], consts[1], consts[2]
    released = cascade(z, consts, release * (pool + lateral))
    pool = pool + lateral + link * shift_slots(released, z.LD) - released
    return pool, total + released


def sum_members(z, x):
    total = x
    for m in range(1, z.M):
        total = total + pltpu.roll(x, z.SR - m * z.LT, 0)
    return jnp.where(row_ids(x.shape) < z.LT, total, 0.0)


def contact_kernel(z, k, last):
    got, consts = k.i.got.v, k.i.consts.v
    lateral = got[0]
    for t in range(1, z.NT):
        lateral += got[t]
    pool, total = step_reservoirs(z, consts, k.i.state.v[0], k.i.state.v[1], lateral)
    k.o.state.v[0] = pool
    k.o.state.v[1] = total
    k.o.state.send()
    k.s.level[...] = levels_of(z, pool, consts[0])
    other, pack = (k.i.from0, k.i.from1), k.i.pack.v
    cross_edges(
        z, k,
        lambda side, n, m: k.i.own.v[side, m],
        lambda n, m: other[n].v[m],
        lambda side, n: [pack[side, i] for i in range(4)],
    )
    sums = contact_step(z, k, k.s.level, lambda side: pack[side, 0])
    payload = k.o.payload.v
    if last:
        summed = sum_members(z, total) * (1.0 / z.NT)
        others = consts[1] * (sum_members(z, sums) + sum_members(z, pool) * (1.0 / z.NT))
        others = others + summed - consts[3] * shift_slots(summed, z.LD)
        member = lax.axis_index("ens")
        for e in range(z.E):
            block = jnp.where(member == e, sums, others)
            for t in range(z.NT):
                payload[e * z.NT + t] = block
    else:
        for t in range(z.NT):
            payload[t] = sums
    send(k.o.payload, k.o.water_c)
    send_edges(z, k, not last)


def own_slots(z, x, tile):
    begin = tile * z.LD
    at = begin % LANES
    j = begin // LANES
    out = jnp.zeros((1, LANES), F32)
    turned = pltpu.roll(x, LANES - at, 1)
    lane = lane_ids((1, LANES))
    for n in range(z.LT):
        out = jnp.where((j == n) & (lane < LANES - at), turned[n : n + 1], out)
        out = jnp.where((j + 1 == n) & (lane >= LANES - at), turned[n : n + 1], out)
    return out


def close_kernel(z, k):
    tile = lax.axis_index("tiles")
    member = lax.axis_index("ens")
    got, consts = k.i.got.v, k.i.consts.v
    lateral = jnp.zeros((z.SR, LANES), F32)
    others = jnp.zeros((z.SR, LANES), F32)
    for e in range(z.E):
        part = got[e * z.NT]
        for t in range(1, z.NT):
            part += got[e * z.NT + t]
        lateral = jnp.where(member == e, part, lateral)
        others = others + jnp.where(member == e, 0.0, part)
    pool, total = step_reservoirs(z, consts, k.i.state.v[0], k.i.state.v[1], lateral)
    for m in range(z.M):
        at = slice(m * z.LT, (m + 1) * z.LT)
        k.o.storage.v[m : m + 1, :] = own_slots(z, pool[at], tile)[:, : z.LD]
    mean = (sum_members(z, total) + cascade(z, consts, others)) * (1.0 / (z.M * z.E))
    k.o.outflow.v[...] = own_slots(z, mean[: z.LT], tile)[:, : z.LD]
    send(k.o.storage, k.o.outflow)


def shards(
    depth, bed, rain, rough_class, class_n, contact_seg, contact_lake, lake_slot, storage, area, release, upstream_link
):
    z = types.SimpleNamespace()
    z.M, z.R, z.W = depth.shape
    z.NT = lax.axis_size("tiles")
    z.E = lax.axis_size("ens")
    z.LD = storage.shape[1]
    z.LK = z.NT * z.LD
    z.CAP = contact_seg.shape[2]
    z.C = contact_seg.shape[1] * z.CAP
    z.CT = -(-z.C // LANES)
    z.PR = z.W // SEG
    z.classes = class_n.shape[0]
    z.LT = z.LK // LANES + 1
    z.SR = up_to(z.M * z.LT, SUBLANES)
    z.BR = up_to(z.M + 3, SUBLANES)
    levels = len(list(laps(z)))
    blocks = z.W // min(BLOCK, z.W)
    tile_shape = (z.M, z.R, z.W)
    edge_shape = (z.M, z.PR, SEG)
    pack_shape = (z.M + 2, z.PR, SEG)
    near_shape = (z.LT, z.C, LANES)
    state_shape = (2, z.SR, LANES)
    const_shape = (3 + levels, z.SR, LANES)
    contact_shape = (z.M * z.C, SEG)
    wide_tile = pltpu.VMEM((z.M, z.R, z.W + 2 * LANES), F32)
    wide_rows = pltpu.VMEM((z.R, z.W + 2 * LANES), F32)
    plain_tile = pltpu.VMEM(tile_shape, F32)
    partner = [i ^ 1 for i in range(z.NT)], [((i + 1) ^ 1) - 1 for i in range(z.NT)]
    pairs = [[(i, j) for i, j in enumerate(js) if 0 <= j < z.NT] for js in partner]

    def share(x, axes):
        return lax.all_to_all(x, axes, 0, 0, tiled=True)

    def swap(x, y):
        return lax.ppermute(x, "tiles", pairs[0]), lax.ppermute(y, "tiles", pairs[1])

    edges_shape = (2,) + edge_shape
    level_buffer = pltpu.VMEM((z.SR, LANES), F32)
    opened = staged_call(
        pack_kernel, z,
        dict(depth=Raw(depth), bed=Raw(bed), cls=Raw(rough_class), class_n=Scalars(class_n)),
        dict(pack0=pack_shape, pack1=pack_shape, table=(z.R, LANES)),
        dict(rows=pltpu.VMEM((2, z.M + 1, z.W), F32), cls_rows=pltpu.VMEM((2, 1, z.W), I32), ids=pltpu.VMEM((z.PR, SEG), I32)),
        extra_sems=2 * (z.M + 2),
    )
    from0, from1 = swap(opened.pack0, opened.pack1)
    kept = staged_call(
        prepare_kernel, z,
        dict(cls=Raw(rough_class), table=opened.table, seg=Scalars(contact_seg), lake=Scalars(contact_lake),
             slot=Scalars(lake_slot), storage=storage, area=area.reshape(1, -1), release=release.reshape(1, -1),
             link=upstream_link.reshape(1, -1)),
        dict(payload=(z.NT, z.BR, LANES), inv=Raw((z.R, z.W)), near=near_shape, near_edges=(2 * z.LT, z.PR, LANES)),
        dict(cls=pltpu.VMEM((z.R, z.W), I32), inv=pltpu.VMEM((z.R, z.W), F32)),
        extra_sems=2 * blocks,
    )
    got = share(kept.payload, "tiles")
    inv, near, near_edges = kept.inv, kept.near, kept.near_edges
    flow_scratch = dict(water=wide_tile, bed=wide_rows, inv=wide_rows, rain=plain_tile, out=plain_tile)
    flow_out = dict(next=Raw(tile_shape), wet_c=Here(contact_shape), edges=Here(edges_shape))
    flow = staged_call(
        functools.partial(flow_kernel, first=True), z,
        dict(wet=Raw(depth), seg=Scalars(contact_seg), bed=Raw(bed), inv=Raw(inv), rain=Raw(rain), near=Passed(near),
             near_edges=Passed(near_edges), own0=Passed(opened.pack0), own1=Passed(opened.pack1)),
        dict(bed_c=Here((z.C, SEG)), bed_kept=Raw((z.C, SEG)), **flow_out),
        dict(bed_c=pltpu.VMEM((z.C, SEG), F32), **flow_scratch),
        extra_sems=5 * blocks + 1,
    )
    bed_kept = flow.bed_kept

    step_out = dict(edges=edges_shape, water_c=contact_shape, state=state_shape)
    exchange_out = dict(edge0=Raw(edge_shape), edge1=Raw(edge_shape))
    now = staged_call(
        open_kernel, z,
        dict(got=Here(got, free=True), from0=Here(from0, free=True), from1=Here(from1, free=True), own0=Here(flow.own0),
             own1=Here(flow.own1), edges=Here(flow.edges), near=Here(flow.near), near_edges=Here(flow.near_edges),
             wet_c=Here(flow.wet_c), bed_c=Here(flow.bed_c)),
        dict(payload=(z.NT, z.SR, LANES), pack=(2, 4, z.PR, SEG), consts=const_shape, **step_out, **exchange_out),
        dict(pool=level_buffer, level=level_buffer),
        extra_sems=2,
    )
    consts, pack = now.consts, now.pack
    for step in range(1, STEPS):
        got = share(now.payload, "tiles")
        from0, from1 = swap(now.edge0, now.edge1)
        last = step == STEPS - 1
        flow = staged_call(
            functools.partial(flow_kernel, first=False), z,
            dict(wet=Raw(flow.next), seg=Scalars(contact_seg), water_c=now.water_c, edges=now.edges, bed=Raw(bed),
                 inv=Raw(inv), rain=Raw(rain), state=Passed(now.state), consts=Passed(consts), near=Passed(near),
                 near_edges=Passed(near_edges), pack=Passed(pack), own=Passed(now.edges), bed_c=Passed(bed_kept)),
            flow_out,
            flow_scratch,
            extra_sems=1 + 4 * blocks,
        )
        now = staged_call(
            functools.partial(contact_kernel, last=last), z,
            dict(got=Here(got, free=True), from0=Here(from0, free=True), from1=Here(from1, free=True), own=Here(flow.own),
                 edges=Here(flow.edges), state=Here(flow.state), consts=Here(flow.consts), pack=Here(flow.pack),
                 near=Here(flow.near), near_edges=Here(flow.near_edges), wet_c=Here(flow.wet_c), bed_c=Here(flow.bed_c)),
            dict(payload=((z.E if last else 1) * z.NT, z.SR, LANES), **step_out, **({} if last else exchange_out)),
            dict(level=level_buffer),
            extra_sems=2,
        )
    got = share(now.payload, ("ens", "tiles"))
    done = staged_call(
        last_kernel, z,
        dict(wet=flow.next, seg=Scalars(contact_seg), water_c=now.water_c, edges=now.edges, state=Passed(now.state),
             consts=Passed(consts)),
        dict(depth=Raw(tile_shape)),
        extra_sems=1,
    )
    closed = staged_call(
        close_kernel, z,
        dict(got=Here(got, free=True), state=Here(done.state), consts=Here(done.consts)),
        dict(storage=(z.M, z.LD), outflow=(1, z.LD)),
    )
    return done.depth, closed.storage, closed.outflow.reshape(-1)


def solution(mesh):
    return jax.shard_map(
        shards,
        mesh=mesh,
        in_specs=(
            P("ens", "tiles", None),
            P("tiles", None),
            P("ens", "tiles", None),
            P("tiles", None),
            P(),
            P("tiles", None, None),
            P("tiles", None, None),
            P(),
            P("ens", "tiles"),
            P("tiles"),
            P("tiles"),
            P("tiles"),
        ),
        out_specs=(P("ens", "tiles", None), P("ens", "tiles"), P("tiles")),
        check_vma=False,
    )
```

```python
import functools
import types

import jax
import jax.numpy as jnp
from jax import lax
from jax.experimental import pallas as pl
from jax.experimental.pallas import tpu as pltpu
from jax.sharding import PartitionSpec as P

SEG = 256
STEPS = 4
LANES = 128
SUBLANES = 8
FAR = 1e30

flow_rate = 0.035
drain_rate = 0.4

F32 = jnp.float32
I32 = jnp.int32
VMEM_LIMIT = 40 * 2**20
BLOCK = 4096


def up_to(value, unit):
    return -(-value // unit) * unit


def lane_ids(shape):
    return lax.broadcasted_iota(I32, shape, len(shape) - 1)


def row_ids(shape):
    return lax.broadcasted_iota(I32, shape, len(shape) - 2)


def mobility(water, inv_n):
    return water * jnp.exp2(jnp.log2(jnp.abs(water)) * (2.0 / 3.0)) * inv_n


def taken_of(water, surface, level):
    excess = jnp.maximum(surface - level, 0.0)
    return drain_rate * water * excess / (1.0 + excess)


class Array:
    def __init__(self, kernel, h, v):
        self.kernel, self.h, self.v = kernel, h, v

    def load(self):
        self.coming = self.kernel.copy(self.h, self.v)

    def wait(self):
        self.coming.wait()

    def send(self):
        self.kernel.stores.append(self.kernel.copy(self.v, self.h))


class Kernel:
    def __init__(self, sems):
        self.sems, self.count, self.stores = sems, 0, []

    def copy(self, source, target):
        copy = pltpu.make_async_copy(source, target, self.sems.at[self.count])
        self.count += 1
        copy.start()
        return copy

    def pass_on(self):
        for source, target in self.passed:
            self.stores.append(self.copy(source, target))

    def finish(self):
        for copy in self.stores:
            copy.wait()


def load(*arrays):
    for array in arrays:
        array.load()


def wait(*arrays):
    for array in arrays:
        array.wait()


def send(*arrays):
    for array in arrays:
        array.send()


class Staged:
    space = pltpu.VMEM

    def __init__(self, x, free=False):
        self.x, self.free = x, free


class Scalars(Staged):
    space = pltpu.SMEM


class Raw(Staged):
    space = None


class Here(Staged):
    space = None


class Passed(Here):
    pass


def staged_call(body, z, ins, outs, scratch=None, alias=None, extra_sems=0, micros=60):
    scratch = scratch or {}
    ins = {n: x if isinstance(x, Staged) else Staged(x) for n, x in ins.items()}
    outs = {n: x if isinstance(x, Staged) else Staged(x) for n, x in outs.items()}
    passed = [n for n, x in ins.items() if isinstance(x, Passed)]
    outs.update({n: Here(ins[n].x.shape) for n in passed})
    extra_sems += len(passed)
    here_in = [isinstance(x, Here) and not isinstance(x, Passed) for x in ins.values()]
    here_out = [isinstance(x, Here) for x in outs.values()]
    shapes = [x.space(x.x.shape, x.x.dtype) for x in ins.values() if x.space]
    shapes += [x.space(x.x, F32) for x in outs.values() if x.space]
    count = len(shapes) + extra_sems
    shapes += list(scratch.values())
    shapes.append(pltpu.SemaphoreType.DMA((count,)))

    def kernel(*refs):
        refs = list(refs)
        k = Kernel(refs.pop())
        arrays_in, arrays_out = [{n: refs.pop(0) for n in names} for names in (ins, outs)]
        for held, kinds in ((arrays_in, ins), (arrays_out, outs)):
            for n, x in kinds.items():
                held[n] = Array(k, held[n], refs.pop(0) if x.space else held[n])
        k.i = types.SimpleNamespace(**arrays_in)
        k.o = types.SimpleNamespace(**arrays_out)
        k.s = types.SimpleNamespace(**{n: refs.pop(0) for n in scratch})
        k.passed = [(arrays_in[n].h, arrays_out[n].h) for n in passed]
        body(z, k)
        k.finish()

    in_hbm = pl.BlockSpec(memory_space=pltpu.HBM)
    in_vmem = pl.BlockSpec(memory_space=pltpu.VMEM)
    order_in, order_out = list(ins), list(outs)
    results = pl.pallas_call(
        kernel,
        out_shape=[(pltpu.VMEM if here else pltpu.HBM)(x.x, F32) for x, here in zip(outs.values(), here_out)],
        in_specs=[in_vmem if here else in_hbm for here in here_in],
        out_specs=[in_vmem if here else in_hbm for here in here_out],
        scratch_shapes=shapes,
        input_output_aliases={order_in.index(a): order_out.index(b) for a, b in (alias or {}).items()},
        compiler_params=pltpu.CompilerParams(vmem_limit_bytes=VMEM_LIMIT),
        cost_estimate=pl.CostEstimate(
            flops=int(micros * 1e9), transcendentals=int(micros * 1e6), bytes_accessed=int(micros * 3e6)
        ),
    )(*[
        pltpu.with_memory_space_constraint(x.x, pltpu.VMEM if here else pltpu.HBM) if not (here and x.free) else x.x
        for x, here in zip(ins.values(), here_in)
    ])
    return types.SimpleNamespace(**dict(zip(order_out, results)))


def side_of(n):
    tile = lax.axis_index("tiles")
    there = tile > 0 if n == 0 else tile < lax.axis_size("tiles") - 1
    return n, jnp.where(there, 1.0, 0.0)


def pack_kernel(z, k):
    k.i.class_n.load()
    rows, cls_rows = k.s.rows, k.s.cls_rows
    copies = []
    for side, row in enumerate((0, z.R - 1)):
        for m in range(z.M):
            copies.append(k.copy(k.i.depth.h.at[m, pl.ds(row, 1)], rows.at[side, pl.ds(m, 1)]))
        copies.append(k.copy(k.i.bed.h.at[pl.ds(row, 1)], rows.at[side, pl.ds(z.M, 1)]))
        copies.append(k.copy(k.i.cls.h.at[pl.ds(row, 1)], cls_rows.at[side]))
    k.i.class_n.wait()
    k.o.table.v[...] = inv_table(z, k.i.class_n.v, z.R)
    k.o.table.send()
    wide = inv_table(z, k.i.class_n.v, z.PR)
    for copy in copies:
        copy.wait()
    ids = k.s.ids
    for n, out in enumerate((k.o.pack0, k.o.pack1)):
        side, _ = side_of(n)
        for g in range(z.PR):
            at = slice(g * SEG, (g + 1) * SEG)
            for m in range(z.M + 1):
                out.v[m, g : g + 1, :] = rows[side, m : m + 1, at]
            ids[g : g + 1, :] = cls_rows[side, :, at]
        for half in range(0, SEG, LANES):
            at = slice(half, half + LANES)
            out.v[z.M + 1, :, at] = look_up(wide, ids[:, at])
        out.send()


def inv_table(z, class_n, rows):
    lane = lane_ids((rows, LANES))
    names = jnp.ones((rows, LANES), F32)
    for n in range(z.classes):
        names = jnp.where(lane == n, class_n[n], names)
    return flow_rate * 0.5 / names


def look_up(table, ids):
    return jnp.take_along_axis(table, ids, axis=1, mode="promise_in_bounds")


def widen(z, ref, index=(), left=True, right=True):
    rows = slice(None)
    if left:
        ref[index + (rows, slice(0, LANES))] = pltpu.roll(ref[index + (rows, slice(LANES, 2 * LANES))], LANES - 1, 1)
    if right:
        ref[index + (rows, slice(z.W + LANES, z.W + 2 * LANES))] = pltpu.roll(
            ref[index + (rows, slice(z.W, z.W + LANES))], 1, 1
        )


def flow_blocks(z, water, bed, inv, rain, out, edges, done, ready=None):
    size = min(BLOCK, z.W)
    segs = size // SEG
    row = row_ids((z.R, size))
    bottom = row == z.R - 1
    top = row == 0

    def block(j, _):
        base = j * size if ready else pl.multiple_of(j * size, size)
        wide = pl.ds(base, size + 2 * LANES)
        at = pl.ds(base, size)
        b, v = bed[:, wide], inv[:, wide]
        for m in range(z.M):
            w = water[m, :, wide]
            s = b + w
            q = mobility(w, v)
            s_right = pltpu.roll(s, size + 2 * LANES - 1, 1)
            q_right = pltpu.roll(q, size + 2 * LANES - 1, 1)
            f = ((q + q_right) * (s - s_right))[:, : size + LANES]
            net = pltpu.roll(f, 1, 1)[:, LANES:] - f[:, LANES:]
            s = s[:, LANES : size + LANES]
            q = q[:, LANES : size + LANES]
            flow = (q + pltpu.roll(q, z.R - 1, 0)) * (s - pltpu.roll(s, z.R - 1, 0))
            flow = jnp.where(bottom, 0.0, flow)
            above = jnp.where(top, 0.0, pltpu.roll(flow, 1, 0))
            wet = w[:, LANES : size + LANES] + (net + (above - flow)) + rain[m, :, at]
            out[m, :, at] = wet
            for i in range(segs):
                part = slice(i * SEG, (i + 1) * SEG)
                edges[0, m, pl.ds(j * segs + i, 1), :] = wet[:1, part]
                edges[1, m, pl.ds(j * segs + i, 1), :] = wet[z.R - 1 :, part]
        done(j, at)
        return 0

    if ready:
        for j in range(z.W // size):
            ready(j)
            block(j, 0)
    else:
        lax.fori_loop(0, z.W // size, block, 0)


def send_blocks(z, k, source, target):
    size = min(BLOCK, z.W)
    first = k.count
    k.count += z.W // size

    def copy(j):
        at = pl.ds(pl.multiple_of(j * size, size), size)
        return pltpu.make_async_copy(source.at[:, :, at], target.at[:, :, at], k.sems.at[first + j])

    for j in range(z.W // size):
        k.stores.append(copy(j))
    return lambda j, at: copy(j).start()


def contact_places(z, seg):
    for c in range(z.C):
        owner, place = divmod(c, z.CAP)
        s = seg[0, owner, place]
        yield c, s // z.PR, pl.multiple_of((s % z.PR) * SEG, SEG)


def gather_contacts(z, seg, water, out):
    for c, r, at in contact_places(z, seg):
        for m in range(z.M):
            out[m * z.C + c : m * z.C + c + 1, :] = water[m, pl.ds(r, 1), pl.ds(at, SEG)]


def scatter_contacts(z, seg, values, water, shift):
    for c, r, at in contact_places(z, seg):
        for m in range(z.M):
            water[m, pl.ds(r, 1), pl.ds(at + shift, SEG)] = values[m * z.C + c : m * z.C + c + 1, :]


def set_edges(z, edges, water, shift):
    for side, row in enumerate((0, z.R - 1)):
        for m in range(z.M):
            for g in range(z.PR):
                at = slice(g * SEG + shift, (g + 1) * SEG + shift)
                water[m, row : row + 1, at] = edges[side, m, g : g + 1, :]


def prepare_kernel(z, k):
    size = min(BLOCK, z.W)
    parts = z.W // size
    small = k.i.seg, k.i.lake, k.i.slot, k.i.storage, k.i.area, k.i.release, k.i.link, k.i.table
    load(*small)
    cls, inv = k.s.cls, k.s.inv
    columns = [pl.ds(p * size, size) for p in range(parts)]
    coming = [k.copy(k.i.cls.h.at[:, at], cls.at[:, at]) for at in columns]
    wait(*small)
    payload = k.o.payload.v
    payload[0] = jnp.zeros((z.BR, LANES), F32)
    payload[0, : z.M, : z.LD] = k.i.storage.v[...]
    for n, x in enumerate((k.i.area, k.i.release, k.i.link)):
        payload[0, z.M + n : z.M + n + 1, : z.LD] = x.v[...].astype(F32)
    for n in range(1, z.NT):
        payload[n] = payload[0]
    k.o.payload.send()
    one_hots(z, k)
    send(k.o.near, k.o.near_edges)
    table = k.i.table.v[...]
    for p in range(parts):
        coming[p].wait()

        def look(i, _):
            at = pl.ds(pl.multiple_of(p * size + i * LANES, LANES), LANES)
            inv[:, at] = look_up(table, cls[:, at])
            return 0

        lax.fori_loop(0, size // LANES, look, 0, unroll=16)
        k.stores.append(k.copy(inv.at[:, columns[p]], k.o.inv.h.at[:, columns[p]]))


def one_hots(z, k):
    lane = lane_ids((1, LANES))
    contact = row_ids((z.C, LANES))
    place_g = row_ids((z.PR, LANES))
    inside = jnp.full((z.C, 1), z.LK, F32)
    on_edge = [jnp.full((z.PR, 1), z.LK, F32) for _ in range(2)]
    firsts = (0, (z.R - 1) * z.PR)
    for tile in range(z.CT):
        segs = jnp.full((1, LANES), -1, I32)
        slots = jnp.full((1, LANES), z.LK, I32)
        for c in range(tile * LANES, min(z.C, (tile + 1) * LANES)):
            owner, place = divmod(c, z.CAP)
            lake_id = k.i.lake.v[0, owner, place]
            found = jnp.where(lake_id >= 0, k.i.slot.v[jnp.maximum(lake_id, 0)], z.LK)
            segs = jnp.where(lane == c - tile * LANES, k.i.seg.v[0, owner, place], segs)
            slots = jnp.where(lane == c - tile * LANES, found, slots)
        more = (slots - z.LK).astype(F32)
        central = (segs >= z.PR) & (segs < firsts[1])
        mine = lane_ids((z.C, LANES)) + tile * LANES == contact
        inside += jnp.sum(jnp.where(mine & central, more, 0.0), axis=1, keepdims=True)
        for side in range(2):
            here = place_g + firsts[side] == segs
            on_edge[side] += jnp.sum(jnp.where(here, more, 0.0), axis=1, keepdims=True)
    for j in range(z.LT):
        k.o.near.v[j] = jnp.where(inside == (lane_ids((z.C, LANES)) + j * LANES).astype(F32), 1.0, 0.0)
        for side in range(2):
            ids = (lane_ids((z.PR, LANES)) + j * LANES).astype(F32)
            k.o.near_edges.v[side * z.LT + j] = jnp.where(on_edge[side] == ids, 1.0, 0.0)


def flow_kernel(z, k, first):
    size = min(BLOCK, z.W)
    parts = z.W // size
    inv, bed, water, rain = k.s.inv, k.s.bed, k.s.water, k.s.rain
    k.i.seg.load()
    columns = [(pl.ds(p * size, size), pl.ds(p * size + LANES, size)) for p in range(parts)]
    if not first:
        k.i.water_c.load()
        whole = k.copy(k.i.wet.h, water.at[:, :, pl.ds(LANES, z.W)])
        k.i.edges.load()
    coming = []
    for at, inner in columns:
        coming.append([
            k.copy(k.i.bed.h.at[:, at], bed.at[:, inner]),
            k.copy(k.i.inv.h.at[:, at], inv.at[:, inner]),
            k.copy(k.i.rain.h.at[:, :, at], rain.at[:, :, at]),
        ])
        if first:
            coming[-1].append(k.copy(k.i.wet.h.at[:, :, at], water.at[:, :, inner]))
    k.pass_on()
    k.i.seg.wait()
    if not first:
        k.i.water_c.wait()
        whole.wait()
        scatter_contacts(z, k.i.seg.v, k.i.water_c.v, water, LANES)
        k.i.edges.wait()
        set_edges(z, k.i.edges.v, water, LANES)

    def prepare(p):
        for copy in coming[p]:
            copy.wait()
        sides = dict(left=p == 0, right=p == parts - 1)
        widen(z, inv, **sides)
        widen(z, bed, **sides)
        for m in range(z.M):
            widen(z, water, (m,), **sides)

    def ready(j):
        if j == 0:
            prepare(0)
        if j + 1 < parts:
            prepare(j + 1)

    done = send_blocks(z, k, k.s.out, k.o.next.h)
    flow_blocks(z, water, bed, inv, rain, k.s.out, k.o.edges.v, done, ready)
    gather_contacts(z, k.i.seg.v, k.s.out, k.o.wet_c.v)
    if first:
        for c, r, at in contact_places(z, k.i.seg.v):
            k.o.bed_c.v[c : c + 1, :] = bed[pl.ds(r, 1), pl.ds(at + LANES, SEG)]
            k.s.bed_c[c : c + 1, :] = bed[pl.ds(r, 1), pl.ds(at + LANES, SEG)]
        k.stores.append(k.copy(k.s.bed_c, k.o.bed_kept.h))


def last_kernel(z, k):
    load(k.i.wet, k.i.seg, k.i.water_c, k.i.edges)
    k.pass_on()
    wait(k.i.wet, k.i.seg, k.i.water_c, k.i.edges)
    scatter_contacts(z, k.i.seg.v, k.i.water_c.v, k.i.wet.v, 0)
    set_edges(z, k.i.edges.v, k.i.wet.v, 0)
    k.stores.append(k.copy(k.i.wet.v, k.o.depth.h))


def pick(z, near, table, m):
    total = near[0] * table[m * z.LT : m * z.LT + 1, :]
    for j in range(1, z.LT):
        total += near[j] * table[m * z.LT + j : m * z.LT + j + 1, :]
    return jnp.sum(total, axis=1, keepdims=True)


def shift_slots(x, count):
    rows, lanes = divmod(count, LANES)
    size = x.shape[0]
    turned = pltpu.roll(x, lanes, 1) if lanes else x
    low = pltpu.roll(turned, rows % size, 0) if rows % size else turned
    if not lanes:
        return low
    high = pltpu.roll(turned, (rows + 1) % size, 0)
    return jnp.where(lane_ids(x.shape) < lanes, high, low)


def laps(z):
    count = z.LD
    while count < z.LK:
        yield count
        count *= 2


def cascade(z, consts, entering):
    for lap, count in enumerate(laps(z)):
        entering = entering + consts[3 + lap] * shift_slots(entering, count)
    return entering


def slot_ids(z):
    shape = (z.SR, LANES)
    return (row_ids(shape) % z.LT) * LANES + lane_ids(shape)


def levels_of(z, pool, area):
    return jnp.where(slot_ids(z) == z.LK, FAR, pool / area)


def lay_out(z, got, pool, consts):
    pool[...] = jnp.zeros_like(pool)
    consts[...] = jnp.zeros_like(consts)
    consts[0] = jnp.ones((z.SR, LANES), F32)
    for t in range(z.NT):
        done = 0
        while done < z.LD:
            j, at = divmod(t * z.LD + done, LANES)
            n = min(z.LD - done, LANES - at)
            for m in range(z.M):
                r = m * z.LT + j
                pool[r : r + 1, at : at + n] = got[t, m : m + 1, done : done + n]
                for i in range(3):
                    consts[i, r : r + 1, at : at + n] = got[t, z.M + i : z.M + i + 1, done : done + n]
            done += n
    consts[2] = jnp.where(slot_ids(z) >= z.LD, consts[2], 0.0)
    factor = consts[1] * consts[2]
    for lap, count in enumerate(laps(z)):
        consts[3 + lap] = factor
        factor = factor * shift_slots(factor, count)


def cross_edges(z, k, own, other, rows):
    for n in range(2):
        side, flag = side_of(n)
        own_bed, own_inv, other_bed, other_inv = rows(side, n)
        for m in range(z.M):
            a, b = own(side, n, m), other(n, m)
            flow = (mobility(a, own_inv) + mobility(b, other_inv)) * ((other_bed + b) - (own_bed + a))
            k.i.edges.v[side, m] += flow * flag


def contact_step(z, k, level, bed_rows):
    rows = [[jnp.zeros((SUBLANES, LANES), F32) for _ in range(z.LT)] for _ in range(z.M)]

    def take(near, m, w, bed):
        taken = taken_of(w, bed + w, pick(z, near, level, m))
        sums = jnp.sum(taken, axis=1, keepdims=True) * (1.0 / SEG)
        for j in range(z.LT):
            part = near[j] * sums
            for r in range(0, part.shape[0], SUBLANES):
                rows[m][j] += part[r : r + SUBLANES]
        return w - taken

    for side in range(2):
        near = k.i.near_edges.v.at[pl.ds(side * z.LT, z.LT)]
        for m in range(z.M):
            k.o.edges.v[side, m] = take(near, m, k.i.edges.v[side, m], bed_rows(side))
    bed = k.i.bed_c.v[...]
    for m in range(z.M):
        at = slice(m * z.C, (m + 1) * z.C)
        k.o.water_c.v[at, :] = take(k.i.near.v, m, k.i.wet_c.v[at, :], bed)
    found = [jnp.sum(rows[m][j], axis=0, keepdims=True) for m in range(z.M) for j in range(z.LT)]
    if z.SR > len(found):
        found.append(jnp.zeros((z.SR - len(found), LANES), F32))
    return jnp.concatenate(found, axis=0)


def send_edges(z, k, exchange):
    k.o.edges.send()
    if exchange:
        for n, out in enumerate((k.o.edge0, k.o.edge1)):
            side, _ = side_of(n)
            k.stores.append(k.copy(k.o.edges.v.at[side], out.h))


def open_kernel(z, k):
    own, other, pack = (k.i.own0, k.i.own1), (k.i.from0, k.i.from1), k.o.pack.v
    for n in range(2):
        side, _ = side_of(n)
        pack[side, :2] = own[n].v[z.M : z.M + 2]
        pack[side, 2:] = other[n].v[z.M : z.M + 2]
    k.o.pack.send()
    cross_edges(
        z, k,
        lambda side, n, m: own[n].v[m],
        lambda n, m: other[n].v[m],
        lambda side, n: [pack[side, i] for i in range(4)],
    )
    pool, consts = k.s.pool, k.o.consts.v
    lay_out(z, k.i.got.v, pool, consts)
    k.o.consts.send()
    k.o.state.v[0] = pool[...]
    k.o.state.v[1] = jnp.zeros((z.SR, LANES), F32)
    k.o.state.send()
    k.s.level[...] = levels_of(z, pool[...], consts[0])
    sums = contact_step(z, k, k.s.level, lambda side: pack[side, 0])
    for n in range(z.NT):
        k.o.payload.v[n] = sums
    send(k.o.payload, k.o.water_c)
    send_edges(z, k, True)


def step_reservoirs(z, consts, pool, total, lateral):
    area, release, link = consts[0], consts[1], consts[2]
    released = cascade(z, consts, release * (pool + lateral))
    pool = pool + lateral + link * shift_slots(released, z.LD) - released
    return pool, total + released


def sum_members(z, x):
    total = x
    for m in range(1, z.M):
        total = total + pltpu.roll(x, z.SR - m * z.LT, 0)
    return jnp.where(row_ids(x.shape) < z.LT, total, 0.0)


def contact_kernel(z, k, last):
    got, consts = k.i.got.v, k.i.consts.v
    lateral = got[0]
    for t in range(1, z.NT):
        lateral += got[t]
    pool, total = step_reservoirs(z, consts, k.i.state.v[0], k.i.state.v[1], lateral)
    k.o.state.v[0] = pool
    k.o.state.v[1] = total
    k.o.state.send()
    k.s.level[...] = levels_of(z, pool, consts[0])
    other, pack = (k.i.from0, k.i.from1), k.i.pack.v
    cross_edges(
        z, k,
        lambda side, n, m: k.i.own.v[side, m],
        lambda n, m: other[n].v[m],
        lambda side, n: [pack[side, i] for i in range(4)],
    )
    sums = contact_step(z, k, k.s.level, lambda side: pack[side, 0])
    payload = k.o.payload.v
    if last:
        summed = sum_members(z, total) * (1.0 / z.NT)
        others = consts[1] * (sum_members(z, sums) + sum_members(z, pool) * (1.0 / z.NT))
        others = others + summed - consts[3] * shift_slots(summed, z.LD)
        member = lax.axis_index("ens")
        for e in range(z.E):
            block = jnp.where(member == e, sums, others)
            for t in range(z.NT):
                payload[e * z.NT + t] = block
    else:
        for t in range(z.NT):
            payload[t] = sums
    send(k.o.payload, k.o.water_c)
    send_edges(z, k, not last)


def own_slots(z, x, tile):
    begin = tile * z.LD
    at = begin % LANES
    j = begin // LANES
    out = jnp.zeros((1, LANES), F32)
    turned = pltpu.roll(x, LANES - at, 1)
    lane = lane_ids((1, LANES))
    for n in range(z.LT):
        out = jnp.where((j == n) & (lane < LANES - at), turned[n : n + 1], out)
        out = jnp.where((j + 1 == n) & (lane >= LANES - at), turned[n : n + 1], out)
    return out


def close_kernel(z, k):
    tile = lax.axis_index("tiles")
    member = lax.axis_index("ens")
    got, consts = k.i.got.v, k.i.consts.v
    lateral = jnp.zeros((z.SR, LANES), F32)
    others = jnp.zeros((z.SR, LANES), F32)
    for e in range(z.E):
        part = got[e * z.NT]
        for t in range(1, z.NT):
            part += got[e * z.NT + t]
        lateral = jnp.where(member == e, part, lateral)
        others = others + jnp.where(member == e, 0.0, part)
    pool, total = step_reservoirs(z, consts, k.i.state.v[0], k.i.state.v[1], lateral)
    for m in range(z.M):
        at = slice(m * z.LT, (m + 1) * z.LT)
        k.o.storage.v[m : m + 1, :] = own_slots(z, pool[at], tile)[:, : z.LD]
    mean = (sum_members(z, total) + cascade(z, consts, others)) * (1.0 / (z.M * z.E))
    k.o.outflow.v[...] = own_slots(z, mean[: z.LT], tile)[:, : z.LD]
    send(k.o.storage, k.o.outflow)


def shards(
    depth, bed, rain, rough_class, class_n, contact_seg, contact_lake, lake_slot, storage, area, release, upstream_link
):
    z = types.SimpleNamespace()
    z.M, z.R, z.W = depth.shape
    z.NT = lax.axis_size("tiles")
    z.E = lax.axis_size("ens")
    z.LD = storage.shape[1]
    z.LK = z.NT * z.LD
    z.CAP = contact_seg.shape[2]
    z.C = contact_seg.shape[1] * z.CAP
    z.CT = -(-z.C // LANES)
    z.PR = z.W // SEG
    z.classes = class_n.shape[0]
    z.LT = z.LK // LANES + 1
    z.SR = up_to(z.M * z.LT, SUBLANES)
    z.BR = up_to(z.M + 3, SUBLANES)
    levels = len(list(laps(z)))
    blocks = z.W // min(BLOCK, z.W)
    tile_shape = (z.M, z.R, z.W)
    edge_shape = (z.M, z.PR, SEG)
    pack_shape = (z.M + 2, z.PR, SEG)
    near_shape = (z.LT, z.C, LANES)
    state_shape = (2, z.SR, LANES)
    const_shape = (3 + levels, z.SR, LANES)
    contact_shape = (z.M * z.C, SEG)
    wide_tile = pltpu.VMEM((z.M, z.R, z.W + 2 * LANES), F32)
    wide_rows = pltpu.VMEM((z.R, z.W + 2 * LANES), F32)
    plain_tile = pltpu.VMEM(tile_shape, F32)
    onward = [(i, (i + 1) % z.NT) for i in range(z.NT)]
    back = [(j, i) for i, j in onward]

    def share(x, axes):
        return lax.all_to_all(x, axes, 0, 0, tiled=True)

    def swap(top, bottom):
        return lax.ppermute(bottom, "tiles", onward), lax.ppermute(top, "tiles", back)

    edges_shape = (2,) + edge_shape
    level_buffer = pltpu.VMEM((z.SR, LANES), F32)
    opened = staged_call(
        pack_kernel, z,
        dict(depth=Raw(depth), bed=Raw(bed), cls=Raw(rough_class), class_n=Scalars(class_n)),
        dict(pack0=pack_shape, pack1=pack_shape, table=(z.R, LANES)),
        dict(rows=pltpu.VMEM((2, z.M + 1, z.W), F32), cls_rows=pltpu.VMEM((2, 1, z.W), I32), ids=pltpu.VMEM((z.PR, SEG), I32)),
        extra_sems=2 * (z.M + 2),
    )
    from0, from1 = swap(opened.pack0, opened.pack1)
    kept = staged_call(
        prepare_kernel, z,
        dict(cls=Raw(rough_class), table=opened.table, seg=Scalars(contact_seg), lake=Scalars(contact_lake),
             slot=Scalars(lake_slot), storage=storage, area=area.reshape(1, -1), release=release.reshape(1, -1),
             link=upstream_link.reshape(1, -1)),
        dict(payload=(z.NT, z.BR, LANES), inv=Raw((z.R, z.W)), near=near_shape, near_edges=(2 * z.LT, z.PR, LANES)),
        dict(cls=pltpu.VMEM((z.R, z.W), I32), inv=pltpu.VMEM((z.R, z.W), F32)),
        extra_sems=2 * blocks,
    )
    got = share(kept.payload, "tiles")
    inv, near, near_edges = kept.inv, kept.near, kept.near_edges
    flow_scratch = dict(water=wide_tile, bed=wide_rows, inv=wide_rows, rain=plain_tile, out=plain_tile)
    flow_out = dict(next=Raw(tile_shape), wet_c=Here(contact_shape), edges=Here(edges_shape))
    flow = staged_call(
        functools.partial(flow_kernel, first=True), z,
        dict(wet=Raw(depth), seg=Scalars(contact_seg), bed=Raw(bed), inv=Raw(inv), rain=Raw(rain), near=Passed(near),
             near_edges=Passed(near_edges), own0=Passed(opened.pack0), own1=Passed(opened.pack1)),
        dict(bed_c=Here((z.C, SEG)), bed_kept=Raw((z.C, SEG)), **flow_out),
        dict(bed_c=pltpu.VMEM((z.C, SEG), F32), **flow_scratch),
        extra_sems=5 * blocks + 1,
    )
    bed_kept = flow.bed_kept

    step_out = dict(edges=edges_shape, water_c=contact_shape, state=state_shape)
    exchange_out = dict(edge0=Raw(edge_shape), edge1=Raw(edge_shape))
    now = staged_call(
        open_kernel, z,
        dict(got=Here(got, free=True), from0=Here(from0, free=True), from1=Here(from1, free=True), own0=Here(flow.own0),
             own1=Here(flow.own1), edges=Here(flow.edges), near=Here(flow.near), near_edges=Here(flow.near_edges),
             wet_c=Here(flow.wet_c), bed_c=Here(flow.bed_c)),
        dict(payload=(z.NT, z.SR, LANES), pack=(2, 4, z.PR, SEG), consts=const_shape, **step_out, **exchange_out),
        dict(pool=level_buffer, level=level_buffer),
        extra_sems=2,
    )
    consts, pack = now.consts, now.pack
    for step in range(1, STEPS):
        got = share(now.payload, "tiles")
        from0, from1 = swap(now.edge0, now.edge1)
        last = step == STEPS - 1
        flow = staged_call(
            functools.partial(flow_kernel, first=False), z,
            dict(wet=Raw(flow.next), seg=Scalars(contact_seg), water_c=now.water_c, edges=now.edges, bed=Raw(bed),
                 inv=Raw(inv), rain=Raw(rain), state=Passed(now.state), consts=Passed(consts), near=Passed(near),
                 near_edges=Passed(near_edges), pack=Passed(pack), own=Passed(now.edges), bed_c=Passed(bed_kept)),
            flow_out,
            flow_scratch,
            extra_sems=1 + 4 * blocks,
        )
        now = staged_call(
            functools.partial(contact_kernel, last=last), z,
            dict(got=Here(got, free=True), from0=Here(from0, free=True), from1=Here(from1, free=True), own=Here(flow.own),
                 edges=Here(flow.edges), state=Here(flow.state), consts=Here(flow.consts), pack=Here(flow.pack),
                 near=Here(flow.near), near_edges=Here(flow.near_edges), wet_c=Here(flow.wet_c), bed_c=Here(flow.bed_c)),
            dict(payload=((z.E if last else 1) * z.NT, z.SR, LANES), **step_out, **({} if last else exchange_out)),
            dict(level=level_buffer),
            extra_sems=2,
        )
    got = share(now.payload, ("ens", "tiles"))
    done = staged_call(
        last_kernel, z,
        dict(wet=flow.next, seg=Scalars(contact_seg), water_c=now.water_c, edges=now.edges, state=Passed(now.state),
             consts=Passed(consts)),
        dict(depth=Raw(tile_shape)),
        extra_sems=1,
    )
    closed = staged_call(
        close_kernel, z,
        dict(got=Here(got, free=True), state=Here(done.state), consts=Here(done.consts)),
        dict(storage=(z.M, z.LD), outflow=(1, z.LD)),
    )
    return done.depth, closed.storage, closed.outflow.reshape(-1)


def solution(mesh):
    return jax.shard_map(
        shards,
        mesh=mesh,
        in_specs=(
            P("ens", "tiles", None),
            P("tiles", None),
            P("ens", "tiles", None),
            P("tiles", None),
            P(),
            P("tiles", None, None),
            P("tiles", None, None),
            P(),
            P("ens", "tiles"),
            P("tiles"),
            P("tiles"),
            P("tiles"),
        ),
        out_specs=(P("ens", "tiles", None), P("ens", "tiles"), P("tiles")),
        check_vma=False,
    )
```

```python
import functools
import types

import jax
import jax.numpy as jnp
from jax import lax
from jax.experimental import pallas as pl
from jax.experimental.pallas import tpu as pltpu
from jax.sharding import PartitionSpec as P

SEG = 256
STEPS = 4
LANES = 128
SUBLANES = 8
FAR = 1e30

flow_rate = 0.035
drain_rate = 0.4

F32 = jnp.float32
I32 = jnp.int32
VMEM_LIMIT = 40 * 2**20
BLOCK = 4096


def up_to(value, unit):
    return -(-value // unit) * unit


def lane_ids(shape):
    return lax.broadcasted_iota(I32, shape, len(shape) - 1)


def row_ids(shape):
    return lax.broadcasted_iota(I32, shape, len(shape) - 2)


def mobility(water, inv_n):
    return water * jnp.exp2(jnp.log2(jnp.abs(water)) * (2.0 / 3.0)) * inv_n


def taken_of(water, surface, level):
    excess = jnp.maximum(surface - level, 0.0)
    return drain_rate * water * excess / (1.0 + excess)


class Array:
    def __init__(self, kernel, h, v):
        self.kernel, self.h, self.v = kernel, h, v

    def load(self):
        self.coming = self.kernel.copy(self.h, self.v)

    def wait(self):
        self.coming.wait()

    def send(self):
        self.kernel.stores.append(self.kernel.copy(self.v, self.h))


class Kernel:
    def __init__(self, sems):
        self.sems, self.count, self.stores = sems, 0, []

    def copy(self, source, target):
        copy = pltpu.make_async_copy(source, target, self.sems.at[self.count])
        self.count += 1
        copy.start()
        return copy

    def pass_on(self):
        for source, target in self.passed:
            self.stores.append(self.copy(source, target))

    def finish(self):
        for copy in self.stores:
            copy.wait()


def load(*arrays):
    for array in arrays:
        array.load()


def wait(*arrays):
    for array in arrays:
        array.wait()


def send(*arrays):
    for array in arrays:
        array.send()


class Staged:
    space = pltpu.VMEM

    def __init__(self, x, free=False):
        self.x, self.free = x, free


class Scalars(Staged):
    space = pltpu.SMEM


class Raw(Staged):
    space = None


class Here(Staged):
    space = None


class Passed(Here):
    pass


def staged_call(body, z, ins, outs, scratch=None, alias=None, extra_sems=0, micros=60):
    scratch = scratch or {}
    ins = {n: x if isinstance(x, Staged) else Staged(x) for n, x in ins.items()}
    outs = {n: x if isinstance(x, Staged) else Staged(x) for n, x in outs.items()}
    passed = [n for n, x in ins.items() if isinstance(x, Passed)]
    outs.update({n: Here(ins[n].x.shape) for n in passed})
    extra_sems += len(passed)
    here_in = [isinstance(x, Here) and not isinstance(x, Passed) for x in ins.values()]
    here_out = [isinstance(x, Here) for x in outs.values()]
    shapes = [x.space(x.x.shape, x.x.dtype) for x in ins.values() if x.space]
    shapes += [x.space(x.x, F32) for x in outs.values() if x.space]
    count = len(shapes) + extra_sems
    shapes += list(scratch.values())
    shapes.append(pltpu.SemaphoreType.DMA((count,)))

    def kernel(*refs):
        refs = list(refs)
        k = Kernel(refs.pop())
        arrays_in, arrays_out = [{n: refs.pop(0) for n in names} for names in (ins, outs)]
        for held, kinds in ((arrays_in, ins), (arrays_out, outs)):
            for n, x in kinds.items():
                held[n] = Array(k, held[n], refs.pop(0) if x.space else held[n])
        k.i = types.SimpleNamespace(**arrays_in)
        k.o = types.SimpleNamespace(**arrays_out)
        k.s = types.SimpleNamespace(**{n: refs.pop(0) for n in scratch})
        k.passed = [(arrays_in[n].h, arrays_out[n].h) for n in passed]
        body(z, k)
        k.finish()

    in_hbm = pl.BlockSpec(memory_space=pltpu.HBM)
    in_vmem = pl.BlockSpec(memory_space=pltpu.VMEM)
    order_in, order_out = list(ins), list(outs)
    results = pl.pallas_call(
        kernel,
        out_shape=[(pltpu.VMEM if here else pltpu.HBM)(x.x, F32) for x, here in zip(outs.values(), here_out)],
        in_specs=[in_vmem if here else in_hbm for here in here_in],
        out_specs=[in_vmem if here else in_hbm for here in here_out],
        scratch_shapes=shapes,
        input_output_aliases={order_in.index(a): order_out.index(b) for a, b in (alias or {}).items()},
        compiler_params=pltpu.CompilerParams(vmem_limit_bytes=VMEM_LIMIT),
        cost_estimate=pl.CostEstimate(
            flops=int(micros * 1e9), transcendentals=int(micros * 1e6), bytes_accessed=int(micros * 3e6)
        ),
    )(*[
        pltpu.with_memory_space_constraint(x.x, pltpu.VMEM if here else pltpu.HBM) if not (here and x.free) else x.x
        for x, here in zip(ins.values(), here_in)
    ])
    return types.SimpleNamespace(**dict(zip(order_out, results)))


def side_of(n):
    tile = lax.axis_index("tiles")
    there = tile > 0 if n == 0 else tile < lax.axis_size("tiles") - 1
    return n, jnp.where(there, 1.0, 0.0)


def pack_kernel(z, k):
    k.i.class_n.load()
    rows, cls_rows = k.s.rows, k.s.cls_rows
    copies = []
    for side, row in enumerate((0, z.R - 1)):
        for m in range(z.M):
            copies.append(k.copy(k.i.depth.h.at[m, pl.ds(row, 1)], rows.at[side, pl.ds(m, 1)]))
        copies.append(k.copy(k.i.bed.h.at[pl.ds(row, 1)], rows.at[side, pl.ds(z.M, 1)]))
        copies.append(k.copy(k.i.cls.h.at[pl.ds(row, 1)], cls_rows.at[side]))
    k.i.class_n.wait()
    k.o.table.v[...] = inv_table(z, k.i.class_n.v, z.R)
    k.o.table.send()
    wide = inv_table(z, k.i.class_n.v, z.PR)
    for copy in copies:
        copy.wait()
    ids = k.s.ids
    for n, out in enumerate((k.o.pack0, k.o.pack1)):
        side, _ = side_of(n)
        for g in range(z.PR):
            at = slice(g * SEG, (g + 1) * SEG)
            for m in range(z.M + 1):
                out.v[m, g : g + 1, :] = rows[side, m : m + 1, at]
            ids[g : g + 1, :] = cls_rows[side, :, at]
        for half in range(0, SEG, LANES):
            at = slice(half, half + LANES)
            out.v[z.M + 1, :, at] = look_up(wide, ids[:, at])
        out.send()


def inv_table(z, class_n, rows):
    lane = lane_ids((rows, LANES))
    names = jnp.ones((rows, LANES), F32)
    for n in range(z.classes):
        names = jnp.where(lane == n, class_n[n], names)
    return flow_rate * 0.5 / names


def look_up(table, ids):
    return jnp.take_along_axis(table, ids, axis=1, mode="promise_in_bounds")


def widen(z, ref, index=(), left=True, right=True):
    rows = slice(None)
    if left:
        ref[index + (rows, slice(0, LANES))] = pltpu.roll(ref[index + (rows, slice(LANES, 2 * LANES))], LANES - 1, 1)
    if right:
        ref[index + (rows, slice(z.W + LANES, z.W + 2 * LANES))] = pltpu.roll(
            ref[index + (rows, slice(z.W, z.W + LANES))], 1, 1
        )


def flow_blocks(z, water, bed, inv, rain, out, edges, done, ready=None):
    size = min(BLOCK, z.W)
    segs = size // SEG
    row = row_ids((z.R, size))
    bottom = row == z.R - 1
    top = row == 0

    def block(j, _):
        base = j * size if ready else pl.multiple_of(j * size, size)
        wide = pl.ds(base, size + 2 * LANES)
        at = pl.ds(base, size)
        b, v = bed[:, wide], inv[:, wide]
        for m in range(z.M):
            w = water[m, :, wide]
            s = b + w
            q = mobility(w, v)
            s_right = pltpu.roll(s, size + 2 * LANES - 1, 1)
            q_right = pltpu.roll(q, size + 2 * LANES - 1, 1)
            f = ((q + q_right) * (s - s_right))[:, : size + LANES]
            net = pltpu.roll(f, 1, 1)[:, LANES:] - f[:, LANES:]
            s = s[:, LANES : size + LANES]
            q = q[:, LANES : size + LANES]
            flow = (q + pltpu.roll(q, z.R - 1, 0)) * (s - pltpu.roll(s, z.R - 1, 0))
            flow = jnp.where(bottom, 0.0, flow)
            above = jnp.where(top, 0.0, pltpu.roll(flow, 1, 0))
            wet = w[:, LANES : size + LANES] + (net + (above - flow)) + rain[m, :, at]
            out[m, :, at] = wet
            for i in range(segs):
                part = slice(i * SEG, (i + 1) * SEG)
                edges[0, m, pl.ds(j * segs + i, 1), :] = wet[:1, part]
                edges[1, m, pl.ds(j * segs + i, 1), :] = wet[z.R - 1 :, part]
        done(j, at)
        return 0

    if ready:
        for j in range(z.W // size):
            ready(j)
            block(j, 0)
    else:
        lax.fori_loop(0, z.W // size, block, 0)


def send_blocks(z, k, source, target):
    size = min(BLOCK, z.W)
    first = k.count
    k.count += z.W // size

    def copy(j):
        at = pl.ds(pl.multiple_of(j * size, size), size)
        return pltpu.make_async_copy(source.at[:, :, at], target.at[:, :, at], k.sems.at[first + j])

    for j in range(z.W // size):
        k.stores.append(copy(j))
    return lambda j, at: copy(j).start()


def contact_places(z, seg):
    for c in range(z.C):
        owner, place = divmod(c, z.CAP)
        s = seg[0, owner, place]
        yield c, s // z.PR, pl.multiple_of((s % z.PR) * SEG, SEG)


def gather_contacts(z, seg, water, out):
    for c, r, at in contact_places(z, seg):
        for m in range(z.M):
            out[m * z.C + c : m * z.C + c + 1, :] = water[m, pl.ds(r, 1), pl.ds(at, SEG)]


def scatter_contacts(z, seg, values, water, shift):
    for c, r, at in contact_places(z, seg):
        for m in range(z.M):
            water[m, pl.ds(r, 1), pl.ds(at + shift, SEG)] = values[m * z.C + c : m * z.C + c + 1, :]


def set_edges(z, edges, water, shift):
    for side, row in enumerate((0, z.R - 1)):
        for m in range(z.M):
            for g in range(z.PR):
                at = slice(g * SEG + shift, (g + 1) * SEG + shift)
                water[m, row : row + 1, at] = edges[side, m, g : g + 1, :]


def prepare_kernel(z, k):
    size = min(BLOCK, z.W)
    parts = z.W // size
    small = k.i.seg, k.i.lake, k.i.slot, k.i.storage, k.i.area, k.i.release, k.i.link, k.i.table
    load(*small)
    cls, inv = k.s.cls, k.s.inv
    columns = [pl.ds(p * size, size) for p in range(parts)]
    coming = [k.copy(k.i.cls.h.at[:, at], cls.at[:, at]) for at in columns]
    wait(*small)
    payload = k.o.payload.v
    payload[0] = jnp.zeros((z.BR, LANES), F32)
    payload[0, : z.M, : z.LD] = k.i.storage.v[...]
    for n, x in enumerate((k.i.area, k.i.release, k.i.link)):
        payload[0, z.M + n : z.M + n + 1, : z.LD] = x.v[...].astype(F32)
    for n in range(1, z.NT):
        payload[n] = payload[0]
    k.o.payload.send()
    one_hots(z, k)
    send(k.o.near, k.o.near_edges)
    table = k.i.table.v[...]
    for p in range(parts):
        coming[p].wait()

        def look(i, _):
            at = pl.ds(pl.multiple_of(p * size + i * LANES, LANES), LANES)
            inv[:, at] = look_up(table, cls[:, at])
            return 0

        lax.fori_loop(0, size // LANES, look, 0, unroll=16)
        k.stores.append(k.copy(inv.at[:, columns[p]], k.o.inv.h.at[:, columns[p]]))


def one_hots(z, k):
    lane = lane_ids((1, LANES))
    contact = row_ids((z.C, LANES))
    place_g = row_ids((z.PR, LANES))
    inside = jnp.full((z.C, 1), z.LK, F32)
    on_edge = [jnp.full((z.PR, 1), z.LK, F32) for _ in range(2)]
    firsts = (0, (z.R - 1) * z.PR)
    for tile in range(z.CT):
        segs = jnp.full((1, LANES), -1, I32)
        slots = jnp.full((1, LANES), z.LK, I32)
        for c in range(tile * LANES, min(z.C, (tile + 1) * LANES)):
            owner, place = divmod(c, z.CAP)
            lake_id = k.i.lake.v[0, owner, place]
            found = jnp.where(lake_id >= 0, k.i.slot.v[jnp.maximum(lake_id, 0)], z.LK)
            segs = jnp.where(lane == c - tile * LANES, k.i.seg.v[0, owner, place], segs)
            slots = jnp.where(lane == c - tile * LANES, found, slots)
        more = (slots - z.LK).astype(F32)
        central = (segs >= z.PR) & (segs < firsts[1])
        mine = lane_ids((z.C, LANES)) + tile * LANES == contact
        inside += jnp.sum(jnp.where(mine & central, more, 0.0), axis=1, keepdims=True)
        for side in range(2):
            here = place_g + firsts[side] == segs
            on_edge[side] += jnp.sum(jnp.where(here, more, 0.0), axis=1, keepdims=True)
    for j in range(z.LT):
        k.o.near.v[j] = jnp.where(inside == (lane_ids((z.C, LANES)) + j * LANES).astype(F32), 1.0, 0.0)
        for side in range(2):
            ids = (lane_ids((z.PR, LANES)) + j * LANES).astype(F32)
            k.o.near_edges.v[side * z.LT + j] = jnp.where(on_edge[side] == ids, 1.0, 0.0)


def flow_kernel(z, k, first):
    size = min(BLOCK, z.W)
    parts = z.W // size
    inv, bed, water, rain = k.s.inv, k.s.bed, k.s.water, k.s.rain
    k.i.seg.load()
    columns = [(pl.ds(p * size, size), pl.ds(p * size + LANES, size)) for p in range(parts)]
    if not first:
        k.i.water_c.load()
        whole = k.copy(k.i.wet.h, water.at[:, :, pl.ds(LANES, z.W)])
        k.i.edges.load()
    coming = []
    for at, inner in columns:
        coming.append([
            k.copy(k.i.bed.h.at[:, at], bed.at[:, inner]),
            k.copy(k.i.inv.h.at[:, at], inv.at[:, inner]),
            k.copy(k.i.rain.h.at[:, :, at], rain.at[:, :, at]),
        ])
        if first:
            coming[-1].append(k.copy(k.i.wet.h.at[:, :, at], water.at[:, :, inner]))
    k.pass_on()
    k.i.seg.wait()
    if not first:
        k.i.water_c.wait()
        whole.wait()
        scatter_contacts(z, k.i.seg.v, k.i.water_c.v, water, LANES)
        k.i.edges.wait()
        set_edges(z, k.i.edges.v, water, LANES)

    def prepare(p):
        for copy in coming[p]:
            copy.wait()
        sides = dict(left=p == 0, right=p == parts - 1)
        widen(z, inv, **sides)
        widen(z, bed, **sides)
        for m in range(z.M):
            widen(z, water, (m,), **sides)

    def ready(j):
        if j == 0:
            prepare(0)
        if j + 1 < parts:
            prepare(j + 1)

    done = send_blocks(z, k, k.s.out, k.o.next.h)
    flow_blocks(z, water, bed, inv, rain, k.s.out, k.o.edges.v, done, ready)
    gather_contacts(z, k.i.seg.v, k.s.out, k.o.wet_c.v)
    if first:
        for c, r, at in contact_places(z, k.i.seg.v):
            k.o.bed_c.v[c : c + 1, :] = bed[pl.ds(r, 1), pl.ds(at + LANES, SEG)]
            k.s.bed_c[c : c + 1, :] = bed[pl.ds(r, 1), pl.ds(at + LANES, SEG)]
        k.stores.append(k.copy(k.s.bed_c, k.o.bed_kept.h))


def last_kernel(z, k):
    load(k.i.wet, k.i.seg, k.i.water_c, k.i.edges)
    k.pass_on()
    wait(k.i.wet, k.i.seg, k.i.water_c, k.i.edges)
    scatter_contacts(z, k.i.seg.v, k.i.water_c.v, k.i.wet.v, 0)
    set_edges(z, k.i.edges.v, k.i.wet.v, 0)
    k.stores.append(k.copy(k.i.wet.v, k.o.depth.h))


def pick(z, near, table, m):
    total = near[0] * table[m * z.LT : m * z.LT + 1, :]
    for j in range(1, z.LT):
        total += near[j] * table[m * z.LT + j : m * z.LT + j + 1, :]
    return jnp.sum(total, axis=1, keepdims=True)


def shift_slots(x, count):
    rows, lanes = divmod(count, LANES)
    size = x.shape[0]
    turned = pltpu.roll(x, lanes, 1) if lanes else x
    low = pltpu.roll(turned, rows % size, 0) if rows % size else turned
    if not lanes:
        return low
    high = pltpu.roll(turned, (rows + 1) % size, 0)
    return jnp.where(lane_ids(x.shape) < lanes, high, low)


def laps(z):
    count = z.LD
    while count < z.LK:
        yield count
        count *= 2


def cascade(z, consts, entering):
    for lap, count in enumerate(laps(z)):
        entering = entering + consts[3 + lap] * shift_slots(entering, count)
    return entering


def slot_ids(z):
    shape = (z.SR, LANES)
    return (row_ids(shape) % z.LT) * LANES + lane_ids(shape)


def levels_of(z, pool, area):
    return jnp.where(slot_ids(z) == z.LK, FAR, pool / area)


def lay_out(z, got, pool, consts):
    pool[...] = jnp.zeros_like(pool)
    consts[...] = jnp.zeros_like(consts)
    consts[0] = jnp.ones((z.SR, LANES), F32)
    for t in range(z.NT):
        done = 0
        while done < z.LD:
            j, at = divmod(t * z.LD + done, LANES)
            n = min(z.LD - done, LANES - at)
            for m in range(z.M):
                r = m * z.LT + j
                pool[r : r + 1, at : at + n] = got[t, m : m + 1, done : done + n]
                for i in range(3):
                    consts[i, r : r + 1, at : at + n] = got[t, z.M + i : z.M + i + 1, done : done + n]
            done += n
    consts[2] = jnp.where(slot_ids(z) >= z.LD, consts[2], 0.0)
    factor = consts[1] * consts[2]
    for lap, count in enumerate(laps(z)):
        consts[3 + lap] = factor
        factor = factor * shift_slots(factor, count)


def cross_edges(z, k, own, other, rows):
    for n in range(2):
        side, flag = side_of(n)
        own_bed, own_inv, other_bed, other_inv = rows(side, n)
        for m in range(z.M):
            a, b = own(side, n, m), other(n, m)
            flow = (mobility(a, own_inv) + mobility(b, other_inv)) * ((other_bed + b) - (own_bed + a))
            k.i.edges.v[side, m] += flow * flag


def contact_step(z, k, level, bed_rows):
    rows = [[jnp.zeros((SUBLANES, LANES), F32) for _ in range(z.LT)] for _ in range(z.M)]

    def take(near, m, w, bed):
        taken = taken_of(w, bed + w, pick(z, near, level, m))
        sums = jnp.sum(taken, axis=1, keepdims=True) * (1.0 / SEG)
        for j in range(z.LT):
            part = near[j] * sums
            for r in range(0, part.shape[0], SUBLANES):
                rows[m][j] += part[r : r + SUBLANES]
        return w - taken

    for side in range(2):
        near = k.i.near_edges.v.at[pl.ds(side * z.LT, z.LT)]
        for m in range(z.M):
            k.o.edges.v[side, m] = take(near, m, k.i.edges.v[side, m], bed_rows(side))
    bed = k.i.bed_c.v[...]
    for m in range(z.M):
        at = slice(m * z.C, (m + 1) * z.C)
        k.o.water_c.v[at, :] = take(k.i.near.v, m, k.i.wet_c.v[at, :], bed)
    found = [jnp.sum(rows[m][j], axis=0, keepdims=True) for m in range(z.M) for j in range(z.LT)]
    if z.SR > len(found):
        found.append(jnp.zeros((z.SR - len(found), LANES), F32))
    return jnp.concatenate(found, axis=0)


def send_edges(z, k, exchange):
    k.o.edges.send()
    if exchange:
        for n, out in enumerate((k.o.edge0, k.o.edge1)):
            side, _ = side_of(n)
            k.stores.append(k.copy(k.o.edges.v.at[side], out.h))


def open_kernel(z, k):
    own, other, pack = (k.i.own0, k.i.own1), (k.i.from0, k.i.from1), k.o.pack.v
    for n in range(2):
        side, _ = side_of(n)
        pack[side, :2] = own[n].v[z.M : z.M + 2]
        pack[side, 2:] = other[n].v[z.M : z.M + 2]
    k.o.pack.send()
    cross_edges(
        z, k,
        lambda side, n, m: own[n].v[m],
        lambda n, m: other[n].v[m],
        lambda side, n: [pack[side, i] for i in range(4)],
    )
    pool, consts = k.s.pool, k.o.consts.v
    lay_out(z, k.i.got.v, pool, consts)
    k.o.consts.send()
    k.o.state.v[0] = pool[...]
    k.o.state.v[1] = jnp.zeros((z.SR, LANES), F32)
    k.o.state.send()
    k.s.level[...] = levels_of(z, pool[...], consts[0])
    sums = contact_step(z, k, k.s.level, lambda side: pack[side, 0])
    for n in range(z.NT):
        k.o.payload.v[n] = sums
    send(k.o.payload, k.o.water_c)
    send_edges(z, k, True)


def step_reservoirs(z, consts, pool, total, lateral):
    area, release, link = consts[0], consts[1], consts[2]
    released = cascade(z, consts, release * (pool + lateral))
    pool = pool + lateral + link * shift_slots(released, z.LD) - released
    return pool, total + released


def sum_members(z, x):
    total = x
    for m in range(1, z.M):
        total = total + pltpu.roll(x, z.SR - m * z.LT, 0)
    return jnp.where(row_ids(x.shape) < z.LT, total, 0.0)


def contact_kernel(z, k, last):
    got, consts = k.i.got.v, k.i.consts.v
    lateral = got[0]
    for t in range(1, z.NT):
        lateral += got[t]
    pool, total = step_reservoirs(z, consts, k.i.state.v[0], k.i.state.v[1], lateral)
    k.o.state.v[0] = pool
    k.o.state.v[1] = total
    k.o.state.send()
    k.s.level[...] = levels_of(z, pool, consts[0])
    other, pack = (k.i.from0, k.i.from1), k.i.pack.v
    cross_edges(
        z, k,
        lambda side, n, m: k.i.own.v[side, m],
        lambda n, m: other[n].v[m],
        lambda side, n: [pack[side, i] for i in range(4)],
    )
    sums = contact_step(z, k, k.s.level, lambda side: pack[side, 0])
    payload = k.o.payload.v
    if last:
        summed = sum_members(z, total) * (1.0 / z.NT)
        others = consts[1] * (sum_members(z, sums) + sum_members(z, pool) * (1.0 / z.NT))
        others = others + summed - consts[3] * shift_slots(summed, z.LD)
        member = lax.axis_index("ens")
        for e in range(z.E):
            block = jnp.where(member == e, sums, others)
            for t in range(z.NT):
                payload[e * z.NT + t] = block
    else:
        for t in range(z.NT):
            payload[t] = sums
    send(k.o.payload, k.o.water_c)
    send_edges(z, k, not last)


def own_slots(z, x, tile):
    begin = tile * z.LD
    at = begin % LANES
    j = begin // LANES
    out = jnp.zeros((1, LANES), F32)
    turned = pltpu.roll(x, LANES - at, 1)
    lane = lane_ids((1, LANES))
    for n in range(z.LT):
        out = jnp.where((j == n) & (lane < LANES - at), turned[n : n + 1], out)
        out = jnp.where((j + 1 == n) & (lane >= LANES - at), turned[n : n + 1], out)
    return out


def close_kernel(z, k):
    tile = lax.axis_index("tiles")
    member = lax.axis_index("ens")
    got, consts = k.i.got.v, k.i.consts.v
    lateral = jnp.zeros((z.SR, LANES), F32)
    others = jnp.zeros((z.SR, LANES), F32)
    for e in range(z.E):
        part = got[e * z.NT]
        for t in range(1, z.NT):
            part += got[e * z.NT + t]
        lateral = jnp.where(member == e, part, lateral)
        others = others + jnp.where(member == e, 0.0, part)
    pool, total = step_reservoirs(z, consts, k.i.state.v[0], k.i.state.v[1], lateral)
    for m in range(z.M):
        at = slice(m * z.LT, (m + 1) * z.LT)
        k.o.storage.v[m : m + 1, :] = own_slots(z, pool[at], tile)[:, : z.LD]
    mean = (sum_members(z, total) + cascade(z, consts, others)) * (1.0 / (z.M * z.E))
    k.o.outflow.v[...] = own_slots(z, mean[: z.LT], tile)[:, : z.LD]
    send(k.o.storage, k.o.outflow)


def shards(
    depth, bed, rain, rough_class, class_n, contact_seg, contact_lake, lake_slot, storage, area, release, upstream_link
):
    z = types.SimpleNamespace()
    z.M, z.R, z.W = depth.shape
    z.NT = lax.axis_size("tiles")
    z.E = lax.axis_size("ens")
    z.LD = storage.shape[1]
    z.LK = z.NT * z.LD
    z.CAP = contact_seg.shape[2]
    z.C = contact_seg.shape[1] * z.CAP
    z.CT = -(-z.C // LANES)
    z.PR = z.W // SEG
    z.classes = class_n.shape[0]
    z.LT = z.LK // LANES + 1
    z.SR = up_to(z.M * z.LT, SUBLANES)
    z.BR = up_to(z.M + 3, SUBLANES)
    levels = len(list(laps(z)))
    blocks = z.W // min(BLOCK, z.W)
    tile_shape = (z.M, z.R, z.W)
    edge_shape = (z.M, z.PR, SEG)
    pack_shape = (z.M + 2, z.PR, SEG)
    near_shape = (z.LT, z.C, LANES)
    state_shape = (2, z.SR, LANES)
    const_shape = (3 + levels, z.SR, LANES)
    contact_shape = (z.M * z.C, SEG)
    wide_tile = pltpu.VMEM((z.M, z.R, z.W + 2 * LANES), F32)
    wide_rows = pltpu.VMEM((z.R, z.W + 2 * LANES), F32)
    plain_tile = pltpu.VMEM(tile_shape, F32)
    onward = [(i, (i + 1) % z.NT) for i in range(z.NT)]
    back = [(j, i) for i, j in onward]

    def share(x, axes):
        return lax.all_to_all(x, axes, 0, 0, tiled=True)

    def swap(top, bottom):
        return lax.ppermute(bottom, "tiles", onward), lax.ppermute(top, "tiles", back)

    edges_shape = (2,) + edge_shape
    level_buffer = pltpu.VMEM((z.SR, LANES), F32)
    opened = staged_call(
        pack_kernel, z,
        dict(depth=Raw(depth), bed=Raw(bed), cls=Raw(rough_class), class_n=Scalars(class_n)),
        dict(pack1=pack_shape, pack0=pack_shape, table=(z.R, LANES)),
        dict(rows=pltpu.VMEM((2, z.M + 1, z.W), F32), cls_rows=pltpu.VMEM((2, 1, z.W), I32), ids=pltpu.VMEM((z.PR, SEG), I32)),
        extra_sems=2 * (z.M + 2),
    )
    from0, from1 = swap(opened.pack0, opened.pack1)
    kept = staged_call(
        prepare_kernel, z,
        dict(cls=Raw(rough_class), table=opened.table, seg=Scalars(contact_seg), lake=Scalars(contact_lake),
             slot=Scalars(lake_slot), storage=storage, area=area.reshape(1, -1), release=release.reshape(1, -1),
             link=upstream_link.reshape(1, -1)),
        dict(payload=(z.NT, z.BR, LANES), inv=Raw((z.R, z.W)), near=near_shape, near_edges=(2 * z.LT, z.PR, LANES)),
        dict(cls=pltpu.VMEM((z.R, z.W), I32), inv=pltpu.VMEM((z.R, z.W), F32)),
        extra_sems=2 * blocks,
    )
    got = share(kept.payload, "tiles")
    inv, near, near_edges = kept.inv, kept.near, kept.near_edges
    flow_scratch = dict(water=wide_tile, bed=wide_rows, inv=wide_rows, rain=plain_tile, out=plain_tile)
    flow_out = dict(next=Raw(tile_shape), wet_c=Here(contact_shape), edges=Here(edges_shape))
    flow = staged_call(
        functools.partial(flow_kernel, first=True), z,
        dict(wet=Raw(depth), seg=Scalars(contact_seg), bed=Raw(bed), inv=Raw(inv), rain=Raw(rain), near=Passed(near),
             near_edges=Passed(near_edges), own1=Passed(opened.pack1), own0=Passed(opened.pack0)),
        dict(bed_c=Here((z.C, SEG)), bed_kept=Raw((z.C, SEG)), **flow_out),
        dict(bed_c=pltpu.VMEM((z.C, SEG), F32), **flow_scratch),
        extra_sems=5 * blocks + 1,
    )
    bed_kept = flow.bed_kept

    step_out = dict(edges=edges_shape, water_c=contact_shape, state=state_shape)
    exchange_out = dict(edge0=Raw(edge_shape), edge1=Raw(edge_shape))
    now = staged_call(
        open_kernel, z,
        dict(got=Here(got, free=True), from1=Here(from1, free=True), from0=Here(from0, free=True), own1=Here(flow.own1),
             own0=Here(flow.own0), edges=Here(flow.edges), near=Here(flow.near), near_edges=Here(flow.near_edges),
             wet_c=Here(flow.wet_c), bed_c=Here(flow.bed_c)),
        dict(payload=(z.NT, z.SR, LANES), pack=(2, 4, z.PR, SEG), consts=const_shape, **step_out, **exchange_out),
        dict(pool=level_buffer, level=level_buffer),
        extra_sems=2,
    )
    consts, pack = now.consts, now.pack
    for step in range(1, STEPS):
        got = share(now.payload, "tiles")
        from0, from1 = swap(now.edge0, now.edge1)
        last = step == STEPS - 1
        flow = staged_call(
            functools.partial(flow_kernel, first=False), z,
            dict(wet=Raw(flow.next), seg=Scalars(contact_seg), water_c=now.water_c, edges=now.edges, bed=Raw(bed),
                 inv=Raw(inv), rain=Raw(rain), state=Passed(now.state), consts=Passed(consts), near=Passed(near),
                 near_edges=Passed(near_edges), pack=Passed(pack), own=Passed(now.edges), bed_c=Passed(bed_kept)),
            flow_out,
            flow_scratch,
            extra_sems=1 + 4 * blocks,
        )
        now = staged_call(
            functools.partial(contact_kernel, last=last), z,
            dict(got=Here(got, free=True), from0=Here(from0, free=True), from1=Here(from1, free=True), own=Here(flow.own),
                 edges=Here(flow.edges), state=Here(flow.state), consts=Here(flow.consts), pack=Here(flow.pack),
                 near=Here(flow.near), near_edges=Here(flow.near_edges), wet_c=Here(flow.wet_c), bed_c=Here(flow.bed_c)),
            dict(payload=((z.E if last else 1) * z.NT, z.SR, LANES), **step_out, **({} if last else exchange_out)),
            dict(level=level_buffer),
            extra_sems=2,
        )
    got = share(now.payload, ("ens", "tiles"))
    done = staged_call(
        last_kernel, z,
        dict(wet=flow.next, seg=Scalars(contact_seg), water_c=now.water_c, edges=now.edges, state=Passed(now.state),
             consts=Passed(consts)),
        dict(depth=Raw(tile_shape)),
        extra_sems=1,
    )
    closed = staged_call(
        close_kernel, z,
        dict(got=Here(got, free=True), state=Here(done.state), consts=Here(done.consts)),
        dict(storage=(z.M, z.LD), outflow=(1, z.LD)),
    )
    return done.depth, closed.storage, closed.outflow.reshape(-1)


def solution(mesh):
    return jax.shard_map(
        shards,
        mesh=mesh,
        in_specs=(
            P("ens", "tiles", None),
            P("tiles", None),
            P("ens", "tiles", None),
            P("tiles", None),
            P(),
            P("tiles", None, None),
            P("tiles", None, None),
            P(),
            P("ens", "tiles"),
            P("tiles"),
            P("tiles"),
            P("tiles"),
        ),
        out_specs=(P("ens", "tiles", None), P("ens", "tiles"), P("tiles")),
        check_vma=False,
    )
```

```python
import functools
import types

import jax
import jax.numpy as jnp
from jax import lax
from jax.experimental import pallas as pl
from jax.experimental.pallas import tpu as pltpu
from jax.sharding import PartitionSpec as P

SEG = 256
STEPS = 4
LANES = 128
SUBLANES = 8
FAR = 1e30

flow_rate = 0.035
drain_rate = 0.4

F32 = jnp.float32
I32 = jnp.int32
VMEM_LIMIT = 40 * 2**20
BLOCK = 4096


def up_to(value, unit):
    return -(-value // unit) * unit


def lane_ids(shape):
    return lax.broadcasted_iota(I32, shape, len(shape) - 1)


def row_ids(shape):
    return lax.broadcasted_iota(I32, shape, len(shape) - 2)


def mobility(water, inv_n):
    return water * jnp.exp2(jnp.log2(jnp.abs(water)) * (2.0 / 3.0)) * inv_n


def taken_of(water, surface, level):
    excess = jnp.maximum(surface - level, 0.0)
    return drain_rate * water * excess / (1.0 + excess)


class Array:
    def __init__(self, kernel, h, v):
        self.kernel, self.h, self.v = kernel, h, v

    def load(self):
        self.coming = self.kernel.copy(self.h, self.v)

    def wait(self):
        self.coming.wait()

    def send(self):
        self.kernel.stores.append(self.kernel.copy(self.v, self.h))


class Kernel:
    def __init__(self, sems):
        self.sems, self.count, self.stores = sems, 0, []

    def copy(self, source, target):
        copy = pltpu.make_async_copy(source, target, self.sems.at[self.count])
        self.count += 1
        copy.start()
        return copy

    def pass_on(self):
        for source, target in self.passed:
            self.stores.append(self.copy(source, target))

    def finish(self):
        for copy in self.stores:
            copy.wait()


def load(*arrays):
    for array in arrays:
        array.load()


def wait(*arrays):
    for array in arrays:
        array.wait()


def send(*arrays):
    for array in arrays:
        array.send()


class Staged:
    space = pltpu.VMEM

    def __init__(self, x, free=False):
        self.x, self.free = x, free


class Scalars(Staged):
    space = pltpu.SMEM


class Raw(Staged):
    space = None


class Here(Staged):
    space = None


class Passed(Here):
    pass


def staged_call(body, z, ins, outs, scratch=None, alias=None, extra_sems=0, micros=60):
    scratch = scratch or {}
    ins = {n: x if isinstance(x, Staged) else Staged(x) for n, x in ins.items()}
    outs = {n: x if isinstance(x, Staged) else Staged(x) for n, x in outs.items()}
    passed = [n for n, x in ins.items() if isinstance(x, Passed)]
    outs.update({n: Here(ins[n].x.shape) for n in passed})
    extra_sems += len(passed)
    here_in = [isinstance(x, Here) and not isinstance(x, Passed) for x in ins.values()]
    here_out = [isinstance(x, Here) for x in outs.values()]
    shapes = [x.space(x.x.shape, x.x.dtype) for x in ins.values() if x.space]
    shapes += [x.space(x.x, F32) for x in outs.values() if x.space]
    count = len(shapes) + extra_sems
    shapes += list(scratch.values())
    shapes.append(pltpu.SemaphoreType.DMA((count,)))

    def kernel(*refs):
        refs = list(refs)
        k = Kernel(refs.pop())
        arrays_in, arrays_out = [{n: refs.pop(0) for n in names} for names in (ins, outs)]
        for held, kinds in ((arrays_in, ins), (arrays_out, outs)):
            for n, x in kinds.items():
                held[n] = Array(k, held[n], refs.pop(0) if x.space else held[n])
        k.i = types.SimpleNamespace(**arrays_in)
        k.o = types.SimpleNamespace(**arrays_out)
        k.s = types.SimpleNamespace(**{n: refs.pop(0) for n in scratch})
        k.passed = [(arrays_in[n].h, arrays_out[n].h) for n in passed]
        body(z, k)
        k.finish()

    in_hbm = pl.BlockSpec(memory_space=pltpu.HBM)
    in_vmem = pl.BlockSpec(memory_space=pltpu.VMEM)
    order_in, order_out = list(ins), list(outs)
    results = pl.pallas_call(
        kernel,
        out_shape=[(pltpu.VMEM if here else pltpu.HBM)(x.x, F32) for x, here in zip(outs.values(), here_out)],
        in_specs=[in_vmem if here else in_hbm for here in here_in],
        out_specs=[in_vmem if here else in_hbm for here in here_out],
        scratch_shapes=shapes,
        input_output_aliases={order_in.index(a): order_out.index(b) for a, b in (alias or {}).items()},
        compiler_params=pltpu.CompilerParams(vmem_limit_bytes=VMEM_LIMIT),
        cost_estimate=pl.CostEstimate(
            flops=int(micros * 1e9), transcendentals=int(micros * 1e6), bytes_accessed=int(micros * 3e6)
        ),
    )(*[
        pltpu.with_memory_space_constraint(x.x, pltpu.VMEM if here else pltpu.HBM) if not (here and x.free) else x.x
        for x, here in zip(ins.values(), here_in)
    ])
    return types.SimpleNamespace(**dict(zip(order_out, results)))


def side_of(n):
    tile = lax.axis_index("tiles")
    there = tile > 0 if n == 0 else tile < lax.axis_size("tiles") - 1
    return n, jnp.where(there, 1.0, 0.0)


def pack_kernel(z, k):
    k.i.class_n.load()
    rows, cls_rows = k.s.rows, k.s.cls_rows
    copies = []
    for side, row in enumerate((0, z.R - 1)):
        for m in range(z.M):
            copies.append(k.copy(k.i.depth.h.at[m, pl.ds(row, 1)], rows.at[side, pl.ds(m, 1)]))
        copies.append(k.copy(k.i.bed.h.at[pl.ds(row, 1)], rows.at[side, pl.ds(z.M, 1)]))
        copies.append(k.copy(k.i.cls.h.at[pl.ds(row, 1)], cls_rows.at[side]))
    k.i.class_n.wait()
    k.o.table.v[...] = inv_table(z, k.i.class_n.v, z.R)
    k.o.table.send()
    wide = inv_table(z, k.i.class_n.v, z.PR)
    for copy in copies:
        copy.wait()
    ids = k.s.ids
    for n, out in enumerate((k.o.pack0, k.o.pack1)):
        side, _ = side_of(n)
        for g in range(z.PR):
            at = slice(g * SEG, (g + 1) * SEG)
            for m in range(z.M + 1):
                out.v[m, g : g + 1, :] = rows[side, m : m + 1, at]
            ids[g : g + 1, :] = cls_rows[side, :, at]
        for half in range(0, SEG, LANES):
            at = slice(half, half + LANES)
            out.v[z.M + 1, :, at] = look_up(wide, ids[:, at])
        out.send()


def inv_table(z, class_n, rows):
    lane = lane_ids((rows, LANES))
    names = jnp.ones((rows, LANES), F32)
    for n in range(z.classes):
        names = jnp.where(lane == n, class_n[n], names)
    return flow_rate * 0.5 / names


def look_up(table, ids):
    return jnp.take_along_axis(table, ids, axis=1, mode="promise_in_bounds")


def widen(z, ref, index=(), left=True, right=True):
    rows = slice(None)
    if left:
        ref[index + (rows, slice(0, LANES))] = pltpu.roll(ref[index + (rows, slice(LANES, 2 * LANES))], LANES - 1, 1)
    if right:
        ref[index + (rows, slice(z.W + LANES, z.W + 2 * LANES))] = pltpu.roll(
            ref[index + (rows, slice(z.W, z.W + LANES))], 1, 1
        )


def flow_blocks(z, water, bed, inv, rain, out, edges, done, ready=None):
    size = min(BLOCK, z.W)
    segs = size // SEG
    row = row_ids((z.R, size))
    bottom = row == z.R - 1
    top = row == 0

    def block(j, _):
        base = j * size if ready else pl.multiple_of(j * size, size)
        wide = pl.ds(base, size + 2 * LANES)
        at = pl.ds(base, size)
        b, v = bed[:, wide], inv[:, wide]
        for m in range(z.M):
            w = water[m, :, wide]
            s = b + w
            q = mobility(w, v)
            s_right = pltpu.roll(s, size + 2 * LANES - 1, 1)
            q_right = pltpu.roll(q, size + 2 * LANES - 1, 1)
            f = ((q + q_right) * (s - s_right))[:, : size + LANES]
            net = pltpu.roll(f, 1, 1)[:, LANES:] - f[:, LANES:]
            s = s[:, LANES : size + LANES]
            q = q[:, LANES : size + LANES]
            flow = (q + pltpu.roll(q, z.R - 1, 0)) * (s - pltpu.roll(s, z.R - 1, 0))
            flow = jnp.where(bottom, 0.0, flow)
            above = jnp.where(top, 0.0, pltpu.roll(flow, 1, 0))
            wet = w[:, LANES : size + LANES] + (net + (above - flow)) + rain[m, :, at]
            out[m, :, at] = wet
            for i in range(segs):
                part = slice(i * SEG, (i + 1) * SEG)
                edges[0, m, pl.ds(j * segs + i, 1), :] = wet[:1, part]
                edges[1, m, pl.ds(j * segs + i, 1), :] = wet[z.R - 1 :, part]
        done(j, at)
        return 0

    if ready:
        for j in range(z.W // size):
            ready(j)
            block(j, 0)
    else:
        lax.fori_loop(0, z.W // size, block, 0)


def send_blocks(z, k, source, target):
    size = min(BLOCK, z.W)
    first = k.count
    k.count += z.W // size

    def copy(j):
        at = pl.ds(pl.multiple_of(j * size, size), size)
        return pltpu.make_async_copy(source.at[:, :, at], target.at[:, :, at], k.sems.at[first + j])

    for j in range(z.W // size):
        k.stores.append(copy(j))
    return lambda j, at: copy(j).start()


def contact_places(z, seg):
    for c in range(z.C):
        owner, place = divmod(c, z.CAP)
        s = seg[0, owner, place]
        yield c, s // z.PR, pl.multiple_of((s % z.PR) * SEG, SEG)


def gather_contacts(z, seg, water, out):
    for c, r, at in contact_places(z, seg):
        for m in range(z.M):
            out[m * z.C + c : m * z.C + c + 1, :] = water[m, pl.ds(r, 1), pl.ds(at, SEG)]


def scatter_contacts(z, seg, values, water, shift):
    for c, r, at in contact_places(z, seg):
        for m in range(z.M):
            water[m, pl.ds(r, 1), pl.ds(at + shift, SEG)] = values[m * z.C + c : m * z.C + c + 1, :]


def set_edges(z, edges, water, shift):
    for side, row in enumerate((0, z.R - 1)):
        for m in range(z.M):
            for g in range(z.PR):
                at = slice(g * SEG + shift, (g + 1) * SEG + shift)
                water[m, row : row + 1, at] = edges[side, m, g : g + 1, :]


def prepare_kernel(z, k):
    size = min(BLOCK, z.W)
    parts = z.W // size
    small = k.i.storage, k.i.area, k.i.release, k.i.link, k.i.table
    load(*small)
    cls, inv = k.s.cls, k.s.inv
    columns = [pl.ds(p * size, size) for p in range(parts)]
    coming = [k.copy(k.i.cls.h.at[:, at], cls.at[:, at]) for at in columns]
    wait(*small)
    payload = k.o.payload.v
    payload[0] = jnp.zeros((z.BR, LANES), F32)
    payload[0, : z.M, : z.LD] = k.i.storage.v[...]
    for n, x in enumerate((k.i.area, k.i.release, k.i.link)):
        payload[0, z.M + n : z.M + n + 1, : z.LD] = x.v[...].astype(F32)
    for n in range(1, z.NT):
        payload[n] = payload[0]
    k.o.payload.send()
    table = k.i.table.v[...]
    for p in range(parts):
        coming[p].wait()

        def look(i, _):
            at = pl.ds(pl.multiple_of(p * size + i * LANES, LANES), LANES)
            inv[:, at] = look_up(table, cls[:, at])
            return 0

        lax.fori_loop(0, size // LANES, look, 0, unroll=16)
        k.stores.append(k.copy(inv.at[:, columns[p]], k.o.inv.h.at[:, columns[p]]))


def one_hots(z, k):
    lane = lane_ids((1, LANES))
    contact = row_ids((z.C, LANES))
    place_g = row_ids((z.PR, LANES))
    inside = jnp.full((z.C, 1), z.LK, F32)
    on_edge = [jnp.full((z.PR, 1), z.LK, F32) for _ in range(2)]
    firsts = (0, (z.R - 1) * z.PR)
    for tile in range(z.CT):
        segs = jnp.full((1, LANES), -1, I32)
        slots = jnp.full((1, LANES), z.LK, I32)
        for c in range(tile * LANES, min(z.C, (tile + 1) * LANES)):
            owner, place = divmod(c, z.CAP)
            lake_id = k.i.lake.v[0, owner, place]
            found = jnp.where(lake_id >= 0, k.i.slot.v[jnp.maximum(lake_id, 0)], z.LK)
            segs = jnp.where(lane == c - tile * LANES, k.i.seg.v[0, owner, place], segs)
            slots = jnp.where(lane == c - tile * LANES, found, slots)
        more = (slots - z.LK).astype(F32)
        central = (segs >= z.PR) & (segs < firsts[1])
        mine = lane_ids((z.C, LANES)) + tile * LANES == contact
        inside += jnp.sum(jnp.where(mine & central, more, 0.0), axis=1, keepdims=True)
        for side in range(2):
            here = place_g + firsts[side] == segs
            on_edge[side] += jnp.sum(jnp.where(here, more, 0.0), axis=1, keepdims=True)
    for j in range(z.LT):
        k.s.near[j] = jnp.where(inside == (lane_ids((z.C, LANES)) + j * LANES).astype(F32), 1.0, 0.0)
        for side in range(2):
            ids = (lane_ids((z.PR, LANES)) + j * LANES).astype(F32)
            k.s.near_edges[side * z.LT + j] = jnp.where(on_edge[side] == ids, 1.0, 0.0)


def flow_kernel(z, k, first):
    size = min(BLOCK, z.W)
    parts = z.W // size
    inv, bed, water, rain = k.s.inv, k.s.bed, k.s.water, k.s.rain
    k.i.seg.load()
    if first:
        load(k.i.lake, k.i.slot)
    columns = [(pl.ds(p * size, size), pl.ds(p * size + LANES, size)) for p in range(parts)]
    if not first:
        k.i.water_c.load()
        whole = k.copy(k.i.wet.h, water.at[:, :, pl.ds(LANES, z.W)])
        k.i.edges.load()
    coming = []
    for at, inner in columns:
        coming.append([
            k.copy(k.i.bed.h.at[:, at], bed.at[:, inner]),
            k.copy(k.i.inv.h.at[:, at], inv.at[:, inner]),
            k.copy(k.i.rain.h.at[:, :, at], rain.at[:, :, at]),
        ])
        if first:
            coming[-1].append(k.copy(k.i.wet.h.at[:, :, at], water.at[:, :, inner]))
    k.pass_on()
    k.i.seg.wait()
    if first:
        wait(k.i.lake, k.i.slot)
        one_hots(z, k)
        for source, here, kept in ((k.s.near, k.o.near, k.o.near_kept), (k.s.near_edges, k.o.near_edges, k.o.near_edges_kept)):
            here.v[...] = source[...]
            k.stores.append(k.copy(source, kept.h))
    else:
        k.i.water_c.wait()
        whole.wait()
        scatter_contacts(z, k.i.seg.v, k.i.water_c.v, water, LANES)
        k.i.edges.wait()
        set_edges(z, k.i.edges.v, water, LANES)

    def prepare(p):
        for copy in coming[p]:
            copy.wait()
        sides = dict(left=p == 0, right=p == parts - 1)
        widen(z, inv, **sides)
        widen(z, bed, **sides)
        for m in range(z.M):
            widen(z, water, (m,), **sides)

    def ready(j):
        if j == 0:
            prepare(0)
        if j + 1 < parts:
            prepare(j + 1)

    done = send_blocks(z, k, k.s.out, k.o.next.h)
    flow_blocks(z, water, bed, inv, rain, k.s.out, k.o.edges.v, done, ready)
    gather_contacts(z, k.i.seg.v, k.s.out, k.o.wet_c.v)
    if first:
        for c, r, at in contact_places(z, k.i.seg.v):
            k.o.bed_c.v[c : c + 1, :] = bed[pl.ds(r, 1), pl.ds(at + LANES, SEG)]
            k.s.bed_c[c : c + 1, :] = bed[pl.ds(r, 1), pl.ds(at + LANES, SEG)]
        k.stores.append(k.copy(k.s.bed_c, k.o.bed_kept.h))


def last_kernel(z, k):
    load(k.i.wet, k.i.seg, k.i.water_c, k.i.edges)
    k.pass_on()
    wait(k.i.wet, k.i.seg, k.i.water_c, k.i.edges)
    scatter_contacts(z, k.i.seg.v, k.i.water_c.v, k.i.wet.v, 0)
    set_edges(z, k.i.edges.v, k.i.wet.v, 0)
    k.stores.append(k.copy(k.i.wet.v, k.o.depth.h))


def pick(z, near, table, m):
    total = near[0] * table[m * z.LT : m * z.LT + 1, :]
    for j in range(1, z.LT):
        total += near[j] * table[m * z.LT + j : m * z.LT + j + 1, :]
    return jnp.sum(total, axis=1, keepdims=True)


def shift_slots(x, count):
    rows, lanes = divmod(count, LANES)
    size = x.shape[0]
    turned = pltpu.roll(x, lanes, 1) if lanes else x
    low = pltpu.roll(turned, rows % size, 0) if rows % size else turned
    if not lanes:
        return low
    high = pltpu.roll(turned, (rows + 1) % size, 0)
    return jnp.where(lane_ids(x.shape) < lanes, high, low)


def laps(z):
    count = z.LD
    while count < z.LK:
        yield count
        count *= 2


def cascade(z, consts, entering):
    for lap, count in enumerate(laps(z)):
        entering = entering + consts[3 + lap] * shift_slots(entering, count)
    return entering


def slot_ids(z):
    shape = (z.SR, LANES)
    return (row_ids(shape) % z.LT) * LANES + lane_ids(shape)


def levels_of(z, pool, area):
    return jnp.where(slot_ids(z) == z.LK, FAR, pool / area)


def lay_out(z, got, pool, consts):
    pool[...] = jnp.zeros_like(pool)
    consts[...] = jnp.zeros_like(consts)
    consts[0] = jnp.ones((z.SR, LANES), F32)
    for t in range(z.NT):
        done = 0
        while done < z.LD:
            j, at = divmod(t * z.LD + done, LANES)
            n = min(z.LD - done, LANES - at)
            for m in range(z.M):
                r = m * z.LT + j
                pool[r : r + 1, at : at + n] = got[t, m : m + 1, done : done + n]
                for i in range(3):
                    consts[i, r : r + 1, at : at + n] = got[t, z.M + i : z.M + i + 1, done : done + n]
            done += n
    consts[2] = jnp.where(slot_ids(z) >= z.LD, consts[2], 0.0)
    factor = consts[1] * consts[2]
    for lap, count in enumerate(laps(z)):
        consts[3 + lap] = factor
        factor = factor * shift_slots(factor, count)


def cross_edges(z, k, own, other, rows):
    for n in range(2):
        side, flag = side_of(n)
        own_bed, own_inv, other_bed, other_inv = rows(side, n)
        for m in range(z.M):
            a, b = own(side, n, m), other(n, m)
            flow = (mobility(a, own_inv) + mobility(b, other_inv)) * ((other_bed + b) - (own_bed + a))
            k.i.edges.v[side, m] += flow * flag


def contact_step(z, k, level, bed_rows):
    rows = [[jnp.zeros((SUBLANES, LANES), F32) for _ in range(z.LT)] for _ in range(z.M)]

    def take(near, m, w, bed):
        taken = taken_of(w, bed + w, pick(z, near, level, m))
        sums = jnp.sum(taken, axis=1, keepdims=True) * (1.0 / SEG)
        for j in range(z.LT):
            part = near[j] * sums
            for r in range(0, part.shape[0], SUBLANES):
                rows[m][j] += part[r : r + SUBLANES]
        return w - taken

    for side in range(2):
        near = k.i.near_edges.v.at[pl.ds(side * z.LT, z.LT)]
        for m in range(z.M):
            k.o.edges.v[side, m] = take(near, m, k.i.edges.v[side, m], bed_rows(side))
    bed = k.i.bed_c.v[...]
    for m in range(z.M):
        at = slice(m * z.C, (m + 1) * z.C)
        k.o.water_c.v[at, :] = take(k.i.near.v, m, k.i.wet_c.v[at, :], bed)
    found = [jnp.sum(rows[m][j], axis=0, keepdims=True) for m in range(z.M) for j in range(z.LT)]
    if z.SR > len(found):
        found.append(jnp.zeros((z.SR - len(found), LANES), F32))
    return jnp.concatenate(found, axis=0)


def send_edges(z, k, exchange):
    k.o.edges.send()
    if exchange:
        for n, out in enumerate((k.o.edge0, k.o.edge1)):
            side, _ = side_of(n)
            k.stores.append(k.copy(k.o.edges.v.at[side], out.h))


def open_kernel(z, k):
    own, other, pack = (k.i.own0, k.i.own1), (k.i.from0, k.i.from1), k.o.pack.v
    for n in range(2):
        side, _ = side_of(n)
        pack[side, :2] = own[n].v[z.M : z.M + 2]
        pack[side, 2:] = other[n].v[z.M : z.M + 2]
    k.o.pack.send()
    cross_edges(
        z, k,
        lambda side, n, m: own[n].v[m],
        lambda n, m: other[n].v[m],
        lambda side, n: [pack[side, i] for i in range(4)],
    )
    pool, consts = k.s.pool, k.o.consts.v
    lay_out(z, k.i.got.v, pool, consts)
    k.o.consts.send()
    k.o.state.v[0] = pool[...]
    k.o.state.v[1] = jnp.zeros((z.SR, LANES), F32)
    k.o.state.send()
    k.s.level[...] = levels_of(z, pool[...], consts[0])
    sums = contact_step(z, k, k.s.level, lambda side: pack[side, 0])
    for n in range(z.NT):
        k.o.payload.v[n] = sums
    send(k.o.payload, k.o.water_c)
    send_edges(z, k, True)


def step_reservoirs(z, consts, pool, total, lateral):
    area, release, link = consts[0], consts[1], consts[2]
    released = cascade(z, consts, release * (pool + lateral))
    pool = pool + lateral + link * shift_slots(released, z.LD) - released
    return pool, total + released


def sum_members(z, x):
    total = x
    for m in range(1, z.M):
        total = total + pltpu.roll(x, z.SR - m * z.LT, 0)
    return jnp.where(row_ids(x.shape) < z.LT, total, 0.0)


def contact_kernel(z, k, last):
    got, consts = k.i.got.v, k.i.consts.v
    lateral = got[0]
    for t in range(1, z.NT):
        lateral += got[t]
    pool, total = step_reservoirs(z, consts, k.i.state.v[0], k.i.state.v[1], lateral)
    k.o.state.v[0] = pool
    k.o.state.v[1] = total
    k.o.state.send()
    k.s.level[...] = levels_of(z, pool, consts[0])
    other, pack = (k.i.from0, k.i.from1), k.i.pack.v
    cross_edges(
        z, k,
        lambda side, n, m: k.i.own.v[side, m],
        lambda n, m: other[n].v[m],
        lambda side, n: [pack[side, i] for i in range(4)],
    )
    sums = contact_step(z, k, k.s.level, lambda side: pack[side, 0])
    payload = k.o.payload.v
    if last:
        summed = sum_members(z, total) * (1.0 / z.NT)
        others = consts[1] * (sum_members(z, sums) + sum_members(z, pool) * (1.0 / z.NT))
        others = others + summed - consts[3] * shift_slots(summed, z.LD)
        member = lax.axis_index("ens")
        for e in range(z.E):
            block = jnp.where(member == e, sums, others)
            for t in range(z.NT):
                payload[e * z.NT + t] = block
    else:
        for t in range(z.NT):
            payload[t] = sums
    send(k.o.payload, k.o.water_c)
    send_edges(z, k, not last)


def own_slots(z, x, tile):
    begin = tile * z.LD
    at = begin % LANES
    j = begin // LANES
    out = jnp.zeros((1, LANES), F32)
    turned = pltpu.roll(x, LANES - at, 1)
    lane = lane_ids((1, LANES))
    for n in range(z.LT):
        out = jnp.where((j == n) & (lane < LANES - at), turned[n : n + 1], out)
        out = jnp.where((j + 1 == n) & (lane >= LANES - at), turned[n : n + 1], out)
    return out


def close_kernel(z, k):
    tile = lax.axis_index("tiles")
    member = lax.axis_index("ens")
    got, consts = k.i.got.v, k.i.consts.v
    lateral = jnp.zeros((z.SR, LANES), F32)
    others = jnp.zeros((z.SR, LANES), F32)
    for e in range(z.E):
        part = got[e * z.NT]
        for t in range(1, z.NT):
            part += got[e * z.NT + t]
        lateral = jnp.where(member == e, part, lateral)
        others = others + jnp.where(member == e, 0.0, part)
    pool, total = step_reservoirs(z, consts, k.i.state.v[0], k.i.state.v[1], lateral)
    for m in range(z.M):
        at = slice(m * z.LT, (m + 1) * z.LT)
        k.o.storage.v[m : m + 1, :] = own_slots(z, pool[at], tile)[:, : z.LD]
    mean = (sum_members(z, total) + cascade(z, consts, others)) * (1.0 / (z.M * z.E))
    k.o.outflow.v[...] = own_slots(z, mean[: z.LT], tile)[:, : z.LD]
    send(k.o.storage, k.o.outflow)


def shards(
    depth, bed, rain, rough_class, class_n, contact_seg, contact_lake, lake_slot, storage, area, release, upstream_link
):
    z = types.SimpleNamespace()
    z.M, z.R, z.W = depth.shape
    z.NT = lax.axis_size("tiles")
    z.E = lax.axis_size("ens")
    z.LD = storage.shape[1]
    z.LK = z.NT * z.LD
    z.CAP = contact_seg.shape[2]
    z.C = contact_seg.shape[1] * z.CAP
    z.CT = -(-z.C // LANES)
    z.PR = z.W // SEG
    z.classes = class_n.shape[0]
    z.LT = z.LK // LANES + 1
    z.SR = up_to(z.M * z.LT, SUBLANES)
    z.BR = up_to(z.M + 3, SUBLANES)
    levels = len(list(laps(z)))
    blocks = z.W // min(BLOCK, z.W)
    tile_shape = (z.M, z.R, z.W)
    edge_shape = (z.M, z.PR, SEG)
    pack_shape = (z.M + 2, z.PR, SEG)
    near_shape = (z.LT, z.C, LANES)
    state_shape = (2, z.SR, LANES)
    const_shape = (3 + levels, z.SR, LANES)
    contact_shape = (z.M * z.C, SEG)
    wide_tile = pltpu.VMEM((z.M, z.R, z.W + 2 * LANES), F32)
    wide_rows = pltpu.VMEM((z.R, z.W + 2 * LANES), F32)
    plain_tile = pltpu.VMEM(tile_shape, F32)
    onward = [(i, (i + 1) % z.NT) for i in range(z.NT)]
    back = [(j, i) for i, j in onward]

    def share(x, axes):
        return lax.all_to_all(x, axes, 0, 0, tiled=True)

    def swap(top, bottom):
        return lax.ppermute(bottom, "tiles", onward), lax.ppermute(top, "tiles", back)

    edges_shape = (2,) + edge_shape
    level_buffer = pltpu.VMEM((z.SR, LANES), F32)
    opened = staged_call(
        pack_kernel, z,
        dict(depth=Raw(depth), bed=Raw(bed), cls=Raw(rough_class), class_n=Scalars(class_n)),
        dict(pack1=pack_shape, pack0=pack_shape, table=(z.R, LANES)),
        dict(rows=pltpu.VMEM((2, z.M + 1, z.W), F32), cls_rows=pltpu.VMEM((2, 1, z.W), I32), ids=pltpu.VMEM((z.PR, SEG), I32)),
        extra_sems=2 * (z.M + 2),
    )
    from0, from1 = swap(opened.pack0, opened.pack1)
    kept = staged_call(
        prepare_kernel, z,
        dict(cls=Raw(rough_class), table=opened.table, storage=storage, area=area.reshape(1, -1), release=release.reshape(1, -1),
             link=upstream_link.reshape(1, -1)),
        dict(payload=(z.NT, z.BR, LANES), inv=Raw((z.R, z.W))),
        dict(cls=pltpu.VMEM((z.R, z.W), I32), inv=pltpu.VMEM((z.R, z.W), F32)),
        extra_sems=2 * blocks,
    )
    got = share(kept.payload, "tiles")
    inv = kept.inv
    near_edges_shape = (2 * z.LT, z.PR, LANES)
    flow_scratch = dict(water=wide_tile, bed=wide_rows, inv=wide_rows, rain=plain_tile, out=plain_tile)
    flow_out = dict(next=Raw(tile_shape), wet_c=Here(contact_shape), edges=Here(edges_shape))
    flow = staged_call(
        functools.partial(flow_kernel, first=True), z,
        dict(wet=Raw(depth), seg=Scalars(contact_seg), bed=Raw(bed), inv=Raw(inv), rain=Raw(rain), lake=Scalars(contact_lake),
             slot=Scalars(lake_slot), own1=Passed(opened.pack1), own0=Passed(opened.pack0)),
        dict(bed_c=Here((z.C, SEG)), bed_kept=Raw((z.C, SEG)), near=Here(near_shape), near_kept=Raw(near_shape),
             near_edges=Here(near_edges_shape), near_edges_kept=Raw(near_edges_shape), **flow_out),
        dict(bed_c=pltpu.VMEM((z.C, SEG), F32), near=pltpu.VMEM(near_shape, F32),
             near_edges=pltpu.VMEM(near_edges_shape, F32), **flow_scratch),
        extra_sems=5 * blocks + 3,
    )
    bed_kept, near, near_edges = flow.bed_kept, flow.near_kept, flow.near_edges_kept

    step_out = dict(edges=edges_shape, water_c=contact_shape, state=state_shape)
    exchange_out = dict(edge0=Raw(edge_shape), edge1=Raw(edge_shape))
    now = staged_call(
        open_kernel, z,
        dict(got=Here(got, free=True), from1=Here(from1, free=True), from0=Here(from0, free=True), own1=Here(flow.own1),
             own0=Here(flow.own0), edges=Here(flow.edges), near=Here(flow.near), near_edges=Here(flow.near_edges),
             wet_c=Here(flow.wet_c), bed_c=Here(flow.bed_c)),
        dict(payload=(z.NT, z.SR, LANES), pack=(2, 4, z.PR, SEG), consts=const_shape, **step_out, **exchange_out),
        dict(pool=level_buffer, level=level_buffer),
        extra_sems=2,
    )
    consts, pack = now.consts, now.pack
    for step in range(1, STEPS):
        got = share(now.payload, "tiles")
        from0, from1 = swap(now.edge0, now.edge1)
        last = step == STEPS - 1
        flow = staged_call(
            functools.partial(flow_kernel, first=False), z,
            dict(wet=Raw(flow.next), seg=Scalars(contact_seg), water_c=now.water_c, edges=now.edges, bed=Raw(bed),
                 inv=Raw(inv), rain=Raw(rain), state=Passed(now.state), consts=Passed(consts), near=Passed(near),
                 near_edges=Passed(near_edges), pack=Passed(pack), own=Passed(now.edges), bed_c=Passed(bed_kept)),
            flow_out,
            flow_scratch,
            extra_sems=1 + 4 * blocks,
        )
        now = staged_call(
            functools.partial(contact_kernel, last=last), z,
            dict(got=Here(got, free=True), from0=Here(from0, free=True), from1=Here(from1, free=True), own=Here(flow.own),
                 edges=Here(flow.edges), state=Here(flow.state), consts=Here(flow.consts), pack=Here(flow.pack),
                 near=Here(flow.near), near_edges=Here(flow.near_edges), wet_c=Here(flow.wet_c), bed_c=Here(flow.bed_c)),
            dict(payload=((z.E if last else 1) * z.NT, z.SR, LANES), **step_out, **({} if last else exchange_out)),
            dict(level=level_buffer),
            extra_sems=2,
        )
    got = share(now.payload, ("ens", "tiles"))
    done = staged_call(
        last_kernel, z,
        dict(wet=flow.next, seg=Scalars(contact_seg), water_c=now.water_c, edges=now.edges, state=Passed(now.state),
             consts=Passed(consts)),
        dict(depth=Raw(tile_shape)),
        extra_sems=1,
    )
    closed = staged_call(
        close_kernel, z,
        dict(got=Here(got, free=True), state=Here(done.state), consts=Here(done.consts)),
        dict(storage=(z.M, z.LD), outflow=(1, z.LD)),
    )
    return done.depth, closed.storage, closed.outflow.reshape(-1)


def solution(mesh):
    return jax.shard_map(
        shards,
        mesh=mesh,
        in_specs=(
            P("ens", "tiles", None),
            P("tiles", None),
            P("ens", "tiles", None),
            P("tiles", None),
            P(),
            P("tiles", None, None),
            P("tiles", None, None),
            P(),
            P("ens", "tiles"),
            P("tiles"),
            P("tiles"),
            P("tiles"),
        ),
        out_specs=(P("ens", "tiles", None), P("ens", "tiles"), P("tiles")),
        check_vma=False,
    )
```
